32 devices in a mesh: parts: 1, rows: 32 (over z, y, x, core), cls: 1.
Axes of the slice: x: 2, y: 2, z: 4, core: 2. Of those that a mesh axis runs over, the one named last changes fastest.
Arguments:
- seeds: bfloat16 [16384, 1024], P(('parts', 'rows'), 'cls'), may hold values from -6 to 6
- neighbor_pos: int32 [16384, 50], P(('parts', 'rows')), may hold values from 0 to 1023, as said below
- edge_weight: int32 [16384, 50], P(('parts', 'rows')), may hold values from 1 to 192
- tile_blocks: int32 [128, 8], P(('parts', 'rows')), may hold values from 0 to 7, as said below
- wanted: int32 [32, 32, 16], P(('parts', 'rows')), may hold values from 0 to 511
Outputs:
- labels: bfloat16 [16384, 1024], P(('parts', 'rows'), 'cls')
The draws below stay inside these ranges and needn't reach their ends.
Inputs may be any that keep to these rules, and one draw needn't show every extreme that they name: `neighbor_pos`: the 50 positions of a row are distinct; position q names column q % 128 of the row block's tile q // 128. `tile_blocks`: the 8 numbers of a row block are distinct; a number below 4 is a row block of the same index of rows, a larger one e a block of 128 received rows, row r = (e - 4) * 128 + c standing for wanted[d, r // 16, r % 16]. wanted[d, p, c] is a row number local to index p of rows.
All inputs are finite; a program needn't handle non-finite values.
Results may differ from the reference program's by a relative error of at most 0.0034.
Values may be sent and summed in bfloat16 or wider, within the bound.
No kernel may reach another device: no remote copies, remote signals or barrier semaphores. Data moves between devices by JAX's collectives and lax.ppermute only.
A program may use at most 64 MiB of HBM per device.

```python
import jax
import jax.numpy as jnp
from jax import lax

CLASSES = 1024
BLK = 128
RB = 4
ROWS_DEV = 512
ROWS = 16384
ROW_BLOCKS = 128
PEERS = 32
NT = 8
K = 50
CAP = 16
EXT_BLK = 8
ITERS = 2


def draw_neighbor_pos(key, part):
    key = jax.random.fold_in(key, 11)
    first, second = jax.random.split(key)
    columns = NT * BLK
    stride = columns // K
    start = jax.random.randint(first, (ROWS, 1), 0, columns)
    jitter = jax.random.randint(second, (ROWS, K), 0, stride)
    offsets = jnp.arange(K, dtype=jnp.int32)[None, :] * stride
    return ((start + offsets + jitter) % columns).astype(jnp.int32)


def draw_edge_weight(key, part):
    key = jax.random.fold_in(key, 12)
    first, second = jax.random.split(key)
    factor = jax.random.randint(first, (ROWS, K), 1, 4)
    power = jax.random.randint(second, (ROWS, K), 0, 7)
    return (factor * jnp.left_shift(jnp.ones((ROWS, K), jnp.int32), power)).astype(jnp.int32)


def draw_tile_blocks(key, part):
    key = jax.random.fold_in(key, 13)
    first, second = jax.random.split(key)
    start = jax.random.randint(first, (PEERS, 1, 1), 0, EXT_BLK)
    keys = jax.random.split(second, PEERS)
    orders = jax.vmap(lambda one_key: jax.random.permutation(one_key, EXT_BLK))(keys).astype(jnp.int32)
    walk = (start + jnp.arange(RB, dtype=jnp.int32)[None, :, None] * NT + jnp.arange(NT, dtype=jnp.int32)[None, None, :]) % EXT_BLK
    picked = jax.vmap(lambda order_row, walk_rows: order_row[walk_rows])(orders, walk)
    return picked.reshape(ROW_BLOCKS, NT).astype(jnp.int32)


def place_ends(result, own_key, low, high):
    spot = [jax.random.randint(jax.random.fold_in(own_key, axis), (), 0, length) for axis, length in enumerate(result.shape)]
    longest = result.shape.index(max(result.shape))
    neighbour = spot[:longest] + [(spot[longest] + 1) % result.shape[longest]] + spot[longest + 1:]
    return result.at[tuple(spot)].set(low).at[tuple(neighbour)].set(high)


def shard_levels(own_key, dims, shards, low, top_value):
    def one(position, blocks):
        steps = jax.random.uniform(jax.random.fold_in(jax.random.fold_in(own_key, 6), position), (blocks,), jnp.float32, low / len(shards), top_value / len(shards))
        return jnp.repeat(jnp.exp(steps), dims[position] // blocks).reshape((-1,) + (1,) * (len(dims) - position - 1))

    factor_of = one(*shards[0])
    for cut in shards[1:]:
        factor_of = factor_of * one(*cut)
    return factor_of


def bell_draw(key, extent, spread, bound, shards=(), held_as=jnp.bfloat16):
    gain = shard_levels(key, extent, shards, -0.22, 0.18) if shards else 1.0
    values = jax.random.normal(key, extent, jnp.float32) * spread * gain
    return jnp.minimum(jnp.maximum(values, -bound), bound).astype(held_as)


def setup_inputs(seed: int = 0, part: int = 0) -> dict:
    key_of = jax.random.split(jax.random.key(seed), 6)
    part_keys = jax.random.split(jax.random.fold_in(key_of[5], part), 6)
    seeds = bell_draw(part_keys[0], (ROWS, CLASSES), 1.0, 6.0, ((0, 32),))
    neighbor_pos = draw_neighbor_pos(jax.random.fold_in(jax.random.fold_in(key_of[5], part), 71), part)
    edge_weight = draw_edge_weight(jax.random.fold_in(jax.random.fold_in(key_of[5], part), 71), part)
    tile_blocks = draw_tile_blocks(jax.random.fold_in(jax.random.fold_in(key_of[5], part), 71), part)
    wanted = place_ends(jax.random.randint(part_keys[4], (PEERS, PEERS, CAP), 0, ROWS_DEV), jax.random.fold_in(part_keys[4], 1), 0, ROWS_DEV - 1).astype(jnp.int32)
    return {"seeds": seeds, "neighbor_pos": neighbor_pos, "edge_weight": edge_weight, "tile_blocks": tile_blocks, "wanted": wanted}


def reference(seeds, neighbor_pos, edge_weight, tile_blocks, wanted):
    weights = edge_weight.astype(jnp.float32)
    share = (weights / jnp.sum(weights, axis=1, keepdims=True)).astype(jnp.bfloat16)
    row_ids = jnp.arange(ROWS, dtype=jnp.int32)
    device = (row_ids // ROWS_DEV).astype(jnp.int32)
    block_rows = tile_blocks[(row_ids // BLK).astype(jnp.int32)]
    block_id = jnp.take_along_axis(block_rows, (neighbor_pos // BLK).astype(jnp.int32), axis=1)
    extended = block_id * BLK + neighbor_pos % BLK
    remote = jnp.maximum(extended - ROWS_DEV, 0)
    peer_of = (remote // CAP).astype(jnp.int32)
    slot_of = (remote % CAP).astype(jnp.int32)
    wanted_row = wanted[device[:, None], peer_of, slot_of]
    source = jnp.where(extended < ROWS_DEV, device[:, None] * ROWS_DEV + extended,
                       peer_of * ROWS_DEV + wanted_row).astype(jnp.int32)
    source_blocks = source.reshape(ROW_BLOCKS, BLK, K)
    share_blocks = share.reshape(ROW_BLOCKS, BLK, K)
    seeds_float = seeds.astype(jnp.float32)
    current = seeds
    for step in range(ITERS):
        def one_block(pair):
            indices, coeffs = pair
            picked = current[indices].astype(jnp.float32)
            return jnp.einsum("rk,rkc->rc", coeffs.astype(jnp.float32), picked)
        summed = lax.map(one_block, (source_blocks, share_blocks)).reshape(ROWS, CLASSES)
        current = (0.85 * summed + 0.15 * seeds_float).astype(jnp.bfloat16)
    return current
```

```python
import functools

import jax
import jax.numpy as jnp
from jax import lax
from jax.experimental import pallas as pl
from jax.experimental.pallas import tpu as pltpu
from jax.sharding import PartitionSpec as P

BLK = 128
COLS = 256
VMEM = 48 * 1024 * 1024


def tiles_kernel(blocks_ref, pos_ref, weight_ref, tiles_ref, column_ref, share_ref):
    block_count, tile_count = blocks_ref.shape
    neighbours = pos_ref.shape[0]
    weights = weight_ref[...].astype(jnp.float32)
    share = weights / jnp.sum(weights, axis=0, keepdims=True)
    share_ref[...] = share.astype(jnp.bfloat16).astype(jnp.float32)
    for block in range(block_count):
        lanes = slice(block * BLK, (block + 1) * BLK)
        pos = pos_ref[:, lanes]
        tile = pos // BLK
        base = jnp.full(pos.shape, blocks_ref[block, 0], jnp.int32)
        for j in range(1, tile_count):
            base = jnp.where(tile == j, blocks_ref[block, j], base)
        column_ref[:, lanes] = base * BLK + pos % BLK

    sub = lax.broadcasted_iota(jnp.int32, (BLK, BLK), 0)

    @pl.loop(0, block_count)
    def _(block):
        lanes = pl.ds(pl.multiple_of(block * BLK, BLK), BLK)

        @pl.loop(0, tiles_ref.shape[1] // BLK)
        def _(chunk):
            first = pl.multiple_of(chunk * BLK, BLK)
            total = jnp.zeros((BLK, BLK), jnp.float32)
            for k in range(neighbours):
                spot = column_ref[k : k + 1, lanes] - first
                total = jnp.where(sub == spot, share_ref[k : k + 1, lanes], total)
            tiles_ref[lanes, pl.ds(first, BLK)] = total.T.astype(jnp.bfloat16)


def build_tiles(blocks, pos, weight, columns):
    neighbours, rows = pos.shape
    return pl.pallas_call(
        tiles_kernel,
        out_shape=jax.ShapeDtypeStruct((rows, columns), jnp.bfloat16),
        in_specs=[
            pl.BlockSpec(memory_space=pltpu.SMEM),
            pl.BlockSpec(memory_space=pltpu.VMEM),
            pl.BlockSpec(memory_space=pltpu.VMEM),
        ],
        out_specs=pl.BlockSpec(memory_space=pltpu.VMEM),
        scratch_shapes=[
            pltpu.VMEM((neighbours, rows), jnp.int32),
            pltpu.VMEM((neighbours, rows), jnp.float32),
        ],
        compiler_params=pltpu.CompilerParams(vmem_limit_bytes=VMEM),
        cost_estimate=pl.CostEstimate(
            flops=2 * neighbours * rows * columns,
            bytes_accessed=rows * columns * 2,
            transcendentals=0,
        ),
        name="build_tiles",
    )(blocks, pos, weight)


def pick_kernel(asked_ref, seeds_ref, out_ref, pick_ref):
    peers, _, slots = asked_ref.shape
    rows = seeds_ref.shape[0]
    count = peers * slots

    @pl.when(pl.program_id(0) == 0)
    def _():
        spread = jnp.broadcast_to(asked_ref[...].astype(jnp.float32), (peers, slots, slots))
        spread = spread.reshape(count, slots)
        slot = lax.broadcasted_iota(jnp.int32, (count, slots), 0) % slots
        lane = lax.broadcasted_iota(jnp.int32, (count, slots), 1)
        row = jnp.sum(jnp.where(slot == lane, spread, 0.0), axis=1, keepdims=True)
        hits = lax.broadcasted_iota(jnp.int32, (count, rows), 1) == row.astype(jnp.int32)
        pick_ref[...] = hits.astype(jnp.float32).astype(jnp.bfloat16)

    out_ref[...] = jnp.dot(
        pick_ref[...], seeds_ref[...], preferred_element_type=jnp.float32
    ).astype(jnp.bfloat16)


def pick_rows(asked, seeds):
    peers, _, slots = asked.shape
    rows, width = seeds.shape
    count = peers * slots
    return pl.pallas_call(
        pick_kernel,
        grid=(width // COLS,),
        out_shape=[
            jax.ShapeDtypeStruct((count, width), jnp.bfloat16),
            jax.ShapeDtypeStruct((count, rows), jnp.bfloat16),
        ],
        in_specs=[
            pl.BlockSpec((peers, 1, slots), lambda c: (0, 0, 0)),
            pl.BlockSpec((rows, COLS), lambda c: (0, c)),
        ],
        out_specs=[
            pl.BlockSpec((count, COLS), lambda c: (0, c)),
            pl.BlockSpec((count, rows), lambda c: (0, 0)),
        ],
        compiler_params=pltpu.CompilerParams(vmem_limit_bytes=VMEM),
        name="pick_rows",
    )(asked, seeds)


def propagate(tiles_ref, current_ref, received_ref, seeds_ref):
    rows = current_ref.shape[0]
    total = jnp.dot(
        tiles_ref[:, :rows], current_ref[...], preferred_element_type=jnp.float32
    ) + jnp.dot(tiles_ref[:, rows:], received_ref[...], preferred_element_type=jnp.float32)
    return (0.85 * total + 0.15 * seeds_ref[...].astype(jnp.float32)).astype(jnp.bfloat16)


def first_kernel(tiles_ref, pick_ref, seeds_ref, received_ref, labels_ref, out_ref):
    labels = propagate(tiles_ref, seeds_ref, received_ref, seeds_ref)
    labels_ref[...] = labels
    out_ref[...] = jnp.dot(
        pick_ref[...], labels, preferred_element_type=jnp.float32
    ).astype(jnp.bfloat16)


def last_kernel(tiles_ref, seeds_ref, current_ref, received_ref, labels_ref):
    labels_ref[...] = propagate(tiles_ref, current_ref, received_ref, seeds_ref)


def first_step(tiles, pick, seeds, received):
    rows, width = seeds.shape
    count = received.shape[0]
    by_columns = lambda c: (0, c)
    whole = lambda c: (0, 0)
    return pl.pallas_call(
        first_kernel,
        grid=(width // COLS,),
        out_shape=[
            jax.ShapeDtypeStruct((rows, width), jnp.bfloat16),
            jax.ShapeDtypeStruct((count, width), jnp.bfloat16),
        ],
        in_specs=[
            pl.BlockSpec(tiles.shape, whole),
            pl.BlockSpec(pick.shape, whole),
            pl.BlockSpec((rows, COLS), by_columns),
            pl.BlockSpec((count, COLS), by_columns),
        ],
        out_specs=[
            pl.BlockSpec((rows, COLS), by_columns),
            pl.BlockSpec((count, COLS), by_columns),
        ],
        compiler_params=pltpu.CompilerParams(vmem_limit_bytes=VMEM),
        name="first_step",
    )(tiles, pick, seeds, received)


def last_step(tiles, seeds, current, received):
    rows, width = seeds.shape
    count = received.shape[0]
    by_columns = lambda c: (0, c)
    return pl.pallas_call(
        last_kernel,
        grid=(width // COLS,),
        out_shape=jax.ShapeDtypeStruct((rows, width), jnp.bfloat16),
        in_specs=[
            pl.BlockSpec(tiles.shape, lambda c: (0, 0)),
            pl.BlockSpec((rows, COLS), by_columns),
            pl.BlockSpec((rows, COLS), by_columns),
            pl.BlockSpec((count, COLS), by_columns),
        ],
        out_specs=pl.BlockSpec((rows, COLS), by_columns),
        compiler_params=pltpu.CompilerParams(vmem_limit_bytes=VMEM),
        name="last_step",
    )(tiles, seeds, current, received)


def exchange(rows_out, peers):
    count, width = rows_out.shape
    sent = rows_out.reshape(peers, count // peers, width)
    got = lax.all_to_all(sent, "rows", split_axis=0, concat_axis=0, tiled=True)
    return got.reshape(count, width)


def on_device(seeds, neighbor_pos, edge_weight, tile_blocks, wanted):
    rows, width = seeds.shape
    peers, slots = wanted.shape[1:]
    asked = lax.all_to_all(
        wanted.reshape(peers, 1, slots), "rows", split_axis=0, concat_axis=0, tiled=True
    )
    tiles = build_tiles(tile_blocks, neighbor_pos.T, edge_weight.T, rows + peers * slots)
    outgoing, pick = pick_rows(asked, seeds)
    received = exchange(outgoing, peers)
    current, outgoing = first_step(tiles, pick, seeds, received)
    received = exchange(outgoing, peers)
    return last_step(tiles, seeds, current, received)


def solution(mesh):
    in_specs = (
        P(("parts", "rows"), "cls"),
        P(("parts", "rows"), None),
        P(("parts", "rows"), None),
        P(("parts", "rows"), None),
        P(("parts", "rows"), None, None),
    )
    out_specs = P(("parts", "rows"), "cls")
    return jax.shard_map(
        on_device, mesh=mesh, in_specs=in_specs, out_specs=out_specs, check_vma=False
    )
```

```python
import jax
import jax.numpy as jnp
from jax import lax
from jax.experimental import pallas as pl
from jax.experimental.pallas import tpu as pltpu
from jax.sharding import PartitionSpec as P

BLK = 128
COLS = 256
VMEM_LIMIT = 32 * 1024 * 1024
KEEP = 0.85
ANCHOR = 0.15

SMEM = pl.BlockSpec(memory_space=pltpu.SMEM)
VMEM = pl.BlockSpec(memory_space=pltpu.VMEM)
ANY = pl.BlockSpec(memory_space=pl.ANY)


def call(kernel, name, out_shape, in_specs, out_specs=VMEM, scratch_shapes=(), flops=0, nbytes=0):
    return pl.pallas_call(
        kernel,
        out_shape=out_shape,
        in_specs=in_specs,
        out_specs=out_specs,
        scratch_shapes=scratch_shapes,
        compiler_params=pltpu.CompilerParams(vmem_limit_bytes=VMEM_LIMIT),
        cost_estimate=pl.CostEstimate(flops=flops, bytes_accessed=nbytes, transcendentals=0),
        name=name,
    )


def dot(a, b):
    return jnp.dot(a, b, preferred_element_type=jnp.float32)


def column_loop(width, body):
    @pl.loop(0, width // COLS)
    def _(c):
        body(pl.ds(pl.multiple_of(c * COLS, COLS), COLS))


def edges_kernel(blocks_ref, pos_ref, weight_ref, column_ref, share_ref):
    block_count, tile_count = blocks_ref.shape
    weights = weight_ref[...].astype(jnp.float32)
    share = weights / jnp.sum(weights, axis=0, keepdims=True)
    share_ref[...] = share.astype(jnp.bfloat16).astype(jnp.float32)
    for block in range(block_count):
        lanes = slice(block * BLK, (block + 1) * BLK)
        pos = pos_ref[:, lanes]
        tile = pos // BLK
        base = jnp.full(pos.shape, blocks_ref[block, 0], jnp.int32)
        for j in range(1, tile_count):
            base = jnp.where(tile == j, blocks_ref[block, j], base)
        column_ref[:, lanes] = base * BLK + pos % BLK


def tiles_kernel(column_ref, share_ref, pick_ref, tiles_ref):
    del pick_ref
    neighbours = column_ref.shape[0]
    sub = lax.broadcasted_iota(jnp.int32, (BLK, BLK), 0)

    @pl.loop(0, tiles_ref.shape[0] // BLK)
    def _(block):
        lanes = pl.ds(pl.multiple_of(block * BLK, BLK), BLK)

        @pl.loop(0, tiles_ref.shape[1] // BLK)
        def _(chunk):
            first = pl.multiple_of(chunk * BLK, BLK)
            total = jnp.zeros((BLK, BLK), jnp.float32)
            for k in range(neighbours):
                spot = column_ref[k : k + 1, lanes] - first
                total = jnp.where(sub == spot, share_ref[k : k + 1, lanes], total)
            tiles_ref[lanes, pl.ds(first, BLK)] = total.T.astype(jnp.bfloat16)


def pick_kernel(asked_ref, seeds_ref, out_ref, pick_ref):
    peers, _, slots = asked_ref.shape
    rows = seeds_ref.shape[0]
    count = peers * slots
    spread = jnp.broadcast_to(asked_ref[...].astype(jnp.float32), (peers, slots, slots))
    spread = spread.reshape(count, slots)
    slot = lax.broadcasted_iota(jnp.int32, (count, slots), 0) % slots
    lane = lax.broadcasted_iota(jnp.int32, (count, slots), 1)
    row = jnp.sum(jnp.where(slot == lane, spread, 0.0), axis=1, keepdims=True)
    hits = lax.broadcasted_iota(jnp.int32, (count, rows), 1) == row.astype(jnp.int32)
    pick_ref[...] = hits.astype(jnp.float32).astype(jnp.bfloat16)

    def body(cols):
        out_ref[:, cols] = dot(pick_ref[...], seeds_ref[:, cols]).astype(jnp.bfloat16)

    column_loop(seeds_ref.shape[1], body)


def own_kernel(tiles_ref, pick_ref, seeds_ref, sent_ref, picked_ref, base_ref, sent_base_ref):
    rows, width = seeds_ref.shape

    def pick_tiles(cols):
        picked_ref[:, cols] = dot(pick_ref[...], tiles_ref[:, cols]).astype(jnp.bfloat16)

    column_loop(tiles_ref.shape[1], pick_tiles)

    def body(cols):
        seeds = seeds_ref[:, cols]
        sent_base_ref[:, cols] = KEEP * dot(picked_ref[:, :rows], seeds) + ANCHOR * sent_ref[
            :, cols
        ].astype(jnp.float32)
        base_ref[:, cols] = KEEP * dot(tiles_ref[:, :rows], seeds) + ANCHOR * seeds.astype(
            jnp.float32
        )

    column_loop(width, body)


def send_kernel(picked_ref, received_ref, sent_base_ref, out_ref):
    rows = picked_ref.shape[1] - received_ref.shape[0]

    def body(cols):
        total = KEEP * dot(picked_ref[:, rows:], received_ref[:, cols]) + sent_base_ref[:, cols]
        out_ref[:, cols] = total.astype(jnp.bfloat16)

    column_loop(received_ref.shape[1], body)


def labels_kernel(tiles_ref, received_ref, base_ref, seeds_ref, next_base_ref):
    rows, width = seeds_ref.shape

    def body(cols):
        total = KEEP * dot(tiles_ref[:, rows:], received_ref[:, cols]) + base_ref[:, cols]
        labels = total.astype(jnp.bfloat16)
        next_base_ref[:, cols] = KEEP * dot(tiles_ref[:, :rows], labels) + ANCHOR * seeds_ref[
            :, cols
        ].astype(jnp.float32)

    column_loop(width, body)


def last_kernel(tiles_ref, received_ref, base_ref, out_ref, labels_ref, sems):
    rows, width = base_ref.shape
    copies = []
    for c in range(width // COLS):
        cols = slice(c * COLS, (c + 1) * COLS)
        total = KEEP * dot(tiles_ref[:, rows:], received_ref[:, cols]) + base_ref[:, cols]
        labels_ref[:, cols] = total.astype(jnp.bfloat16)
        copies.append(
            pltpu.make_async_copy(labels_ref.at[:, cols], out_ref.at[:, cols], sems.at[c])
        )
        copies[-1].start()
    for copy in copies:
        copy.wait()


def exchange(rows_out, peers):
    count, width = rows_out.shape
    sent = rows_out.reshape(peers, count // peers, width)
    got = lax.all_to_all(sent, "rows", split_axis=0, concat_axis=0, tiled=True)
    return got.reshape(count, width)


def on_device(seeds, neighbor_pos, edge_weight, tile_blocks, wanted):
    rows, width = seeds.shape
    peers, slots = wanted.shape[1:]
    count = peers * slots
    columns = rows + count
    neighbours = neighbor_pos.shape[1]
    bf16 = lambda *shape: jax.ShapeDtypeStruct(shape, jnp.bfloat16)
    f32 = lambda *shape: jax.ShapeDtypeStruct(shape, jnp.float32)

    asked = lax.all_to_all(
        wanted.reshape(peers, 1, slots), "rows", split_axis=0, concat_axis=0, tiled=True
    )
    column, share = call(
        edges_kernel,
        "edges",
        [jax.ShapeDtypeStruct((neighbours, rows), jnp.int32), f32(neighbours, rows)],
        [SMEM, VMEM, VMEM],
        [VMEM, VMEM],
        nbytes=16 * neighbours * rows,
    )(tile_blocks, neighbor_pos.T, edge_weight.T)
    outgoing, pick = call(
        pick_kernel,
        "pick",
        [bf16(count, width), bf16(count, rows)],
        [VMEM, VMEM],
        [VMEM, VMEM],
        flops=2 * count * rows * width,
        nbytes=2 * (2 * count * width + count * rows),
    )(asked, seeds)
    received = exchange(outgoing, peers)
    tiles = call(
        tiles_kernel,
        "tiles",
        bf16(rows, columns),
        [VMEM, VMEM, ANY],
        flops=2 * neighbours * rows * columns,
        nbytes=rows * columns * 2,
    )(column, share, pick)
    picked, base, sent_base = call(
        own_kernel,
        "own",
        [bf16(count, columns), f32(rows, width), f32(count, width)],
        [VMEM] * 4,
        [VMEM] * 3,
        flops=2 * rows * (count * columns + count * width + rows * width),
        nbytes=4 * (rows + count) * width,
    )(tiles, pick, seeds, outgoing)
    outgoing = call(
        send_kernel,
        "send",
        bf16(count, width),
        [VMEM] * 3,
        flops=2 * count * count * width,
        nbytes=8 * count * width,
    )(picked, received, sent_base)
    received_next = exchange(outgoing, peers)
    next_base = call(
        labels_kernel,
        "labels",
        f32(rows, width),
        [VMEM] * 4,
        flops=2 * rows * (count + rows) * width,
        nbytes=8 * (rows + count) * width,
    )(tiles, received, base, seeds)
    return call(
        last_kernel,
        "last",
        bf16(rows, width),
        [VMEM] * 3,
        ANY,
        [pltpu.VMEM((rows, width), jnp.bfloat16), pltpu.SemaphoreType.DMA((width // COLS,))],
        flops=2 * rows * count * width,
        nbytes=8 * rows * width,
    )(tiles, received_next, next_base)


def solution(mesh):
    in_specs = (
        P(("parts", "rows"), "cls"),
        P(("parts", "rows"), None),
        P(("parts", "rows"), None),
        P(("parts", "rows"), None),
        P(("parts", "rows"), None, None),
    )
    out_specs = P(("parts", "rows"), "cls")
    return jax.shard_map(
        on_device, mesh=mesh, in_specs=in_specs, out_specs=out_specs, check_vma=False
    )
```

```python
import jax
import jax.numpy as jnp
from jax import lax
from jax.experimental import pallas as pl
from jax.experimental.pallas import tpu as pltpu
from jax.sharding import PartitionSpec as P

BLK = 128
COLS = 256
VMEM_LIMIT = 32 * 1024 * 1024
KEEP = 0.85
ANCHOR = 0.15

SMEM = pl.BlockSpec(memory_space=pltpu.SMEM)
VMEM = pl.BlockSpec(memory_space=pltpu.VMEM)
HBM = pl.BlockSpec(memory_space=pltpu.HBM)


def call(kernel, name, out_shape, in_specs, out_specs=VMEM, scratch_shapes=(), flops=0, nbytes=0):
    return pl.pallas_call(
        kernel,
        out_shape=out_shape,
        in_specs=in_specs,
        out_specs=out_specs,
        scratch_shapes=scratch_shapes,
        compiler_params=pltpu.CompilerParams(vmem_limit_bytes=VMEM_LIMIT),
        cost_estimate=pl.CostEstimate(flops=flops, bytes_accessed=nbytes, transcendentals=0),
        name=name,
    )


def dot(a, b):
    return jnp.dot(a, b, preferred_element_type=jnp.float32)


def column_loop(width, body):
    @pl.loop(0, width // COLS)
    def _(c):
        body(pl.ds(pl.multiple_of(c * COLS, COLS), COLS))


def pull(source, target, sems, columns):
    copies = []
    for c in range(columns // COLS):
        cols = slice(c * COLS, (c + 1) * COLS)
        copies.append(pltpu.make_async_copy(source.at[:, cols], target.at[:, cols], sems.at[c]))
        copies[-1].start()
    return copies


def push(source, target, sems, c):
    cols = slice(c * COLS, (c + 1) * COLS)
    copy = pltpu.make_async_copy(source.at[:, cols], target.at[:, cols], sems.at[c])
    copy.start()
    return copy


def picks(asked, rows):
    peers, _, slots = asked.shape
    count = peers * slots
    spread = jnp.broadcast_to(asked.astype(jnp.float32), (peers, slots, slots))
    spread = spread.reshape(count, slots)
    slot = lax.broadcasted_iota(jnp.int32, (count, slots), 0) % slots
    lane = lax.broadcasted_iota(jnp.int32, (count, slots), 1)
    row = jnp.sum(jnp.where(slot == lane, spread, 0.0), axis=1, keepdims=True)
    hits = lax.broadcasted_iota(jnp.int32, (count, rows), 1) == row.astype(jnp.int32)
    return hits.astype(jnp.float32).astype(jnp.bfloat16)


def pick_kernel(asked_ref, seeds_hbm, out_hbm, seeds_ref, pick_ref, out_ref, in_sems, out_sems):
    rows, width = seeds_ref.shape
    copies = pull(seeds_hbm, seeds_ref, in_sems, width)
    pick_ref[...] = picks(asked_ref[...], rows)
    pushed = []
    for c, copy in enumerate(copies):
        cols = slice(c * COLS, (c + 1) * COLS)
        copy.wait()
        out_ref[:, cols] = dot(pick_ref[...], seeds_ref[:, cols]).astype(jnp.bfloat16)
        pushed.append(push(out_ref, out_hbm, out_sems, c))
    for copy in pushed:
        copy.wait()


def fill_edges(blocks_ref, pos_ref, weight_ref, column_ref, share_ref):
    block_count, tile_count = blocks_ref.shape
    weights = weight_ref[...].astype(jnp.float32)
    share = weights / jnp.sum(weights, axis=0, keepdims=True)
    share_ref[...] = share.astype(jnp.bfloat16).astype(jnp.float32)
    for block in range(block_count):
        lanes = slice(block * BLK, (block + 1) * BLK)
        pos = pos_ref[:, lanes]
        tile = pos // BLK
        base = jnp.full(pos.shape, blocks_ref[block, 0], jnp.int32)
        for j in range(1, tile_count):
            base = jnp.where(tile == j, blocks_ref[block, j], base)
        column_ref[:, lanes] = base * BLK + pos % BLK


def fill_tiles(column_ref, share_ref, tiles_ref):
    neighbours = column_ref.shape[0]
    sub = lax.broadcasted_iota(jnp.int32, (BLK, BLK), 0)

    @pl.loop(0, tiles_ref.shape[0] // BLK)
    def _(block):
        lanes = pl.ds(pl.multiple_of(block * BLK, BLK), BLK)

        @pl.loop(0, tiles_ref.shape[1] // BLK)
        def _(chunk):
            first = pl.multiple_of(chunk * BLK, BLK)
            total = jnp.zeros((BLK, BLK), jnp.float32)
            for k in range(neighbours):
                spot = column_ref[k : k + 1, lanes] - first
                total = jnp.where(sub == spot, share_ref[k : k + 1, lanes], total)
            tiles_ref[lanes, pl.ds(first, BLK)] = total.T.astype(jnp.bfloat16)


def tiles_kernel(
    blocks_ref,
    pos_ref,
    weight_ref,
    asked_ref,
    seeds_ref,
    sent_ref,
    own_ref,
    far_ref,
    picked_far_ref,
    base_ref,
    sent_base_ref,
    column_ref,
    share_ref,
    tiles_ref,
    pick_ref,
    picked_ref,
):
    rows, width = seeds_ref.shape
    fill_edges(blocks_ref, pos_ref, weight_ref, column_ref, share_ref)
    fill_tiles(column_ref, share_ref, tiles_ref)
    own_ref[...] = tiles_ref[:, :rows]
    far_ref[...] = tiles_ref[:, rows:]
    pick_ref[...] = picks(asked_ref[...], rows)

    def pick_tiles(cols):
        picked_ref[:, cols] = dot(pick_ref[...], tiles_ref[:, cols]).astype(jnp.bfloat16)

    column_loop(tiles_ref.shape[1], pick_tiles)
    picked_far_ref[...] = picked_ref[:, rows:]

    def body(cols):
        seeds = seeds_ref[:, cols]
        sent_base_ref[:, cols] = KEEP * dot(picked_ref[:, :rows], seeds) + ANCHOR * sent_ref[
            :, cols
        ].astype(jnp.float32)
        base_ref[:, cols] = KEEP * dot(tiles_ref[:, :rows], seeds) + ANCHOR * seeds.astype(
            jnp.float32
        )

    column_loop(width, body)


def step_kernel(tiles_ref, received_ref, base_hbm, out_hbm, base_ref, out_ref, in_sems, out_sems):
    copies = pull(base_hbm, base_ref, in_sems, base_ref.shape[1])
    pushed = []
    for c, copy in enumerate(copies):
        cols = slice(c * COLS, (c + 1) * COLS)
        total = KEEP * dot(tiles_ref[...], received_ref[:, cols])
        copy.wait()
        out_ref[:, cols] = (total + base_ref[:, cols]).astype(jnp.bfloat16)
        pushed.append(push(out_ref, out_hbm, out_sems, c))
    for copy in pushed:
        copy.wait()


def labels_kernel(own_ref, far_ref, received_ref, base_ref, seeds_ref, next_base_ref):
    def body(cols):
        total = KEEP * dot(far_ref[...], received_ref[:, cols]) + base_ref[:, cols]
        labels = total.astype(jnp.bfloat16)
        next_base_ref[:, cols] = KEEP * dot(own_ref[...], labels) + ANCHOR * seeds_ref[
            :, cols
        ].astype(jnp.float32)

    column_loop(seeds_ref.shape[1], body)


def step(tiles, received, base, name):
    rows, width = base.shape
    pieces = pltpu.SemaphoreType.DMA((width // COLS,))
    return call(
        step_kernel,
        name,
        jax.ShapeDtypeStruct((rows, width), jnp.bfloat16),
        [VMEM, VMEM, HBM],
        HBM,
        [
            pltpu.VMEM((rows, width), jnp.float32),
            pltpu.VMEM((rows, width), jnp.bfloat16),
            pieces,
            pieces,
        ],
        flops=2 * rows * received.shape[0] * width,
        nbytes=8 * rows * width,
    )(tiles, received, base)


def exchange(rows_out, peers):
    count, width = rows_out.shape
    sent = rows_out.reshape(peers, count // peers, width)
    got = lax.all_to_all(sent, "rows", split_axis=0, concat_axis=0, tiled=True)
    return got.reshape(count, width)


def on_device(seeds, neighbor_pos, edge_weight, tile_blocks, wanted):
    rows, width = seeds.shape
    peers, slots = wanted.shape[1:]
    count = peers * slots
    columns = rows + count
    neighbours = neighbor_pos.shape[1]
    bf16 = lambda *shape: jax.ShapeDtypeStruct(shape, jnp.bfloat16)
    f32 = lambda *shape: jax.ShapeDtypeStruct(shape, jnp.float32)

    pieces = pltpu.SemaphoreType.DMA((width // COLS,))

    asked = lax.all_to_all(
        wanted.reshape(peers, 1, slots), "rows", split_axis=0, concat_axis=0, tiled=True
    )
    outgoing = call(
        pick_kernel,
        "pick",
        bf16(count, width),
        [VMEM, HBM],
        HBM,
        [
            pltpu.VMEM((rows, width), jnp.bfloat16),
            pltpu.VMEM((count, rows), jnp.bfloat16),
            pltpu.VMEM((count, width), jnp.bfloat16),
            pieces,
            pieces,
        ],
        flops=2 * count * rows * width,
        nbytes=2 * (rows + count) * width,
    )(asked, seeds)
    received = exchange(outgoing, peers)
    own, far, picked_far, base, sent_base = call(
        tiles_kernel,
        "tiles",
        [
            bf16(rows, rows),
            bf16(rows, count),
            bf16(count, count),
            f32(rows, width),
            f32(count, width),
        ],
        [SMEM, VMEM, VMEM, VMEM, VMEM, VMEM],
        [VMEM] * 5,
        [
            pltpu.VMEM((neighbours, rows), jnp.int32),
            pltpu.VMEM((neighbours, rows), jnp.float32),
            pltpu.VMEM((rows, columns), jnp.bfloat16),
            pltpu.VMEM((count, rows), jnp.bfloat16),
            pltpu.VMEM((count, columns), jnp.bfloat16),
        ],
        flops=2 * neighbours * rows * columns,
        nbytes=4 * (rows + count) * width,
    )(tile_blocks, neighbor_pos.T, edge_weight.T, asked, seeds, outgoing)
    outgoing = step(picked_far, received, sent_base, "send")
    received_next = exchange(outgoing, peers)
    next_base = call(
        labels_kernel,
        "labels",
        f32(rows, width),
        [VMEM] * 5,
        flops=2 * rows * (count + rows) * width,
        nbytes=8 * (rows + count) * width,
    )(own, far, received, base, seeds)
    return step(far, received_next, next_base, "last")


def solution(mesh):
    in_specs = (
        P(("parts", "rows"), "cls"),
        P(("parts", "rows"), None),
        P(("parts", "rows"), None),
        P(("parts", "rows"), None),
        P(("parts", "rows"), None, None),
    )
    out_specs = P(("parts", "rows"), "cls")
    return jax.shard_map(
        on_device, mesh=mesh, in_specs=in_specs, out_specs=out_specs, check_vma=False
    )
```

```python
import math

import jax
import jax.numpy as jnp
from jax import lax
from jax.experimental import pallas as pl
from jax.experimental.pallas import tpu as pltpu
from jax.sharding import PartitionSpec as P

BLK = 128
COLS = 256
VMEM_LIMIT = 32 * 1024 * 1024
NEAR_BYTES = 1024 * 1024
KEEP = 0.85
ANCHOR = 0.15

SMEM = pl.BlockSpec(memory_space=pltpu.SMEM)
VMEM = pl.BlockSpec(memory_space=pltpu.VMEM)
HBM = pl.BlockSpec(memory_space=pltpu.HBM)


def far_out(shape, dtype):
    return pltpu.HBM(shape, dtype)


def far_in(x):
    return pltpu.with_memory_space_constraint(x, pltpu.HBM)


def near_out(shape, dtype):
    small = math.prod(shape) * jnp.dtype(dtype).itemsize <= NEAR_BYTES
    return pltpu.VMEM(shape, dtype) if small else jax.ShapeDtypeStruct(shape, dtype)


def call(kernel, name, out_shape, in_specs, out_specs=VMEM, scratch_shapes=(), flops=0, nbytes=0, aliases=None):
    return pl.pallas_call(
        kernel,
        out_shape=out_shape,
        in_specs=in_specs,
        out_specs=out_specs,
        scratch_shapes=scratch_shapes,
        input_output_aliases=aliases or {},
        compiler_params=pltpu.CompilerParams(vmem_limit_bytes=VMEM_LIMIT),
        cost_estimate=pl.CostEstimate(flops=flops, bytes_accessed=nbytes, transcendentals=0),
        name=name,
    )


def dot(a, b):
    return jnp.dot(a, b, preferred_element_type=jnp.float32)


def column_loop(width, body):
    @pl.loop(0, width // COLS)
    def _(c):
        body(pl.ds(pl.multiple_of(c * COLS, COLS), COLS))


def push(source, target, sems, c):
    cols = slice(c * COLS, (c + 1) * COLS)
    copy = pltpu.make_async_copy(source.at[:, cols], target.at[:, cols], sems.at[c])
    copy.start()
    return copy


def picks(asked, rows):
    peers, _, slots = asked.shape
    count = peers * slots
    spread = jnp.broadcast_to(asked.astype(jnp.float32), (peers, slots, slots))
    spread = spread.reshape(count, slots)
    slot = lax.broadcasted_iota(jnp.int32, (count, slots), 0) % slots
    lane = lax.broadcasted_iota(jnp.int32, (count, slots), 1)
    row = jnp.sum(jnp.where(slot == lane, spread, 0.0), axis=1, keepdims=True)
    hits = lax.broadcasted_iota(jnp.int32, (count, rows), 1) == row.astype(jnp.int32)
    return hits.astype(jnp.float32).astype(jnp.bfloat16)


def stage_kernel(seeds_hbm, seeds_ref, sem):
    copy = pltpu.make_async_copy(seeds_hbm, seeds_ref, sem)
    copy.start()
    copy.wait()


def pick_kernel(asked_ref, seeds_ref, out_hbm, pick_ref, out_ref, out_sems):
    rows, width = seeds_ref.shape
    pick_ref[...] = picks(asked_ref[...], rows)
    pushed = []
    for c in range(width // COLS):
        cols = slice(c * COLS, (c + 1) * COLS)
        out_ref[:, cols] = dot(pick_ref[...], seeds_ref[:, cols]).astype(jnp.bfloat16)
        pushed.append(push(out_ref, out_hbm, out_sems, c))
    for copy in pushed:
        copy.wait()


def fill_edges(blocks_ref, pos_ref, weight_ref, column_ref, share_ref):
    block_count, tile_count = blocks_ref.shape
    weights = weight_ref[...].astype(jnp.float32)
    share = weights / jnp.sum(weights, axis=0, keepdims=True)
    share_ref[...] = share.astype(jnp.bfloat16).astype(jnp.float32)
    for block in range(block_count):
        lanes = slice(block * BLK, (block + 1) * BLK)
        pos = pos_ref[:, lanes]
        tile = pos // BLK
        base = jnp.full(pos.shape, blocks_ref[block, 0], jnp.int32)
        for j in range(1, tile_count):
            base = jnp.where(tile == j, blocks_ref[block, j], base)
        column_ref[:, lanes] = base * BLK + pos % BLK


def fill_tiles(column_ref, share_ref, tiles_ref):
    neighbours = column_ref.shape[0]
    sub = lax.broadcasted_iota(jnp.int32, (BLK, BLK), 0)

    @pl.loop(0, tiles_ref.shape[0] // BLK)
    def _(block):
        lanes = pl.ds(pl.multiple_of(block * BLK, BLK), BLK)

        @pl.loop(0, tiles_ref.shape[1] // BLK)
        def _(chunk):
            first = pl.multiple_of(chunk * BLK, BLK)
            total = jnp.zeros((BLK, BLK), jnp.float32)
            for k in range(neighbours):
                spot = column_ref[k : k + 1, lanes] - first
                total = jnp.where(sub == spot, share_ref[k : k + 1, lanes], total)
            tiles_ref[lanes, pl.ds(first, BLK)] = total.T.astype(jnp.bfloat16)


def tiles_kernel(
    blocks_ref,
    pos_ref,
    weight_ref,
    asked_ref,
    seeds_ref,
    sent_ref,
    own_ref,
    far_ref,
    picked_far_ref,
    base_ref,
    sent_base_ref,
    column_ref,
    share_ref,
    tiles_ref,
    pick_ref,
    picked_ref,
):
    rows, width = seeds_ref.shape
    fill_edges(blocks_ref, pos_ref, weight_ref, column_ref, share_ref)
    fill_tiles(column_ref, share_ref, tiles_ref)
    own_ref[...] = tiles_ref[:, :rows]
    far_ref[...] = tiles_ref[:, rows:]
    pick_ref[...] = picks(asked_ref[...], rows)

    def pick_tiles(cols):
        picked_ref[:, cols] = dot(pick_ref[...], tiles_ref[:, cols]).astype(jnp.bfloat16)

    column_loop(tiles_ref.shape[1], pick_tiles)
    picked_far_ref[...] = picked_ref[:, rows:]

    def body(cols):
        seeds = seeds_ref[:, cols]
        sent = ANCHOR * sent_ref[:, cols].astype(jnp.float32)
        sent_base = KEEP * dot(picked_ref[:, :rows], seeds) + sent
        sent_base_ref[:, cols] = sent_base.astype(jnp.bfloat16)
        base_ref[:, cols] = KEEP * dot(tiles_ref[:, :rows], seeds) + ANCHOR * seeds.astype(
            jnp.float32
        )

    column_loop(width, body)


def step_kernel(tiles_ref, received_ref, base_ref, out_hbm, out_ref, out_sems):
    pushed = []
    for c in range(base_ref.shape[1] // COLS):
        cols = slice(c * COLS, (c + 1) * COLS)
        total = KEEP * dot(tiles_ref[...], received_ref[:, cols])
        out_ref[:, cols] = (total + base_ref[:, cols].astype(jnp.float32)).astype(jnp.bfloat16)
        pushed.append(push(out_ref, out_hbm, out_sems, c))
    for copy in pushed:
        copy.wait()


def labels_kernel(own_ref, far_ref, received_ref, base_ref, seeds_ref, next_base_ref):
    def body(cols):
        total = KEEP * dot(far_ref[...], received_ref[:, cols]) + base_ref[:, cols]
        labels = total.astype(jnp.bfloat16)
        seeds = ANCHOR * seeds_ref[:, cols].astype(jnp.float32)
        next_base_ref[:, cols] = (KEEP * dot(own_ref[...], labels) + seeds).astype(jnp.bfloat16)

    column_loop(seeds_ref.shape[1], body)


def step(tiles, received, base, name):
    rows, width = base.shape
    pieces = pltpu.SemaphoreType.DMA((width // COLS,))
    return call(
        step_kernel,
        name,
        far_out((rows, width), jnp.bfloat16),
        [VMEM, VMEM, VMEM],
        HBM,
        [pltpu.VMEM((rows, width), jnp.bfloat16), pieces],
        flops=2 * rows * received.shape[0] * width,
        nbytes=8 * rows * width,
    )(tiles, received, base)


def exchange(rows_out, peers):
    count, width = rows_out.shape
    sent = rows_out.reshape(peers, count // peers, width)
    got = lax.all_to_all(sent, "rows", split_axis=0, concat_axis=0, tiled=True)
    return got.reshape(count, width)


def on_device(seeds, neighbor_pos, edge_weight, tile_blocks, wanted):
    rows, width = seeds.shape
    peers, slots = wanted.shape[1:]
    count = peers * slots
    columns = rows + count
    neighbours = neighbor_pos.shape[1]

    pieces = pltpu.SemaphoreType.DMA((width // COLS,))

    asked = lax.all_to_all(
        wanted.reshape(peers, 1, slots), "rows", split_axis=0, concat_axis=0, tiled=True
    )
    staged = call(
        stage_kernel,
        "stage",
        near_out((rows, width), jnp.bfloat16),
        [HBM],
        VMEM,
        [pltpu.SemaphoreType.DMA],
        nbytes=4 * rows * width,
    )(far_in(seeds))
    outgoing = call(
        pick_kernel,
        "pick",
        far_out((count, width), jnp.bfloat16),
        [VMEM, VMEM],
        HBM,
        [
            pltpu.VMEM((count, rows), jnp.bfloat16),
            pltpu.VMEM((count, width), jnp.bfloat16),
            pieces,
        ],
        flops=2 * count * rows * width,
        nbytes=2 * (rows + count) * width,
    )(asked, staged)
    received = exchange(outgoing, peers)
    own, far, picked_far, base, sent_base = call(
        tiles_kernel,
        "tiles",
        [
            far_out((rows, rows), jnp.bfloat16),
            near_out((rows, count), jnp.bfloat16),
            near_out((count, count), jnp.bfloat16),
            far_out((rows, width), jnp.float32),
            near_out((count, width), jnp.bfloat16),
        ],
        [SMEM, VMEM, VMEM, VMEM, VMEM, VMEM],
        [VMEM] * 5,
        [
            pltpu.VMEM((neighbours, rows), jnp.int32),
            pltpu.VMEM((neighbours, rows), jnp.float32),
            pltpu.VMEM((rows, columns), jnp.bfloat16),
            pltpu.VMEM((count, rows), jnp.bfloat16),
            pltpu.VMEM((count, columns), jnp.bfloat16),
        ],
        flops=2 * neighbours * rows * columns,
        nbytes=4 * (rows + count) * width,
    )(tile_blocks, neighbor_pos.T, edge_weight.T, asked, far_in(seeds), far_in(outgoing))
    outgoing = step(picked_far, received, sent_base, "send")
    received_next = exchange(outgoing, peers)
    next_base = call(
        labels_kernel,
        "labels",
        near_out((rows, width), jnp.bfloat16),
        [VMEM] * 5,
        flops=2 * rows * (count + rows) * width,
        nbytes=8 * (rows + count) * width,
        aliases={2: 0} if count == rows else None,
    )(far_in(own), far, received, far_in(base), far_in(seeds))
    return step(far, received_next, next_base, "last")


def solution(mesh):
    in_specs = (
        P(("parts", "rows"), "cls"),
        P(("parts", "rows"), None),
        P(("parts", "rows"), None),
        P(("parts", "rows"), None),
        P(("parts", "rows"), None, None),
    )
    out_specs = P(("parts", "rows"), "cls")
    return jax.shard_map(
        on_device, mesh=mesh, in_specs=in_specs, out_specs=out_specs, check_vma=False
    )
```

```python
import math

import jax
import jax.numpy as jnp
from jax import lax
from jax.experimental import pallas as pl
from jax.experimental.pallas import tpu as pltpu
from jax.sharding import PartitionSpec as P

BLK = 128
COLS = 256
VMEM_LIMIT = 32 * 1024 * 1024
NEAR_BYTES = 1024 * 1024
KEEP = 0.85
ANCHOR = 0.15
REST_SCALE = 4096.0

SMEM = pl.BlockSpec(memory_space=pltpu.SMEM)
VMEM = pl.BlockSpec(memory_space=pltpu.VMEM)
HBM = pl.BlockSpec(memory_space=pltpu.HBM)


def far_out(shape, dtype):
    return pltpu.HBM(shape, dtype)


def far_in(x):
    return pltpu.with_memory_space_constraint(x, pltpu.HBM)


def near_out(shape, dtype):
    small = math.prod(shape) * jnp.dtype(dtype).itemsize <= NEAR_BYTES
    return pltpu.VMEM(shape, dtype) if small else jax.ShapeDtypeStruct(shape, dtype)


def call(kernel, name, out_shape, in_specs, out_specs=VMEM, scratch_shapes=(), flops=0, nbytes=0, aliases=None):
    return pl.pallas_call(
        kernel,
        out_shape=out_shape,
        in_specs=in_specs,
        out_specs=out_specs,
        scratch_shapes=scratch_shapes,
        input_output_aliases=aliases or {},
        compiler_params=pltpu.CompilerParams(vmem_limit_bytes=VMEM_LIMIT),
        cost_estimate=pl.CostEstimate(flops=flops, bytes_accessed=nbytes, transcendentals=0),
        name=name,
    )


def dot(a, b):
    return jnp.dot(a, b, preferred_element_type=jnp.float32)


def column_loop(width, body):
    @pl.loop(0, width // COLS)
    def _(c):
        body(pl.ds(pl.multiple_of(c * COLS, COLS), COLS))


def push(source, target, sems, c):
    cols = slice(c * COLS, (c + 1) * COLS)
    copy = pltpu.make_async_copy(source.at[:, cols], target.at[:, cols], sems.at[c])
    copy.start()
    return copy


def picks(asked, rows):
    peers, _, slots = asked.shape
    count = peers * slots
    spread = jnp.broadcast_to(asked.astype(jnp.float32), (peers, slots, slots))
    spread = spread.reshape(count, slots)
    slot = lax.broadcasted_iota(jnp.int32, (count, slots), 0) % slots
    lane = lax.broadcasted_iota(jnp.int32, (count, slots), 1)
    row = jnp.sum(jnp.where(slot == lane, spread, 0.0), axis=1, keepdims=True)
    hits = lax.broadcasted_iota(jnp.int32, (count, rows), 1) == row.astype(jnp.int32)
    return hits.astype(jnp.float32).astype(jnp.bfloat16)


def stage_kernel(seeds_hbm, seeds_ref, sem):
    copy = pltpu.make_async_copy(seeds_hbm, seeds_ref, sem)
    copy.start()
    copy.wait()


def pick_kernel(asked_ref, seeds_ref, out_hbm, pick_ref, out_ref, out_sems):
    rows, width = seeds_ref.shape
    pick_ref[...] = picks(asked_ref[...], rows)
    pushed = []
    for c in range(width // COLS):
        cols = slice(c * COLS, (c + 1) * COLS)
        out_ref[:, cols] = dot(pick_ref[...], seeds_ref[:, cols]).astype(jnp.bfloat16)
        pushed.append(push(out_ref, out_hbm, out_sems, c))
    for copy in pushed:
        copy.wait()


def fill_edges(blocks_ref, pos_ref, weight_ref, column_ref, share_ref):
    block_count, tile_count = blocks_ref.shape
    weights = weight_ref[...].astype(jnp.float32)
    share = weights / jnp.sum(weights, axis=0, keepdims=True)
    share_ref[...] = share.astype(jnp.bfloat16).astype(jnp.float32)
    for block in range(block_count):
        lanes = slice(block * BLK, (block + 1) * BLK)
        pos = pos_ref[:, lanes]
        tile = pos // BLK
        base = jnp.full(pos.shape, blocks_ref[block, 0], jnp.int32)
        for j in range(1, tile_count):
            base = jnp.where(tile == j, blocks_ref[block, j], base)
        column_ref[:, lanes] = base * BLK + pos % BLK


def fill_tiles(column_ref, share_ref, tiles_ref):
    neighbours = column_ref.shape[0]
    sub = lax.broadcasted_iota(jnp.int32, (BLK, BLK), 0)

    @pl.loop(0, tiles_ref.shape[0] // BLK)
    def _(block):
        lanes = pl.ds(pl.multiple_of(block * BLK, BLK), BLK)

        @pl.loop(0, tiles_ref.shape[1] // BLK)
        def _(chunk):
            first = pl.multiple_of(chunk * BLK, BLK)
            total = jnp.zeros((BLK, BLK), jnp.float32)
            for k in range(neighbours):
                spot = column_ref[k : k + 1, lanes] - first
                total = jnp.where(sub == spot, share_ref[k : k + 1, lanes], total)
            tiles_ref[lanes, pl.ds(first, BLK)] = total.T.astype(jnp.bfloat16)


def tiles_kernel(
    blocks_ref,
    pos_ref,
    weight_ref,
    asked_ref,
    seeds_ref,
    sent_ref,
    own_ref,
    far_ref,
    picked_far_ref,
    base_ref,
    sent_base_ref,
    column_ref,
    share_ref,
    tiles_ref,
    pick_ref,
    picked_ref,
):
    rows, width = seeds_ref.shape
    fill_edges(blocks_ref, pos_ref, weight_ref, column_ref, share_ref)
    fill_tiles(column_ref, share_ref, tiles_ref)
    own_ref[...] = tiles_ref[:, :rows]
    far_ref[...] = tiles_ref[:, rows:]
    pick_ref[...] = picks(asked_ref[...], rows)

    def pick_tiles(cols):
        picked_ref[:, cols] = dot(pick_ref[...], tiles_ref[:, cols]).astype(jnp.bfloat16)

    column_loop(tiles_ref.shape[1], pick_tiles)
    picked_far_ref[...] = picked_ref[:, rows:]

    def body(cols):
        seeds = seeds_ref[:, cols]
        sent = ANCHOR * sent_ref[:, cols].astype(jnp.float32)
        sent_base = KEEP * dot(picked_ref[:, :rows], seeds) + sent
        sent_base_ref[:, cols] = sent_base.astype(jnp.bfloat16)
        base_ref[:, cols] = KEEP * dot(tiles_ref[:, :rows], seeds) + ANCHOR * seeds.astype(
            jnp.float32
        )

    column_loop(width, body)


def step_kernel(tiles_ref, received_ref, base_ref, *refs):
    *rest_ref, out_hbm, out_ref, out_sems = refs
    pushed = []
    for c in range(base_ref.shape[1] // COLS):
        cols = slice(c * COLS, (c + 1) * COLS)
        total = KEEP * dot(tiles_ref[...], received_ref[:, cols])
        total = total + base_ref[:, cols].astype(jnp.float32)
        if rest_ref:
            total = total + rest_ref[0][:, cols].astype(jnp.float32) * (1 / REST_SCALE)
        out_ref[:, cols] = total.astype(jnp.bfloat16)
        pushed.append(push(out_ref, out_hbm, out_sems, c))
    for copy in pushed:
        copy.wait()


def labels_kernel(own_ref, far_ref, received_ref, base_ref, seeds_ref, next_base_ref, rest_ref):
    def body(cols):
        total = KEEP * dot(far_ref[...], received_ref[:, cols]) + base_ref[:, cols]
        labels = total.astype(jnp.bfloat16)
        seeds = ANCHOR * seeds_ref[:, cols].astype(jnp.float32)
        next_base = KEEP * dot(own_ref[...], labels) + seeds
        kept = next_base.astype(jnp.bfloat16)
        next_base_ref[:, cols] = kept
        rest = (next_base - kept.astype(jnp.float32)) * REST_SCALE
        rest_ref[:, cols] = rest.astype(jnp.float8_e4m3fn)

    column_loop(seeds_ref.shape[1], body)


def step(name, tiles, received, base, *rest):
    rows, width = base.shape
    pieces = pltpu.SemaphoreType.DMA((width // COLS,))
    return call(
        step_kernel,
        name,
        far_out((rows, width), jnp.bfloat16),
        [VMEM] * (3 + len(rest)),
        HBM,
        [pltpu.VMEM((rows, width), jnp.bfloat16), pieces],
        flops=2 * rows * received.shape[0] * width,
        nbytes=8 * rows * width,
    )(tiles, received, base, *rest)


def exchange(rows_out, peers):
    count, width = rows_out.shape
    sent = rows_out.reshape(peers, count // peers, width)
    got = lax.all_to_all(sent, "rows", split_axis=0, concat_axis=0, tiled=True)
    return got.reshape(count, width)


def on_device(seeds, neighbor_pos, edge_weight, tile_blocks, wanted):
    rows, width = seeds.shape
    peers, slots = wanted.shape[1:]
    count = peers * slots
    columns = rows + count
    neighbours = neighbor_pos.shape[1]

    pieces = pltpu.SemaphoreType.DMA((width // COLS,))

    asked = lax.all_to_all(
        wanted.reshape(peers, 1, slots), "rows", split_axis=0, concat_axis=0, tiled=True
    )
    staged = call(
        stage_kernel,
        "stage",
        near_out((rows, width), jnp.bfloat16),
        [HBM],
        VMEM,
        [pltpu.SemaphoreType.DMA],
        nbytes=4 * rows * width,
    )(far_in(seeds))
    outgoing = call(
        pick_kernel,
        "pick",
        far_out((count, width), jnp.bfloat16),
        [VMEM, VMEM],
        HBM,
        [
            pltpu.VMEM((count, rows), jnp.bfloat16),
            pltpu.VMEM((count, width), jnp.bfloat16),
            pieces,
        ],
        flops=2 * count * rows * width,
        nbytes=2 * (rows + count) * width,
    )(asked, staged)
    received = exchange(outgoing, peers)
    own, far, picked_far, base, sent_base = call(
        tiles_kernel,
        "tiles",
        [
            far_out((rows, rows), jnp.bfloat16),
            near_out((rows, count), jnp.bfloat16),
            near_out((count, count), jnp.bfloat16),
            far_out((rows, width), jnp.float32),
            near_out((count, width), jnp.bfloat16),
        ],
        [SMEM, VMEM, VMEM, VMEM, VMEM, VMEM],
        [VMEM] * 5,
        [
            pltpu.VMEM((neighbours, rows), jnp.int32),
            pltpu.VMEM((neighbours, rows), jnp.float32),
            pltpu.VMEM((rows, columns), jnp.bfloat16),
            pltpu.VMEM((count, rows), jnp.bfloat16),
            pltpu.VMEM((count, columns), jnp.bfloat16),
        ],
        flops=2 * neighbours * rows * columns,
        nbytes=4 * (rows + count) * width,
    )(tile_blocks, neighbor_pos.T, edge_weight.T, asked, far_in(seeds), far_in(outgoing))
    outgoing = step("send", picked_far, received, sent_base)
    received_next = exchange(outgoing, peers)
    next_base, rest = call(
        labels_kernel,
        "labels",
        [near_out((rows, width), jnp.bfloat16), near_out((rows, width), jnp.float8_e4m3fn)],
        [VMEM] * 5,
        [VMEM, VMEM],
        flops=2 * rows * (count + rows) * width,
        nbytes=8 * (rows + count) * width,
        aliases={2: 0} if count == rows else None,
    )(far_in(own), far, received, far_in(base), far_in(seeds))
    return step("last", far, received_next, next_base, rest)


def solution(mesh):
    in_specs = (
        P(("parts", "rows"), "cls"),
        P(("parts", "rows"), None),
        P(("parts", "rows"), None),
        P(("parts", "rows"), None),
        P(("parts", "rows"), None, None),
    )
    out_specs = P(("parts", "rows"), "cls")
    return jax.shard_map(
        on_device, mesh=mesh, in_specs=in_specs, out_specs=out_specs, check_vma=False
    )
```

```python
import functools
import math

import jax
import jax.numpy as jnp
from jax import lax
from jax.experimental import pallas as pl
from jax.experimental.pallas import tpu as pltpu
from jax.sharding import PartitionSpec as P

BLK = 128
COLS = 256
GROUP = 8
PACK = 16
VMEM_LIMIT = 32 * 1024 * 1024
NEAR_BYTES = 1024 * 1024
KEEP = 0.85
ANCHOR = 0.15
REST_SCALE = 4096.0
LONG = 10**12

SMEM = pl.BlockSpec(memory_space=pltpu.SMEM)
VMEM = pl.BlockSpec(memory_space=pltpu.VMEM)
HBM = pl.BlockSpec(memory_space=pltpu.HBM)
ANY = pl.BlockSpec(memory_space=pl.ANY)


def far_out(shape, dtype=jnp.bfloat16):
    return pltpu.HBM(shape, dtype)


def far_in(x):
    return pltpu.with_memory_space_constraint(x, pltpu.HBM)


def near_out(shape, dtype=jnp.bfloat16):
    small = math.prod(shape) * jnp.dtype(dtype).itemsize <= NEAR_BYTES
    return pltpu.VMEM(shape, dtype) if small else jax.ShapeDtypeStruct(shape, dtype)


def call(kernel, name, out_shape, in_specs, out_specs, scratch_shapes=(), flops=0, aliases=None):
    return pl.pallas_call(
        kernel,
        out_shape=out_shape,
        in_specs=in_specs,
        out_specs=out_specs,
        scratch_shapes=scratch_shapes,
        input_output_aliases=aliases or {},
        compiler_params=pltpu.CompilerParams(vmem_limit_bytes=VMEM_LIMIT),
        cost_estimate=pl.CostEstimate(flops=flops, bytes_accessed=0, transcendentals=0),
        name=name,
    )


def dot(a, b):
    return jnp.dot(a, b, preferred_element_type=jnp.float32)


def pieces_of(first, last):
    return [slice(c, min(c + COLS, last)) for c in range(first, last, COLS)]


def moved(cols, by):
    return slice(cols.start + by, cols.stop + by)


def push(source, target, sem):
    copy = pltpu.make_async_copy(source, target, sem)
    copy.start()
    return copy


def picks(asked, rows):
    peers, _, slots = asked.shape
    count = peers * slots
    spread = jnp.broadcast_to(asked.astype(jnp.float32), (peers, slots, slots))
    spread = spread.reshape(count, slots)
    slot = lax.broadcasted_iota(jnp.int32, (count, slots), 0) % slots
    lane = lax.broadcasted_iota(jnp.int32, (count, slots), 1)
    row = jnp.sum(jnp.where(slot == lane, spread, 0.0), axis=1, keepdims=True)
    hits = lax.broadcasted_iota(jnp.int32, (count, rows), 1) == row.astype(jnp.int32)
    return hits.astype(jnp.float32).astype(jnp.bfloat16)


def block(peer, slots):
    return pl.ds(pl.multiple_of(peer * slots, slots), slots)


def to_planes(me, rows_ref, plane_refs, slots):
    for z, plane_ref in enumerate(plane_refs):
        for s in range(2):
            for q in range(GROUP // 2):
                peer = me ^ (GROUP * z + 2 * q + s)
                at = (s * (GROUP // 2) + q) * slots
                plane_ref[at : at + slots, :] = rows_ref[block(peer, slots), :]


def from_pairs(me, pair_refs, rows_ref, slots):
    planes = pair_refs[0].shape[0] // (2 * slots)
    for q, pair_ref in enumerate(pair_refs):
        for s in range(2):
            for z in range(planes):
                peer = me ^ (GROUP * z + 2 * q + s)
                at = (s * planes + z) * slots
                rows_ref[block(peer, slots), :] = pair_ref[at : at + slots, :]


def fill_edges(blocks_ref, pos_ref, weight_ref, column_ref, share_ref):
    block_count, tile_count = blocks_ref.shape
    weights = weight_ref[...].astype(jnp.float32)
    share = weights / jnp.sum(weights, axis=0, keepdims=True)
    share_ref[...] = share.astype(jnp.bfloat16).astype(jnp.float32)
    for b in range(block_count):
        lanes = slice(b * BLK, (b + 1) * BLK)
        pos = pos_ref[:, lanes]
        tile = pos // BLK
        base = jnp.full(pos.shape, blocks_ref[b, 0], jnp.int32)
        for j in range(1, tile_count):
            base = jnp.where(tile == j, blocks_ref[b, j], base)
        column_ref[:, lanes] = base * BLK + pos % BLK


def fill_tiles(column_ref, share_ref, tiles_ref, spot_ref, start, chunks):
    neighbours, rows = column_ref.shape
    sub = lax.broadcasted_iota(jnp.int32, (BLK, BLK), 0).astype(jnp.float32).astype(jnp.bfloat16)
    sub = sub.reshape(BLK // PACK, PACK, BLK)

    @pl.loop(*chunks)
    def _(chunk):
        first = pl.multiple_of(chunk * BLK, BLK)
        spot = column_ref[...] - (start + first)
        spot_ref[...] = jnp.where((spot >= 0) & (spot < BLK), spot, -1).astype(jnp.float32)

        @pl.loop(0, rows // BLK)
        def _(b):
            lanes = pl.ds(pl.multiple_of(b * BLK, BLK), BLK)
            row = lambda ref, k: jnp.broadcast_to(ref[k : k + 1, lanes], (PACK, BLK))
            total = jnp.zeros(sub.shape, jnp.bfloat16)
            for k in range(neighbours):
                spot = row(spot_ref, k).astype(jnp.bfloat16)
                share = row(share_ref, k).astype(jnp.bfloat16)
                total = jnp.where(sub == spot[None], share[None], total)
            tiles_ref[lanes, pl.ds(first, BLK)] = total.reshape(BLK, BLK).T


def own_tiles_kernel(
    blocks_ref, pos_ref, weight_ref, seeds_hbm, own_ref, column_ref, share_ref, near_ref, spot_ref, sem
):
    copy = push(seeds_hbm, near_ref, sem)
    fill_edges(blocks_ref, pos_ref, weight_ref, column_ref, share_ref)
    fill_tiles(column_ref, share_ref, own_ref, spot_ref, 0, (0, own_ref.shape[1] // BLK))
    copy.wait()


def pick_kernel(me_ref, asked_ref, seeds_ref, after_ref, out_a, out_b, *refs):
    *plane_refs, pick_ref, a_ref, b_ref, sems = refs
    del after_ref
    slots = asked_ref.shape[2]
    rows, width = seeds_ref.shape
    wide = a_ref.shape[1]
    pick_ref[...] = picks(asked_ref[...], rows)
    for cols in pieces_of(0, wide):
        a_ref[:, cols] = dot(pick_ref[...], seeds_ref[:, cols]).astype(jnp.bfloat16)
    copies = [push(a_ref, out_a, sems.at[0])]
    to_planes(me_ref[0], a_ref, plane_refs, slots)
    for i, cols in enumerate(pieces_of(wide, width)):
        here = moved(cols, -wide)
        b_ref[:, here] = dot(pick_ref[...], seeds_ref[:, cols]).astype(jnp.bfloat16)
        copies.append(push(b_ref.at[:, here], out_b.at[:, here], sems.at[1 + i]))
    for copy in copies:
        copy.wait()


def far_kernel(
    asked_ref,
    own_ref,
    column_ref,
    share_ref,
    seeds_ref,
    sent_a_ref,
    sent_b_ref,
    after_ref,
    far_ref,
    picked_far_ref,
    sent_base_ref,
    pick_ref,
    picked_ref,
    spot_ref,
):
    del after_ref
    rows, width = seeds_ref.shape
    wide = sent_a_ref.shape[1]
    fill_tiles(column_ref, share_ref, far_ref, spot_ref, rows, (0, far_ref.shape[1] // BLK))
    pick_ref[...] = picks(asked_ref[...], rows)
    for cols in pieces_of(0, far_ref.shape[1]):
        picked_far_ref[:, cols] = dot(pick_ref[...], far_ref[:, cols]).astype(jnp.bfloat16)
    for cols in pieces_of(0, rows):
        picked_ref[:, cols] = dot(pick_ref[...], own_ref[:, cols]).astype(jnp.bfloat16)
    for cols in pieces_of(0, wide) + pieces_of(wide, width):
        sent = sent_a_ref[:, cols] if cols.stop <= wide else sent_b_ref[:, moved(cols, -wide)]
        sent_base = KEEP * dot(picked_ref[...], seeds_ref[:, cols])
        sent_base = sent_base + ANCHOR * sent.astype(jnp.float32)
        sent_base_ref[:, cols] = sent_base.astype(jnp.bfloat16)


def gather_kernel(*refs):
    *plane_refs, out_ref = refs
    half = plane_refs[0].shape[0] // 2
    for z, plane_ref in enumerate(plane_refs):
        out_ref[z * half : (z + 1) * half, :] = plane_ref[half:, :]


def pair_kernel(slots, *refs):
    count = GROUP // 2
    *plane_refs, other_ref = refs[:-count]
    planes = len(plane_refs)
    for q, out_ref in enumerate(refs[-count:]):
        for z, plane_ref in enumerate(plane_refs):
            here = slice(z * slots, (z + 1) * slots)
            there = slice((planes + z) * slots, (planes + z + 1) * slots)
            other = (z * count + q) * slots
            out_ref[here, :] = plane_ref[q * slots : (q + 1) * slots, :]
            out_ref[there, :] = other_ref[other : other + slots, :]


def send_a_kernel(me_ref, tiles_ref, base_ref, *refs, slots):
    pair_refs = refs[: GROUP // 2]
    out_hbm, *plane_refs, received_ref, out_ref, sem = refs[GROUP // 2 :]
    me = me_ref[0]
    from_pairs(me, pair_refs, received_ref, slots)
    copy = push(received_ref, out_hbm, sem)
    for cols in pieces_of(0, received_ref.shape[1]):
        total = KEEP * dot(tiles_ref[...], received_ref[:, cols])
        out_ref[:, cols] = (total + base_ref[:, cols].astype(jnp.float32)).astype(jnp.bfloat16)
    to_planes(me, out_ref, plane_refs, slots)
    copy.wait()


def send_b_kernel(tiles_ref, base_ref, received_ref, after_ref, out_hbm, kept_hbm, out_ref, sems):
    del after_ref
    wide = base_ref.shape[1] - received_ref.shape[1]
    copies = [push(received_ref, kept_hbm, sems.at[0])]
    for i, cols in enumerate(pieces_of(0, received_ref.shape[1])):
        total = KEEP * dot(tiles_ref[...], received_ref[:, cols])
        total = total + base_ref[:, moved(cols, wide)].astype(jnp.float32)
        out_ref[:, cols] = total.astype(jnp.bfloat16)
        copies.append(push(out_ref.at[:, cols], out_hbm.at[:, cols], sems.at[1 + i]))
    for copy in copies:
        copy.wait()


def labels_kernel(
    own_ref,
    far_ref,
    seeds_ref,
    received_a_ref,
    received_b_ref,
    after_ref,
    next_ref,
    rest_ref,
    near_ref,
):
    del after_ref
    near_ref[...] = far_ref[...]
    wide = received_a_ref.shape[1]
    width = seeds_ref.shape[1]
    for cols in pieces_of(0, wide) + pieces_of(wide, width):
        first = cols.stop <= wide
        received = received_a_ref[:, cols] if first else received_b_ref[:, moved(cols, -wide)]
        seeds = ANCHOR * seeds_ref[:, cols].astype(jnp.float32)
        total = dot(own_ref[...], seeds_ref[:, cols]) + dot(far_ref[...], received)
        labels = (KEEP * total + seeds).astype(jnp.bfloat16)
        base = KEEP * dot(own_ref[...], labels) + seeds
        kept = base.astype(jnp.bfloat16)
        next_ref[:, cols] = kept
        rest = (base - kept.astype(jnp.float32)) * REST_SCALE
        rest_ref[:, cols] = rest.astype(jnp.float8_e4m3fn)


def last_kernel(me_ref, tiles_ref, base_ref, rest_ref, received_b_ref, *refs, slots):
    pair_refs = refs[: GROUP // 2]
    out_hbm, received_a_ref, out_ref, sems = refs[GROUP // 2 :]
    wide = received_a_ref.shape[1]
    width = rest_ref.shape[1]
    from_pairs(me_ref[0], pair_refs, received_a_ref, slots)
    copies = []
    for i, cols in enumerate(pieces_of(wide, width) + pieces_of(0, wide)):
        first = cols.stop <= wide
        received = received_a_ref[:, cols] if first else received_b_ref[:, moved(cols, -wide)]
        total = KEEP * dot(tiles_ref[...], received) + base_ref[:, cols].astype(jnp.float32)
        total = total + rest_ref[:, cols].astype(jnp.float32) * (1 / REST_SCALE)
        out_ref[:, cols] = total.astype(jnp.bfloat16)
        copies.append(push(out_ref.at[:, cols], out_hbm.at[:, cols], sems.at[i]))
    for copy in copies:
        copy.wait()


def swap(x, peers, distance):
    return lax.ppermute(x, "rows", [(i, i ^ distance) for i in range(peers)])


def exchange(rows_out, peers):
    count, width = rows_out.shape
    sent = rows_out.reshape(peers, count // peers, width)
    got = lax.all_to_all(sent, "rows", split_axis=0, concat_axis=0, tiled=True)
    return got.reshape(count, width)


def across(planes, peers):
    return [planes[0]] + [swap(x, peers, GROUP * z) for z, x in enumerate(planes) if z]


def within(planes, peers, slots):
    depth, wide = planes[0].shape
    n = len(planes)
    other = call(
        gather_kernel,
        "gather",
        jax.ShapeDtypeStruct((n * depth // 2, wide), jnp.bfloat16),
        [VMEM] * n,
        VMEM,
        flops=LONG,
    )(*planes)
    other = swap(other, peers, 1)
    pairs = call(
        functools.partial(pair_kernel, slots),
        "pair",
        [jax.ShapeDtypeStruct((2 * n * slots, wide), jnp.bfloat16)] * (GROUP // 2),
        [VMEM] * (n + 1),
        [VMEM] * (GROUP // 2),
    )(*planes, other)
    return [pairs[0]] + [swap(x, peers, 2 * q) for q, x in enumerate(pairs) if q]


def on_device(seeds, neighbor_pos, edge_weight, tile_blocks, wanted):
    rows, width = seeds.shape
    peers, slots = wanted.shape[1:]
    count = peers * slots
    neighbours = neighbor_pos.shape[1]
    planes = peers // GROUP
    wide = max(3 * width // 8 // BLK, 1) * BLK
    assert peers & (peers - 1) == 0 and peers >= GROUP
    me = lax.axis_index("rows").astype(jnp.int32).reshape(1)
    sems = pltpu.SemaphoreType.DMA
    bf16 = jnp.bfloat16
    plane_shape = jax.ShapeDtypeStruct((GROUP * slots, wide), bf16)
    n_b = len(pieces_of(wide, width))
    n_all = n_b + len(pieces_of(0, wide))

    asked = lax.all_to_all(
        wanted.reshape(peers, 1, slots), "rows", split_axis=0, concat_axis=0, tiled=True
    )
    own, column, share, near_seeds = call(
        own_tiles_kernel,
        "own_tiles",
        [
            far_out((rows, rows)),
            far_out((neighbours, rows), jnp.int32),
            far_out((neighbours, rows), jnp.float32),
            near_out((rows, width)),
        ],
        [SMEM, VMEM, VMEM, HBM],
        [VMEM] * 4,
        [pltpu.VMEM((neighbours, rows), jnp.float32), sems],
        flops=neighbours * rows * rows,
    )(far_in(tile_blocks), far_in(neighbor_pos.T), far_in(edge_weight.T), far_in(seeds))
    sent_a, sent_b, *sent_planes = call(
        pick_kernel,
        "pick",
        [far_out((count, wide)), far_out((count, width - wide))] + [plane_shape] * planes,
        [SMEM, VMEM, VMEM, HBM],
        [HBM, HBM] + [VMEM] * planes,
        [
            pltpu.VMEM((count, rows), bf16),
            pltpu.VMEM((count, wide), bf16),
            pltpu.VMEM((count, width - wide), bf16),
            sems((1 + n_b,)),
        ],
        flops=2 * count * rows * width,
    )(me, asked, near_seeds, far_in(own))
    got_planes = across(sent_planes, peers)
    received_b = exchange(sent_b, peers)
    got_pairs = within(got_planes, peers, slots)
    far, picked_far, sent_base = call(
        far_kernel,
        "far",
        [far_out((rows, count)), near_out((count, count)), near_out((count, width))],
        [VMEM] * 7 + [ANY],
        [VMEM] * 3,
        [
            pltpu.VMEM((count, rows), bf16),
            pltpu.VMEM((count, rows), bf16),
            pltpu.VMEM((neighbours, rows), jnp.float32),
        ],
        flops=2 * rows * count * (count + rows + width) + neighbours * rows * count,
    )(
        asked,
        far_in(own),
        far_in(column),
        far_in(share),
        far_in(seeds),
        far_in(sent_a),
        far_in(sent_b),
        got_pairs[0],
    )
    received_a, *sent_planes = call(
        functools.partial(send_a_kernel, slots=slots),
        "send_a",
        [far_out((count, wide))] + [plane_shape] * planes,
        [SMEM] + [VMEM] * (2 + GROUP // 2),
        [HBM] + [VMEM] * planes,
        [pltpu.VMEM((count, wide), bf16), pltpu.VMEM((count, wide), bf16), sems],
        flops=2 * count * count * wide,
    )(me, picked_far, sent_base, *got_pairs)
    got_planes = across(sent_planes, peers)
    sent_b, received_b = call(
        send_b_kernel,
        "send_b",
        [far_out((count, width - wide)), far_out((count, width - wide))],
        [VMEM] * 3 + [ANY],
        [HBM, HBM],
        [pltpu.VMEM((count, width - wide), bf16), sems((1 + n_b,))],
        flops=2 * count * count * (width - wide),
    )(picked_far, sent_base, received_b, sent_planes[0])
    last_b = exchange(sent_b, peers)
    got_pairs = within(got_planes, peers, slots)
    next_base, rest, near_far = call(
        labels_kernel,
        "labels",
        [
            near_out((rows, width)),
            near_out((rows, width), jnp.float8_e4m3fn),
            near_out((rows, count)),
        ],
        [VMEM] * 5 + [ANY],
        [VMEM] * 3,
        flops=2 * rows * (count + 2 * rows) * width,
    )(
        far_in(own),
        far_in(far),
        far_in(seeds),
        far_in(received_a),
        far_in(received_b),
        got_pairs[0],
    )
    return call(
        functools.partial(last_kernel, slots=slots),
        "last",
        far_out((rows, width)),
        [SMEM] + [VMEM] * (4 + GROUP // 2),
        HBM,
        [pltpu.VMEM((count, wide), bf16), pltpu.VMEM((rows, width), bf16), sems((n_all,))],
        flops=2 * rows * count * width,
    )(me, near_far, next_base, rest, last_b, *got_pairs)


def solution(mesh):
    in_specs = (
        P(("parts", "rows"), "cls"),
        P(("parts", "rows"), None),
        P(("parts", "rows"), None),
        P(("parts", "rows"), None),
        P(("parts", "rows"), None, None),
    )
    out_specs = P(("parts", "rows"), "cls")
    return jax.shard_map(
        on_device, mesh=mesh, in_specs=in_specs, out_specs=out_specs, check_vma=False
    )
```

```python
import functools
import math

import jax
import jax.numpy as jnp
from jax import lax
from jax.experimental import pallas as pl
from jax.experimental.pallas import tpu as pltpu
from jax.sharding import PartitionSpec as P

BLK = 128
COLS = 256
GROUP = 8
PACK = 16
VMEM_LIMIT = 32 * 1024 * 1024
NEAR_BYTES = 1024 * 1024
KEEP = 0.85
ANCHOR = 0.15
REST_SCALE = 4096.0
LONG = 4 * 10**10

SMEM = pl.BlockSpec(memory_space=pltpu.SMEM)
VMEM = pl.BlockSpec(memory_space=pltpu.VMEM)
HBM = pl.BlockSpec(memory_space=pltpu.HBM)
ANY = pl.BlockSpec(memory_space=pl.ANY)


def far_out(shape, dtype=jnp.bfloat16):
    return pltpu.HBM(shape, dtype)


def far_in(x):
    return pltpu.with_memory_space_constraint(x, pltpu.HBM)


def near_out(shape, dtype=jnp.bfloat16):
    small = math.prod(shape) * jnp.dtype(dtype).itemsize <= NEAR_BYTES
    return pltpu.VMEM(shape, dtype) if small else jax.ShapeDtypeStruct(shape, dtype)


def call(kernel, name, out_shape, in_specs, out_specs, scratch_shapes=(), flops=0, nbytes=0):
    return pl.pallas_call(
        kernel,
        out_shape=out_shape,
        in_specs=in_specs,
        out_specs=out_specs,
        scratch_shapes=scratch_shapes,
        compiler_params=pltpu.CompilerParams(vmem_limit_bytes=VMEM_LIMIT),
        cost_estimate=pl.CostEstimate(flops=flops, bytes_accessed=nbytes, transcendentals=0),
        name=name,
    )


def dot(a, b):
    return jnp.dot(a, b, preferred_element_type=jnp.float32)


def pieces_of(first, last):
    return [slice(c, min(c + COLS, last)) for c in range(first, last, COLS)]


def moved(cols, by):
    return slice(cols.start + by, cols.stop + by)


def push(source, target, sem):
    copy = pltpu.make_async_copy(source, target, sem)
    copy.start()
    return copy


def picks(asked, rows):
    peers, _, slots = asked.shape
    count = peers * slots
    spread = jnp.broadcast_to(asked.astype(jnp.float32), (peers, slots, slots))
    spread = spread.reshape(count, slots)
    slot = lax.broadcasted_iota(jnp.int32, (count, slots), 0) % slots
    lane = lax.broadcasted_iota(jnp.int32, (count, slots), 1)
    row = jnp.sum(jnp.where(slot == lane, spread, 0.0), axis=1, keepdims=True)
    hits = lax.broadcasted_iota(jnp.int32, (count, rows), 1) == row.astype(jnp.int32)
    return hits.astype(jnp.float32).astype(jnp.bfloat16)


def block(peer, slots):
    return pl.ds(pl.multiple_of(peer * slots, slots), slots)


def to_planes(me, rows_ref, plane_refs, slots):
    for z, plane_ref in enumerate(plane_refs):
        for s in range(2):
            for q in range(GROUP // 2):
                peer = me ^ (GROUP * z + 2 * q + s)
                at = (s * (GROUP // 2) + q) * slots
                plane_ref[at : at + slots, :] = rows_ref[block(peer, slots), :]


def from_pairs(me, pair_refs, rows_ref, slots):
    planes = pair_refs[0].shape[0] // (2 * slots)
    for q, pair_ref in enumerate(pair_refs):
        for s in range(2):
            for z in range(planes):
                peer = me ^ (GROUP * z + 2 * q + s)
                at = (s * planes + z) * slots
                rows_ref[block(peer, slots), :] = pair_ref[at : at + slots, :]


def fill_edges(blocks_ref, pos_ref, weight_ref, column_ref, share_ref):
    block_count, tile_count = blocks_ref.shape
    weights = weight_ref[...].astype(jnp.float32)
    share = weights / jnp.sum(weights, axis=0, keepdims=True)
    share_ref[...] = share.astype(jnp.bfloat16).astype(jnp.float32)
    for b in range(block_count):
        lanes = slice(b * BLK, (b + 1) * BLK)
        pos = pos_ref[:, lanes]
        tile = pos // BLK
        base = jnp.full(pos.shape, blocks_ref[b, 0], jnp.int32)
        for j in range(1, tile_count):
            base = jnp.where(tile == j, blocks_ref[b, j], base)
        column_ref[:, lanes] = base * BLK + pos % BLK


def fill_tiles(column_ref, share_ref, tiles_ref, spot_ref, start, chunks):
    neighbours, rows = column_ref.shape
    sub = lax.broadcasted_iota(jnp.int32, (BLK, BLK), 0).astype(jnp.float32).astype(jnp.bfloat16)
    sub = sub.reshape(BLK // PACK, PACK, BLK)

    @pl.loop(*chunks)
    def _(chunk):
        first = pl.multiple_of(chunk * BLK, BLK)
        spot = column_ref[...] - (start + first)
        spot_ref[...] = jnp.where((spot >= 0) & (spot < BLK), spot, -1).astype(jnp.float32)

        @pl.loop(0, rows // BLK)
        def _(b):
            lanes = pl.ds(pl.multiple_of(b * BLK, BLK), BLK)
            row = lambda ref, k: jnp.broadcast_to(ref[k : k + 1, lanes], (PACK, BLK))
            total = jnp.zeros(sub.shape, jnp.bfloat16)
            for k in range(neighbours):
                spot = row(spot_ref, k).astype(jnp.bfloat16)
                share = row(share_ref, k).astype(jnp.bfloat16)
                total = jnp.where(sub == spot[None], share[None], total)
            tiles_ref[lanes, pl.ds(first, BLK)] = total.reshape(BLK, BLK).T


def own_tiles_kernel(
    blocks_ref,
    pos_ref,
    weight_ref,
    seeds_hbm,
    own_hbm,
    column_hbm,
    share_hbm,
    near_ref,
    own_ref,
    column_ref,
    share_ref,
    spot_ref,
    sems,
):
    copies = [push(seeds_hbm, near_ref, sems.at[0])]
    fill_edges(blocks_ref, pos_ref, weight_ref, column_ref, share_ref)
    copies.append(push(column_ref, column_hbm, sems.at[1]))
    copies.append(push(share_ref, share_hbm, sems.at[2]))
    for i in range(own_ref.shape[1] // BLK):
        cols = slice(i * BLK, (i + 1) * BLK)
        fill_tiles(column_ref, share_ref, own_ref, spot_ref, 0, (i, i + 1))
        copies.append(push(own_ref.at[:, cols], own_hbm.at[:, cols], sems.at[3 + i]))
    for copy in copies:
        copy.wait()


def pick_kernel(me_ref, asked_ref, seeds_ref, after_ref, out_a, out_b, *refs):
    *plane_refs, pick_ref, a_ref, b_ref, sems = refs
    del after_ref
    slots = asked_ref.shape[2]
    rows, width = seeds_ref.shape
    wide = a_ref.shape[1]
    pick_ref[...] = picks(asked_ref[...], rows)
    for cols in pieces_of(0, wide):
        a_ref[:, cols] = dot(pick_ref[...], seeds_ref[:, cols]).astype(jnp.bfloat16)
    copies = [push(a_ref, out_a, sems.at[0])]
    to_planes(me_ref[0], a_ref, plane_refs, slots)
    for i, cols in enumerate(pieces_of(wide, width)):
        here = moved(cols, -wide)
        b_ref[:, here] = dot(pick_ref[...], seeds_ref[:, cols]).astype(jnp.bfloat16)
        copies.append(push(b_ref.at[:, here], out_b.at[:, here], sems.at[1 + i]))
    for copy in copies:
        copy.wait()


def far_kernel(
    asked_ref,
    own_ref,
    column_ref,
    share_ref,
    seeds_ref,
    sent_a_ref,
    sent_b_ref,
    after_ref,
    far_ref,
    picked_far_ref,
    sent_base_ref,
    pick_ref,
    picked_ref,
    spot_ref,
):
    del after_ref
    rows, width = seeds_ref.shape
    wide = sent_a_ref.shape[1]
    fill_tiles(column_ref, share_ref, far_ref, spot_ref, rows, (0, far_ref.shape[1] // BLK))
    pick_ref[...] = picks(asked_ref[...], rows)
    for cols in pieces_of(0, far_ref.shape[1]):
        picked_far_ref[:, cols] = dot(pick_ref[...], far_ref[:, cols]).astype(jnp.bfloat16)
    for cols in pieces_of(0, rows):
        picked_ref[:, cols] = dot(pick_ref[...], own_ref[:, cols]).astype(jnp.bfloat16)
    for cols in pieces_of(0, wide) + pieces_of(wide, width):
        sent = sent_a_ref[:, cols] if cols.stop <= wide else sent_b_ref[:, moved(cols, -wide)]
        sent_base = KEEP * dot(picked_ref[...], seeds_ref[:, cols])
        sent_base = sent_base + ANCHOR * sent.astype(jnp.float32)
        sent_base_ref[:, cols] = sent_base.astype(jnp.bfloat16)


def gather_kernel(*refs):
    *plane_refs, out_ref = refs
    half = plane_refs[0].shape[0] // 2
    for z, plane_ref in enumerate(plane_refs):
        out_ref[z * half : (z + 1) * half, :] = plane_ref[half:, :]


def pair_kernel(slots, *refs):
    count = GROUP // 2
    *plane_refs, other_ref = refs[:-count]
    planes = len(plane_refs)
    for q, out_ref in enumerate(refs[-count:]):
        for z, plane_ref in enumerate(plane_refs):
            here = slice(z * slots, (z + 1) * slots)
            there = slice((planes + z) * slots, (planes + z + 1) * slots)
            other = (z * count + q) * slots
            out_ref[here, :] = plane_ref[q * slots : (q + 1) * slots, :]
            out_ref[there, :] = other_ref[other : other + slots, :]


def send_a_kernel(me_ref, tiles_ref, base_ref, *refs, slots):
    pair_refs = refs[: GROUP // 2]
    out_hbm, *plane_refs, received_ref, out_ref, sem = refs[GROUP // 2 :]
    me = me_ref[0]
    from_pairs(me, pair_refs, received_ref, slots)
    copy = push(received_ref, out_hbm, sem)
    for cols in pieces_of(0, received_ref.shape[1]):
        total = KEEP * dot(tiles_ref[...], received_ref[:, cols])
        out_ref[:, cols] = (total + base_ref[:, cols].astype(jnp.float32)).astype(jnp.bfloat16)
    to_planes(me, out_ref, plane_refs, slots)
    copy.wait()


def send_b_kernel(tiles_ref, base_ref, received_ref, after_ref, out_hbm, kept_hbm, out_ref, sems):
    del after_ref
    wide = base_ref.shape[1] - received_ref.shape[1]
    copies = [push(received_ref, kept_hbm, sems.at[0])]
    for i, cols in enumerate(pieces_of(0, received_ref.shape[1])):
        total = KEEP * dot(tiles_ref[...], received_ref[:, cols])
        total = total + base_ref[:, moved(cols, wide)].astype(jnp.float32)
        out_ref[:, cols] = total.astype(jnp.bfloat16)
        copies.append(push(out_ref.at[:, cols], out_hbm.at[:, cols], sems.at[1 + i]))
    for copy in copies:
        copy.wait()


def labels_kernel(
    own_ref,
    far_ref,
    seeds_ref,
    received_a_ref,
    received_b_ref,
    after_ref,
    next_ref,
    rest_ref,
    near_ref,
):
    del after_ref
    near_ref[...] = far_ref[...]
    wide = received_a_ref.shape[1]
    width = seeds_ref.shape[1]
    for cols in pieces_of(0, wide) + pieces_of(wide, width):
        first = cols.stop <= wide
        received = received_a_ref[:, cols] if first else received_b_ref[:, moved(cols, -wide)]
        seeds = ANCHOR * seeds_ref[:, cols].astype(jnp.float32)
        total = dot(own_ref[...], seeds_ref[:, cols]) + dot(far_ref[...], received)
        labels = (KEEP * total + seeds).astype(jnp.bfloat16)
        base = KEEP * dot(own_ref[...], labels) + seeds
        kept = base.astype(jnp.bfloat16)
        next_ref[:, cols] = kept
        rest = (base - kept.astype(jnp.float32)) * REST_SCALE
        rest_ref[:, cols] = rest.astype(jnp.float8_e4m3fn)


def last_kernel(me_ref, tiles_ref, base_ref, rest_ref, received_b_ref, *refs, slots):
    pair_refs = refs[: GROUP // 2]
    out_hbm, received_a_ref, out_ref, sems = refs[GROUP // 2 :]
    wide = received_a_ref.shape[1]
    width = rest_ref.shape[1]
    from_pairs(me_ref[0], pair_refs, received_a_ref, slots)
    copies = []
    for i, cols in enumerate(pieces_of(wide, width) + pieces_of(0, wide)):
        first = cols.stop <= wide
        received = received_a_ref[:, cols] if first else received_b_ref[:, moved(cols, -wide)]
        total = KEEP * dot(tiles_ref[...], received) + base_ref[:, cols].astype(jnp.float32)
        total = total + rest_ref[:, cols].astype(jnp.float32) * (1 / REST_SCALE)
        out_ref[:, cols] = total.astype(jnp.bfloat16)
        copies.append(push(out_ref.at[:, cols], out_hbm.at[:, cols], sems.at[i]))
    for copy in copies:
        copy.wait()


def swap(x, peers, distance):
    return lax.ppermute(x, "rows", [(i, i ^ distance) for i in range(peers)])


def exchange(rows_out, peers):
    count, width = rows_out.shape
    sent = rows_out.reshape(peers, count // peers, width)
    got = lax.all_to_all(sent, "rows", split_axis=0, concat_axis=0, tiled=True)
    return got.reshape(count, width)


def across(planes, peers):
    return [planes[0]] + [swap(x, peers, GROUP * z) for z, x in enumerate(planes) if z]


def within(planes, peers, slots):
    depth, wide = planes[0].shape
    n = len(planes)
    other = call(
        gather_kernel,
        "gather",
        jax.ShapeDtypeStruct((n * depth // 2, wide), jnp.bfloat16),
        [VMEM] * n,
        VMEM,
        flops=LONG,
    )(*planes)
    other = swap(other, peers, 1)
    pairs = call(
        functools.partial(pair_kernel, slots),
        "pair",
        [jax.ShapeDtypeStruct((2 * n * slots, wide), jnp.bfloat16)] * (GROUP // 2),
        [VMEM] * (n + 1),
        [VMEM] * (GROUP // 2),
    )(*planes, other)
    return [pairs[0]] + [swap(x, peers, 2 * q) for q, x in enumerate(pairs) if q]


def on_device(seeds, neighbor_pos, edge_weight, tile_blocks, wanted):
    rows, width = seeds.shape
    peers, slots = wanted.shape[1:]
    count = peers * slots
    neighbours = neighbor_pos.shape[1]
    planes = peers // GROUP
    wide = max(3 * width // 8 // BLK, 1) * BLK
    assert peers & (peers - 1) == 0 and peers >= GROUP
    me = lax.axis_index("rows").astype(jnp.int32).reshape(1)
    sems = pltpu.SemaphoreType.DMA
    bf16 = jnp.bfloat16
    plane_shape = jax.ShapeDtypeStruct((GROUP * slots, wide), bf16)
    n_b = len(pieces_of(wide, width))
    n_all = n_b + len(pieces_of(0, wide))

    asked = lax.all_to_all(
        wanted.reshape(peers, 1, slots), "rows", split_axis=0, concat_axis=0, tiled=True
    )
    own, column, share, near_seeds = call(
        own_tiles_kernel,
        "own_tiles",
        [
            far_out((rows, rows)),
            far_out((neighbours, rows), jnp.int32),
            far_out((neighbours, rows), jnp.float32),
            near_out((rows, width)),
        ],
        [SMEM, VMEM, VMEM, HBM],
        [HBM, HBM, HBM, VMEM],
        [
            pltpu.VMEM((rows, rows), bf16),
            pltpu.VMEM((neighbours, rows), jnp.int32),
            pltpu.VMEM((neighbours, rows), jnp.float32),
            pltpu.VMEM((neighbours, rows), jnp.float32),
            sems((3 + rows // BLK,)),
        ],
        flops=neighbours * rows * rows,
    )(far_in(tile_blocks), far_in(neighbor_pos.T), far_in(edge_weight.T), far_in(seeds))
    sent_a, sent_b, *sent_planes = call(
        pick_kernel,
        "pick",
        [far_out((count, wide)), far_out((count, width - wide))] + [plane_shape] * planes,
        [SMEM, VMEM, VMEM, HBM],
        [HBM, HBM] + [VMEM] * planes,
        [
            pltpu.VMEM((count, rows), bf16),
            pltpu.VMEM((count, wide), bf16),
            pltpu.VMEM((count, width - wide), bf16),
            sems((1 + n_b,)),
        ],
        flops=2 * count * rows * width,
    )(me, asked, near_seeds, far_in(own))
    got_planes = across(sent_planes, peers)
    received_b = exchange(sent_b, peers)
    got_pairs = within(got_planes, peers, slots)
    far, picked_far, sent_base = call(
        far_kernel,
        "far",
        [far_out((rows, count)), near_out((count, count)), near_out((count, width))],
        [VMEM] * 7 + [ANY],
        [VMEM] * 3,
        [
            pltpu.VMEM((count, rows), bf16),
            pltpu.VMEM((count, rows), bf16),
            pltpu.VMEM((neighbours, rows), jnp.float32),
        ],
        flops=2 * rows * count * (count + rows + width) + neighbours * rows * count,
    )(
        asked,
        far_in(own),
        far_in(column),
        far_in(share),
        far_in(seeds),
        far_in(sent_a),
        far_in(sent_b),
        got_pairs[0],
    )
    received_a, *sent_planes = call(
        functools.partial(send_a_kernel, slots=slots),
        "send_a",
        [far_out((count, wide))] + [plane_shape] * planes,
        [SMEM] + [VMEM] * (2 + GROUP // 2),
        [HBM] + [VMEM] * planes,
        [pltpu.VMEM((count, wide), bf16), pltpu.VMEM((count, wide), bf16), sems],
        flops=2 * count * count * wide,
    )(me, picked_far, sent_base, *got_pairs)
    got_planes = across(sent_planes, peers)
    sent_b, received_b = call(
        send_b_kernel,
        "send_b",
        [far_out((count, width - wide)), far_out((count, width - wide))],
        [VMEM] * 3 + [ANY],
        [HBM, HBM],
        [pltpu.VMEM((count, width - wide), bf16), sems((1 + n_b,))],
        flops=2 * count * count * (width - wide),
        nbytes=2 * count * (3 * (width - wide) + count + width),
    )(picked_far, sent_base, received_b, sent_planes[0])
    last_b = exchange(sent_b, peers)
    got_pairs = within(got_planes, peers, slots)
    next_base, rest, near_far = call(
        labels_kernel,
        "labels",
        [
            near_out((rows, width)),
            near_out((rows, width), jnp.float8_e4m3fn),
            near_out((rows, count)),
        ],
        [VMEM] * 5 + [ANY],
        [VMEM] * 3,
        flops=2 * rows * (count + 2 * rows) * width,
    )(
        far_in(own),
        far_in(far),
        far_in(seeds),
        far_in(received_a),
        far_in(received_b),
        got_pairs[0],
    )
    return call(
        functools.partial(last_kernel, slots=slots),
        "last",
        far_out((rows, width)),
        [SMEM] + [VMEM] * (4 + GROUP // 2),
        HBM,
        [pltpu.VMEM((count, wide), bf16), pltpu.VMEM((rows, width), bf16), sems((n_all,))],
        flops=2 * rows * count * width,
        nbytes=2 * rows * count + 5 * rows * width + 2 * count * width,
    )(me, near_far, next_base, rest, last_b, *got_pairs)


def solution(mesh):
    in_specs = (
        P(("parts", "rows"), "cls"),
        P(("parts", "rows"), None),
        P(("parts", "rows"), None),
        P(("parts", "rows"), None),
        P(("parts", "rows"), None, None),
    )
    out_specs = P(("parts", "rows"), "cls")
    return jax.shard_map(
        on_device, mesh=mesh, in_specs=in_specs, out_specs=out_specs, check_vma=False
    )
```

```python
import functools
import math

import jax
import jax.numpy as jnp
from jax import lax
from jax.experimental import pallas as pl
from jax.experimental.pallas import tpu as pltpu
from jax.sharding import PartitionSpec as P

BLK = 128
COLS = 256
GROUP = 8
PACK = 16
VMEM_LIMIT = 32 * 1024 * 1024
NEAR_BYTES = 1024 * 1024
KEEP = 0.85
ANCHOR = 0.15
REST_SCALE = 4096.0
LONG = 4 * 10**10
EARLY = 2

SMEM = pl.BlockSpec(memory_space=pltpu.SMEM)
VMEM = pl.BlockSpec(memory_space=pltpu.VMEM)
HBM = pl.BlockSpec(memory_space=pltpu.HBM)
ANY = pl.BlockSpec(memory_space=pl.ANY)


def far_out(shape, dtype=jnp.bfloat16):
    return pltpu.HBM(shape, dtype)


def far_in(x):
    return pltpu.with_memory_space_constraint(x, pltpu.HBM)


def near_out(shape, dtype=jnp.bfloat16):
    small = math.prod(shape) * jnp.dtype(dtype).itemsize <= NEAR_BYTES
    return pltpu.VMEM(shape, dtype) if small else jax.ShapeDtypeStruct(shape, dtype)


def call(kernel, name, out_shape, in_specs, out_specs, scratch_shapes=(), flops=0, nbytes=0, aliases=None):
    return pl.pallas_call(
        kernel,
        out_shape=out_shape,
        in_specs=in_specs,
        out_specs=out_specs,
        scratch_shapes=scratch_shapes,
        input_output_aliases=aliases or {},
        compiler_params=pltpu.CompilerParams(vmem_limit_bytes=VMEM_LIMIT),
        cost_estimate=pl.CostEstimate(flops=flops, bytes_accessed=nbytes, transcendentals=0),
        name=name,
    )


def dot(a, b):
    return jnp.dot(a, b, preferred_element_type=jnp.float32)


def pieces_of(first, last):
    return [slice(c, min(c + COLS, last)) for c in range(first, last, COLS)]


def moved(cols, by):
    return slice(cols.start + by, cols.stop + by)


def push(source, target, sem):
    copy = pltpu.make_async_copy(source, target, sem)
    copy.start()
    return copy


def picks(asked, rows):
    peers, _, slots = asked.shape
    count = peers * slots
    spread = jnp.broadcast_to(asked.astype(jnp.float32), (peers, slots, slots))
    spread = spread.reshape(count, slots)
    slot = lax.broadcasted_iota(jnp.int32, (count, slots), 0) % slots
    lane = lax.broadcasted_iota(jnp.int32, (count, slots), 1)
    row = jnp.sum(jnp.where(slot == lane, spread, 0.0), axis=1, keepdims=True)
    hits = lax.broadcasted_iota(jnp.int32, (count, rows), 1) == row.astype(jnp.int32)
    return hits.astype(jnp.float32).astype(jnp.bfloat16)


def block(peer, slots):
    return pl.ds(pl.multiple_of(peer * slots, slots), slots)


def to_planes(me, rows_ref, plane_refs, slots):
    for z, plane_ref in enumerate(plane_refs):
        for s in range(2):
            for q in range(GROUP // 2):
                peer = me ^ (GROUP * z + 2 * q + s)
                at = (s * (GROUP // 2) + q) * slots
                plane_ref[at : at + slots, :] = rows_ref[block(peer, slots), :]


def from_pairs(me, pair_refs, rows_ref, slots):
    planes = pair_refs[0].shape[0] // (2 * slots)
    for q, pair_ref in enumerate(pair_refs):
        for s in range(2):
            for z in range(planes):
                peer = me ^ (GROUP * z + 2 * q + s)
                at = (s * planes + z) * slots
                rows_ref[block(peer, slots), :] = pair_ref[at : at + slots, :]


def fill_edges(blocks_ref, pos_ref, weight_ref, column_ref, share_ref):
    block_count, tile_count = blocks_ref.shape
    weights = weight_ref[...].astype(jnp.float32)
    share = weights / jnp.sum(weights, axis=0, keepdims=True)
    share_ref[...] = share.astype(jnp.bfloat16).astype(jnp.float32)
    for b in range(block_count):
        lanes = slice(b * BLK, (b + 1) * BLK)
        pos = pos_ref[:, lanes]
        tile = pos // BLK
        base = jnp.full(pos.shape, blocks_ref[b, 0], jnp.int32)
        for j in range(1, tile_count):
            base = jnp.where(tile == j, blocks_ref[b, j], base)
        column_ref[:, lanes] = base * BLK + pos % BLK


def fill_tiles(column_ref, share_ref, tiles_ref, spot_ref, start, chunks):
    neighbours, rows = column_ref.shape
    sub = lax.broadcasted_iota(jnp.int32, (BLK, BLK), 0).astype(jnp.float32).astype(jnp.bfloat16)
    sub = sub.reshape(BLK // PACK, PACK, BLK)

    @pl.loop(*chunks)
    def _(chunk):
        first = pl.multiple_of(chunk * BLK, BLK)
        spot = column_ref[...] - (start + first)
        spot_ref[...] = jnp.where((spot >= 0) & (spot < BLK), spot, -1).astype(jnp.float32)

        @pl.loop(0, rows // BLK)
        def _(b):
            lanes = pl.ds(pl.multiple_of(b * BLK, BLK), BLK)
            row = lambda ref, k: jnp.broadcast_to(ref[k : k + 1, lanes], (PACK, BLK))
            total = jnp.zeros(sub.shape, jnp.bfloat16)
            for k in range(neighbours):
                spot = row(spot_ref, k).astype(jnp.bfloat16)
                share = row(share_ref, k).astype(jnp.bfloat16)
                total = jnp.where(sub == spot[None], share[None], total)
            tiles_ref[lanes, pl.ds(first, BLK)] = total.reshape(BLK, BLK).T


def own_tiles_kernel(
    blocks_ref,
    pos_ref,
    weight_ref,
    seeds_hbm,
    own_hbm,
    column_ref,
    share_ref,
    near_ref,
    own_ref,
    spot_ref,
    sems,
):
    copies = [push(seeds_hbm, near_ref, sems.at[0])]
    fill_edges(blocks_ref, pos_ref, weight_ref, column_ref, share_ref)
    for i in range(own_ref.shape[1] // BLK):
        cols = slice(i * BLK, (i + 1) * BLK)
        fill_tiles(column_ref, share_ref, own_ref, spot_ref, 0, (i, i + 1))
        copies.append(push(own_ref.at[:, cols], own_hbm.at[:, cols], sems.at[1 + i]))
    for copy in copies:
        copy.wait()


def pick_a_kernel(me_ref, asked_ref, seeds_ref, after_ref, pick_ref, a_ref, *plane_refs):
    del after_ref
    pick_ref[...] = picks(asked_ref[...], seeds_ref.shape[0])
    for cols in pieces_of(0, a_ref.shape[1]):
        a_ref[:, cols] = dot(pick_ref[...], seeds_ref[:, cols]).astype(jnp.bfloat16)
    to_planes(me_ref[0], a_ref, plane_refs, asked_ref.shape[2])


def pick_b_kernel(
    pick_ref, seeds_ref, a_ref, column_ref, share_ref, out_a, out_b, early_ref, b_ref, spot_ref, sems
):
    rows, width = seeds_ref.shape
    wide = a_ref.shape[1]
    copies = [push(a_ref, out_a, sems.at[0])]
    for i, cols in enumerate(pieces_of(wide, width)):
        here = moved(cols, -wide)
        b_ref[:, here] = dot(pick_ref[...], seeds_ref[:, cols]).astype(jnp.bfloat16)
        copies.append(push(b_ref.at[:, here], out_b.at[:, here], sems.at[1 + i]))
    fill_tiles(column_ref, share_ref, early_ref, spot_ref, rows, (0, early_ref.shape[1] // BLK))
    for copy in copies:
        copy.wait()


def far_kernel(
    asked_ref,
    early_ref,
    own_ref,
    column_ref,
    share_ref,
    seeds_ref,
    sent_a_ref,
    sent_b_ref,
    after_ref,
    far_ref,
    picked_far_ref,
    sent_base_ref,
    pick_ref,
    picked_ref,
    spot_ref,
):
    del after_ref
    rows, width = seeds_ref.shape
    wide = sent_a_ref.shape[1]
    done = early_ref.shape[1]
    far_ref[:, :done] = early_ref[...]
    fill_tiles(column_ref, share_ref, far_ref, spot_ref, rows, (done // BLK, far_ref.shape[1] // BLK))
    pick_ref[...] = picks(asked_ref[...], rows)
    for cols in pieces_of(0, far_ref.shape[1]):
        picked_far_ref[:, cols] = dot(pick_ref[...], far_ref[:, cols]).astype(jnp.bfloat16)
    for cols in pieces_of(0, rows):
        picked_ref[:, cols] = dot(pick_ref[...], own_ref[:, cols]).astype(jnp.bfloat16)
    for cols in pieces_of(0, wide) + pieces_of(wide, width):
        sent = sent_a_ref[:, cols] if cols.stop <= wide else sent_b_ref[:, moved(cols, -wide)]
        sent_base = KEEP * dot(picked_ref[...], seeds_ref[:, cols])
        sent_base = sent_base + ANCHOR * sent.astype(jnp.float32)
        sent_base_ref[:, cols] = sent_base.astype(jnp.bfloat16)


def gather_kernel(*refs):
    *plane_refs, out_ref = refs
    half = plane_refs[0].shape[0] // 2
    for z, plane_ref in enumerate(plane_refs):
        out_ref[z * half : (z + 1) * half, :] = plane_ref[half:, :]


def pair_kernel(slots, *refs):
    count = GROUP // 2
    *plane_refs, other_ref = refs[:-count]
    planes = len(plane_refs)
    for q, out_ref in enumerate(refs[-count:]):
        for z, plane_ref in enumerate(plane_refs):
            here = slice(z * slots, (z + 1) * slots)
            there = slice((planes + z) * slots, (planes + z + 1) * slots)
            other = (z * count + q) * slots
            out_ref[here, :] = plane_ref[q * slots : (q + 1) * slots, :]
            out_ref[there, :] = other_ref[other : other + slots, :]


def send_a_kernel(me_ref, tiles_ref, base_ref, *refs, slots):
    pair_refs = refs[: GROUP // 2]
    out_hbm, *plane_refs, received_ref, out_ref, sem = refs[GROUP // 2 :]
    me = me_ref[0]
    from_pairs(me, pair_refs, received_ref, slots)
    copy = push(received_ref, out_hbm, sem)
    for cols in pieces_of(0, received_ref.shape[1]):
        total = KEEP * dot(tiles_ref[...], received_ref[:, cols])
        out_ref[:, cols] = (total + base_ref[:, cols].astype(jnp.float32)).astype(jnp.bfloat16)
    to_planes(me, out_ref, plane_refs, slots)
    copy.wait()


def send_b_kernel(tiles_ref, base_ref, received_ref, after_ref, out_hbm, kept_hbm, out_ref, sems):
    del after_ref
    wide = base_ref.shape[1] - received_ref.shape[1]
    copies = [push(received_ref, kept_hbm, sems.at[0])]
    for i, cols in enumerate(pieces_of(0, received_ref.shape[1])):
        total = KEEP * dot(tiles_ref[...], received_ref[:, cols])
        total = total + base_ref[:, moved(cols, wide)].astype(jnp.float32)
        out_ref[:, cols] = total.astype(jnp.bfloat16)
        copies.append(push(out_ref.at[:, cols], out_hbm.at[:, cols], sems.at[1 + i]))
    for copy in copies:
        copy.wait()


def labels_kernel(
    own_ref,
    far_ref,
    seeds_ref,
    received_a_ref,
    received_b_ref,
    after_ref,
    next_ref,
    rest_ref,
    near_ref,
):
    del after_ref
    near_ref[...] = far_ref[...]
    wide = received_a_ref.shape[1]
    width = seeds_ref.shape[1]
    for cols in pieces_of(0, wide) + pieces_of(wide, width):
        first = cols.stop <= wide
        received = received_a_ref[:, cols] if first else received_b_ref[:, moved(cols, -wide)]
        seeds = ANCHOR * seeds_ref[:, cols].astype(jnp.float32)
        total = dot(own_ref[...], seeds_ref[:, cols]) + dot(far_ref[...], received)
        labels = (KEEP * total + seeds).astype(jnp.bfloat16)
        base = KEEP * dot(own_ref[...], labels) + seeds
        kept = base.astype(jnp.bfloat16)
        next_ref[:, cols] = kept
        rest = (base - kept.astype(jnp.float32)) * REST_SCALE
        rest_ref[:, cols] = rest.astype(jnp.float8_e4m3fn)


def result(tiles_ref, received, base_ref, rest_ref, cols):
    total = KEEP * dot(tiles_ref[...], received) + base_ref[:, cols].astype(jnp.float32)
    total = total + rest_ref[:, cols].astype(jnp.float32) * (1 / REST_SCALE)
    return total.astype(jnp.bfloat16)


def last_a_kernel(me_ref, tiles_ref, base_ref, rest_ref, *refs, slots):
    pair_refs = refs[: GROUP // 2]
    out_hbm, received_ref, out_ref, sems = refs[GROUP // 2 :]
    from_pairs(me_ref[0], pair_refs, received_ref, slots)
    copies = []
    for i, cols in enumerate(pieces_of(0, received_ref.shape[1])):
        out_ref[:, cols] = result(tiles_ref, received_ref[:, cols], base_ref, rest_ref, cols)
        copies.append(push(out_ref.at[:, cols], out_hbm.at[:, cols], sems.at[i]))
    for copy in copies:
        copy.wait()


def last_b_kernel(tiles_ref, base_ref, rest_ref, received_ref, same_ref, out_hbm, out_ref, sems):
    del same_ref
    width = base_ref.shape[1]
    wide = width - received_ref.shape[1]
    copies = []
    for i, cols in enumerate(pieces_of(wide, width)):
        here = moved(cols, -wide)
        out_ref[:, here] = result(tiles_ref, received_ref[:, here], base_ref, rest_ref, cols)
        copies.append(push(out_ref.at[:, here], out_hbm.at[:, cols], sems.at[i]))
    for copy in copies:
        copy.wait()


def swap(x, peers, distance):
    return lax.ppermute(x, "rows", [(i, i ^ distance) for i in range(peers)])


def exchange(rows_out, peers):
    count, width = rows_out.shape
    sent = rows_out.reshape(peers, count // peers, width)
    got = lax.all_to_all(sent, "rows", split_axis=0, concat_axis=0, tiled=True)
    return got.reshape(count, width)


def across(planes, peers):
    return [planes[0]] + [swap(x, peers, GROUP * z) for z, x in enumerate(planes) if z]


def within(planes, peers, slots):
    depth, wide = planes[0].shape
    n = len(planes)
    other = call(
        gather_kernel,
        "gather",
        jax.ShapeDtypeStruct((n * depth // 2, wide), jnp.bfloat16),
        [VMEM] * n,
        VMEM,
        flops=LONG,
    )(*planes)
    other = swap(other, peers, 1)
    pairs = call(
        functools.partial(pair_kernel, slots),
        "pair",
        [jax.ShapeDtypeStruct((2 * n * slots, wide), jnp.bfloat16)] * (GROUP // 2),
        [VMEM] * (n + 1),
        [VMEM] * (GROUP // 2),
    )(*planes, other)
    return [pairs[0]] + [swap(x, peers, 2 * q) for q, x in enumerate(pairs) if q]


def on_device(seeds, neighbor_pos, edge_weight, tile_blocks, wanted):
    rows, width = seeds.shape
    peers, slots = wanted.shape[1:]
    count = peers * slots
    neighbours = neighbor_pos.shape[1]
    planes = peers // GROUP
    wide = max(3 * width // 8 // BLK, 1) * BLK
    assert peers & (peers - 1) == 0 and peers >= GROUP
    me = lax.axis_index("rows").astype(jnp.int32).reshape(1)
    sems = pltpu.SemaphoreType.DMA
    bf16 = jnp.bfloat16
    plane_shape = jax.ShapeDtypeStruct((GROUP * slots, wide), bf16)
    n_b = len(pieces_of(wide, width))
    n_all = n_b + len(pieces_of(0, wide))

    asked = lax.all_to_all(
        wanted.reshape(peers, 1, slots), "rows", split_axis=0, concat_axis=0, tiled=True
    )
    own, column, share, near_seeds = call(
        own_tiles_kernel,
        "own_tiles",
        [
            far_out((rows, rows)),
            near_out((neighbours, rows), jnp.int32),
            near_out((neighbours, rows), jnp.float32),
            near_out((rows, width)),
        ],
        [SMEM, VMEM, VMEM, HBM],
        [HBM, VMEM, VMEM, VMEM],
        [
            pltpu.VMEM((rows, rows), bf16),
            pltpu.VMEM((neighbours, rows), jnp.float32),
            sems((1 + rows // BLK,)),
        ],
        flops=neighbours * rows * rows,
    )(far_in(tile_blocks), far_in(neighbor_pos.T), far_in(edge_weight.T), far_in(seeds))
    pick, near_a, *sent_planes = call(
        pick_a_kernel,
        "pick_a",
        [near_out((count, rows)), near_out((count, wide))] + [plane_shape] * planes,
        [SMEM, VMEM, VMEM, HBM],
        [VMEM] * (2 + planes),
        flops=2 * count * rows * wide,
    )(me, asked, near_seeds, far_in(own))
    got_planes = across(sent_planes, peers)
    sent_a, sent_b, early = call(
        pick_b_kernel,
        "pick_b",
        [
            far_out((count, wide)),
            far_out((count, width - wide)),
            near_out((rows, count // BLK * EARLY // 8 * BLK)),
        ],
        [VMEM] * 5,
        [HBM, HBM, VMEM],
        [
            pltpu.VMEM((count, width - wide), bf16),
            pltpu.VMEM((neighbours, rows), jnp.float32),
            sems((1 + n_b,)),
        ],
        flops=2 * count * rows * (width - wide),
    )(pick, near_seeds, near_a, column, share)
    received_b = exchange(sent_b, peers)
    got_pairs = within(got_planes, peers, slots)
    far, picked_far, sent_base = call(
        far_kernel,
        "far",
        [far_out((rows, count)), near_out((count, count)), near_out((count, width))],
        [VMEM] * 8 + [ANY],
        [VMEM] * 3,
        [
            pltpu.VMEM((count, rows), bf16),
            pltpu.VMEM((count, rows), bf16),
            pltpu.VMEM((neighbours, rows), jnp.float32),
        ],
        flops=2 * rows * count * (count + rows + width) + neighbours * rows * count,
    )(
        asked,
        early,
        far_in(own),
        column,
        share,
        far_in(seeds),
        far_in(sent_a),
        far_in(sent_b),
        got_pairs[0],
    )
    received_a, *sent_planes = call(
        functools.partial(send_a_kernel, slots=slots),
        "send_a",
        [far_out((count, wide))] + [plane_shape] * planes,
        [SMEM] + [VMEM] * (2 + GROUP // 2),
        [HBM] + [VMEM] * planes,
        [pltpu.VMEM((count, wide), bf16), pltpu.VMEM((count, wide), bf16), sems],
        flops=2 * count * count * wide,
    )(me, picked_far, sent_base, *got_pairs)
    got_planes = across(sent_planes, peers)
    sent_b, received_b = call(
        send_b_kernel,
        "send_b",
        [far_out((count, width - wide)), far_out((count, width - wide))],
        [VMEM] * 3 + [ANY],
        [HBM, HBM],
        [pltpu.VMEM((count, width - wide), bf16), sems((1 + n_b,))],
        flops=2 * count * count * (width - wide),
        nbytes=2 * count * (3 * (width - wide) + count + width),
    )(picked_far, sent_base, received_b, sent_planes[0])
    last_b = exchange(sent_b, peers)
    got_pairs = within(got_planes, peers, slots)
    next_base, rest, near_far = call(
        labels_kernel,
        "labels",
        [
            near_out((rows, width)),
            near_out((rows, width), jnp.float8_e4m3fn),
            near_out((rows, count)),
        ],
        [VMEM] * 5 + [ANY],
        [VMEM] * 3,
        flops=2 * rows * (count + 2 * rows) * width,
    )(
        far_in(own),
        far_in(far),
        far_in(seeds),
        far_in(received_a),
        far_in(received_b),
        got_pairs[0],
    )
    first = call(
        functools.partial(last_a_kernel, slots=slots),
        "last_a",
        far_out((rows, width)),
        [SMEM] + [VMEM] * (3 + GROUP // 2),
        HBM,
        [pltpu.VMEM((count, wide), bf16), pltpu.VMEM((rows, wide), bf16), sems((n_all - n_b,))],
        flops=2 * rows * count * wide,
    )(me, near_far, next_base, rest, *got_pairs)
    return call(
        last_b_kernel,
        "last_b",
        far_out((rows, width)),
        [VMEM] * 4 + [HBM],
        HBM,
        [pltpu.VMEM((rows, width - wide), bf16), sems((n_b,))],
        flops=2 * rows * count * (width - wide),
        nbytes=2 * rows * count + 5 * rows * width + 2 * count * width,
        aliases={4: 0},
    )(near_far, next_base, rest, last_b, far_in(first))


def solution(mesh):
    in_specs = (
        P(("parts", "rows"), "cls"),
        P(("parts", "rows"), None),
        P(("parts", "rows"), None),
        P(("parts", "rows"), None),
        P(("parts", "rows"), None, None),
    )
    out_specs = P(("parts", "rows"), "cls")
    return jax.shard_map(
        on_device, mesh=mesh, in_specs=in_specs, out_specs=out_specs, check_vma=False
    )
```

```python
import functools
import math

import jax
import jax.numpy as jnp
from jax import lax
from jax.experimental import pallas as pl
from jax.experimental.pallas import tpu as pltpu
from jax.sharding import PartitionSpec as P

BLK = 128
COLS = 256
GROUP = 8
PACK = 16
VMEM_LIMIT = 32 * 1024 * 1024
NEAR_BYTES = 1024 * 1024
KEEP = 0.85
ANCHOR = 0.15
REST_SCALE = 4096.0
LONG = 4 * 10**10
EARLY = 2

SMEM = pl.BlockSpec(memory_space=pltpu.SMEM)
VMEM = pl.BlockSpec(memory_space=pltpu.VMEM)
HBM = pl.BlockSpec(memory_space=pltpu.HBM)
ANY = pl.BlockSpec(memory_space=pl.ANY)


def far_out(shape, dtype=jnp.bfloat16):
    return pltpu.HBM(shape, dtype)


def far_in(x):
    return pltpu.with_memory_space_constraint(x, pltpu.HBM)


def near_out(shape, dtype=jnp.bfloat16):
    small = math.prod(shape) * jnp.dtype(dtype).itemsize <= NEAR_BYTES
    return pltpu.VMEM(shape, dtype) if small else jax.ShapeDtypeStruct(shape, dtype)


def call(kernel, name, out_shape, in_specs, out_specs, scratch_shapes=(), flops=0, nbytes=0, aliases=None):
    return pl.pallas_call(
        kernel,
        out_shape=out_shape,
        in_specs=in_specs,
        out_specs=out_specs,
        scratch_shapes=scratch_shapes,
        input_output_aliases=aliases or {},
        compiler_params=pltpu.CompilerParams(vmem_limit_bytes=VMEM_LIMIT),
        cost_estimate=pl.CostEstimate(flops=flops, bytes_accessed=nbytes, transcendentals=0),
        name=name,
    )


def dot(a, b):
    return jnp.dot(a, b, preferred_element_type=jnp.float32)


def pieces_of(first, last):
    return [slice(c, min(c + COLS, last)) for c in range(first, last, COLS)]


def strips_of(count):
    return [slice(r, r + BLK) for r in range(0, count, BLK)]


def moved(cols, by):
    return slice(cols.start + by, cols.stop + by)


def push(source, target, sem):
    copy = pltpu.make_async_copy(source, target, sem)
    copy.start()
    return copy


def picks(asked, rows):
    peers, _, slots = asked.shape
    count = peers * slots
    spread = jnp.broadcast_to(asked.astype(jnp.float32), (peers, slots, slots))
    spread = spread.reshape(count, slots)
    slot = lax.broadcasted_iota(jnp.int32, (count, slots), 0) % slots
    lane = lax.broadcasted_iota(jnp.int32, (count, slots), 1)
    row = jnp.sum(jnp.where(slot == lane, spread, 0.0), axis=1, keepdims=True)
    hits = lax.broadcasted_iota(jnp.int32, (count, rows), 1) == row.astype(jnp.int32)
    return hits.astype(jnp.float32).astype(jnp.bfloat16)


def block(peer, slots):
    return pl.ds(pl.multiple_of(peer * slots, slots), slots)


def pair_order(pairs):
    return [0] + list(range(pairs - 1, 0, -1))


def plane_order(planes):
    return [0] + list(range(2, planes)) + [1]


def to_planes(me, rows_ref, plane_refs, slots):
    for z, plane_ref in zip(plane_order(len(plane_refs)), plane_refs):
        for s in range(2):
            for q in range(GROUP // 2):
                peer = me ^ (GROUP * z + 2 * q + s)
                at = (s * (GROUP // 2) + q) * slots
                plane_ref[at : at + slots, :] = rows_ref[block(peer, slots), :]


def from_pairs(me, pair_refs, rows_ref, slots):
    planes = pair_refs[0].shape[0] // (2 * slots)
    for q, pair_ref in zip(pair_order(len(pair_refs)), pair_refs):
        for s in range(2):
            for i, z in enumerate(plane_order(planes)):
                peer = me ^ (GROUP * z + 2 * q + s)
                at = (s * planes + i) * slots
                rows_ref[block(peer, slots), :] = pair_ref[at : at + slots, :]


def fill_edges(blocks_ref, pos_ref, weight_ref, column_ref, share_ref):
    block_count, tile_count = blocks_ref.shape
    weights = weight_ref[...].astype(jnp.float32)
    share = weights / jnp.sum(weights, axis=0, keepdims=True)
    share_ref[...] = share.astype(jnp.bfloat16).astype(jnp.float32)
    for b in range(block_count):
        lanes = slice(b * BLK, (b + 1) * BLK)
        pos = pos_ref[:, lanes]
        tile = pos // BLK
        base = jnp.full(pos.shape, blocks_ref[b, 0], jnp.int32)
        for j in range(1, tile_count):
            base = jnp.where(tile == j, blocks_ref[b, j], base)
        column_ref[:, lanes] = base * BLK + pos % BLK


def fill_tiles(column_ref, share_ref, tiles_ref, spot_ref, start, chunks):
    neighbours, rows = column_ref.shape
    sub = lax.broadcasted_iota(jnp.int32, (BLK, BLK), 0).astype(jnp.float32).astype(jnp.bfloat16)
    sub = sub.reshape(BLK // PACK, PACK, BLK)

    @pl.loop(*chunks)
    def _(chunk):
        first = pl.multiple_of(chunk * BLK, BLK)
        spot = column_ref[...] - (start + first)
        spot_ref[...] = jnp.where((spot >= 0) & (spot < BLK), spot, -1).astype(jnp.float32)

        @pl.loop(0, rows // BLK)
        def _(b):
            lanes = pl.ds(pl.multiple_of(b * BLK, BLK), BLK)
            row = lambda ref, k: jnp.broadcast_to(ref[k : k + 1, lanes], (PACK, BLK))
            total = jnp.zeros(sub.shape, jnp.bfloat16)
            for k in range(neighbours):
                spot = row(spot_ref, k).astype(jnp.bfloat16)
                share = row(share_ref, k).astype(jnp.bfloat16)
                total = jnp.where(sub == spot[None], share[None], total)
            tiles_ref[lanes, pl.ds(first, BLK)] = total.reshape(BLK, BLK).T


def own_tiles_kernel(
    blocks_ref,
    pos_ref,
    weight_ref,
    seeds_hbm,
    own_hbm,
    column_ref,
    share_ref,
    near_ref,
    own_ref,
    spot_ref,
    sems,
):
    copies = [push(seeds_hbm, near_ref, sems.at[0])]
    fill_edges(blocks_ref, pos_ref, weight_ref, column_ref, share_ref)
    for i in range(own_ref.shape[1] // BLK):
        cols = slice(i * BLK, (i + 1) * BLK)
        fill_tiles(column_ref, share_ref, own_ref, spot_ref, 0, (i, i + 1))
        copies.append(push(own_ref.at[:, cols], own_hbm.at[:, cols], sems.at[1 + i]))
    for copy in copies:
        copy.wait()


def pick_a_kernel(me_ref, asked_ref, seeds_ref, after_ref, pick_ref, a_ref, *plane_refs):
    del after_ref
    pick_ref[...] = picks(asked_ref[...], seeds_ref.shape[0])
    for cols in pieces_of(0, a_ref.shape[1]):
        a_ref[:, cols] = dot(pick_ref[...], seeds_ref[:, cols]).astype(jnp.bfloat16)
    to_planes(me_ref[0], a_ref, plane_refs, asked_ref.shape[2])


def pick_b_kernel(
    pick_ref, seeds_ref, a_ref, column_ref, share_ref, out_a, out_b, early_ref, b_ref, spot_ref, sems
):
    rows = seeds_ref.shape[0]
    wide = a_ref.shape[1]
    copies = [push(a_ref, out_a, sems.at[0])]
    for i, rows_here in enumerate(strips_of(pick_ref.shape[0])):
        b_ref[rows_here, :] = dot(pick_ref[rows_here, :], seeds_ref[:, wide:]).astype(jnp.bfloat16)
        copies.append(push(b_ref.at[rows_here], out_b.at[rows_here], sems.at[1 + i]))
    fill_tiles(column_ref, share_ref, early_ref, spot_ref, rows, (0, early_ref.shape[1] // BLK))
    for copy in copies:
        copy.wait()


def far_kernel(
    asked_ref,
    early_ref,
    own_ref,
    column_ref,
    share_ref,
    seeds_ref,
    sent_a_ref,
    sent_b_ref,
    after_ref,
    far_ref,
    picked_far_ref,
    sent_base_ref,
    pick_ref,
    picked_ref,
    spot_ref,
):
    del after_ref
    rows, width = seeds_ref.shape
    wide = sent_a_ref.shape[1]
    done = early_ref.shape[1]
    far_ref[:, :done] = early_ref[...]
    fill_tiles(column_ref, share_ref, far_ref, spot_ref, rows, (done // BLK, far_ref.shape[1] // BLK))
    pick_ref[...] = picks(asked_ref[...], rows)
    for cols in pieces_of(0, far_ref.shape[1]):
        picked_far_ref[:, cols] = dot(pick_ref[...], far_ref[:, cols]).astype(jnp.bfloat16)
    for cols in pieces_of(0, rows):
        picked_ref[:, cols] = dot(pick_ref[...], own_ref[:, cols]).astype(jnp.bfloat16)
    for cols in pieces_of(0, wide) + pieces_of(wide, width):
        sent = sent_a_ref[:, cols] if cols.stop <= wide else sent_b_ref[:, moved(cols, -wide)]
        sent_base = KEEP * dot(picked_ref[...], seeds_ref[:, cols])
        sent_base = sent_base + ANCHOR * sent.astype(jnp.float32)
        sent_base_ref[:, cols] = sent_base.astype(jnp.bfloat16)


def gather_kernel(*refs):
    *plane_refs, out_ref = refs
    half = plane_refs[0].shape[0] // 2
    for z, plane_ref in enumerate(plane_refs):
        out_ref[z * half : (z + 1) * half, :] = plane_ref[half:, :]


def pair_kernel(slots, *refs):
    count = GROUP // 2
    *plane_refs, other_ref = refs[:-count]
    planes = len(plane_refs)
    for q, out_ref in zip(pair_order(count), refs[-count:]):
        for z, plane_ref in enumerate(plane_refs):
            here = slice(z * slots, (z + 1) * slots)
            there = slice((planes + z) * slots, (planes + z + 1) * slots)
            other = (z * count + q) * slots
            out_ref[here, :] = plane_ref[q * slots : (q + 1) * slots, :]
            out_ref[there, :] = other_ref[other : other + slots, :]


def send_a_kernel(me_ref, tiles_ref, base_ref, *refs, slots):
    pair_refs = refs[: GROUP // 2]
    out_hbm, *plane_refs, received_ref, out_ref, sem = refs[GROUP // 2 :]
    me = me_ref[0]
    from_pairs(me, pair_refs, received_ref, slots)
    copy = push(received_ref, out_hbm, sem)
    for cols in pieces_of(0, received_ref.shape[1]):
        total = KEEP * dot(tiles_ref[...], received_ref[:, cols])
        out_ref[:, cols] = (total + base_ref[:, cols].astype(jnp.float32)).astype(jnp.bfloat16)
    to_planes(me, out_ref, plane_refs, slots)
    copy.wait()


def send_b_kernel(tiles_ref, base_ref, received_ref, after_ref, out_hbm, kept_hbm, out_ref, sems):
    del after_ref
    wide = base_ref.shape[1] - received_ref.shape[1]
    copies = [push(received_ref, kept_hbm, sems.at[0])]
    for i, rows in enumerate(strips_of(out_ref.shape[0])):
        total = KEEP * dot(tiles_ref[rows, :], received_ref[...])
        total = total + base_ref[rows, wide:].astype(jnp.float32)
        out_ref[rows, :] = total.astype(jnp.bfloat16)
        copies.append(push(out_ref.at[rows], out_hbm.at[rows], sems.at[1 + i]))
    for copy in copies:
        copy.wait()


def labels_kernel(
    own_ref,
    far_ref,
    seeds_ref,
    received_a_ref,
    received_b_ref,
    after_ref,
    next_ref,
    rest_ref,
    near_ref,
):
    del after_ref
    near_ref[...] = far_ref[...]
    wide = received_a_ref.shape[1]
    width = seeds_ref.shape[1]
    for cols in pieces_of(0, wide) + pieces_of(wide, width):
        first = cols.stop <= wide
        received = received_a_ref[:, cols] if first else received_b_ref[:, moved(cols, -wide)]
        seeds = ANCHOR * seeds_ref[:, cols].astype(jnp.float32)
        total = dot(own_ref[...], seeds_ref[:, cols]) + dot(far_ref[...], received)
        labels = (KEEP * total + seeds).astype(jnp.bfloat16)
        base = KEEP * dot(own_ref[...], labels) + seeds
        kept = base.astype(jnp.bfloat16)
        next_ref[:, cols] = kept
        rest = (base - kept.astype(jnp.float32)) * REST_SCALE
        rest_ref[:, cols] = rest.astype(jnp.float8_e4m3fn)


def result(tiles_ref, received, base_ref, rest_ref, rows, cols):
    total = KEEP * dot(tiles_ref[rows, :], received) + base_ref[rows, cols].astype(jnp.float32)
    total = total + rest_ref[rows, cols].astype(jnp.float32) * (1 / REST_SCALE)
    return total.astype(jnp.bfloat16)


def last_a_kernel(me_ref, tiles_ref, base_ref, rest_ref, *refs, slots):
    pair_refs = refs[: GROUP // 2]
    out_hbm, received_ref, out_ref, sems = refs[GROUP // 2 :]
    from_pairs(me_ref[0], pair_refs, received_ref, slots)
    copies = []
    for i, cols in enumerate(pieces_of(0, received_ref.shape[1])):
        received = received_ref[:, cols]
        out_ref[:, cols] = result(tiles_ref, received, base_ref, rest_ref, slice(None), cols)
        copies.append(push(out_ref.at[:, cols], out_hbm.at[:, cols], sems.at[i]))
    for copy in copies:
        copy.wait()


def last_b_kernel(tiles_ref, base_ref, rest_ref, received_ref, same_ref, out_hbm, out_ref, sems):
    del same_ref
    width = base_ref.shape[1]
    wide = width - received_ref.shape[1]
    copies = []
    cols = slice(wide, width)
    for i, rows in enumerate(strips_of(out_ref.shape[0])):
        out_ref[rows, :] = result(tiles_ref, received_ref[...], base_ref, rest_ref, rows, cols)
        copies.append(push(out_ref.at[rows], out_hbm.at[rows, cols], sems.at[i]))
    for copy in copies:
        copy.wait()


def swap(x, peers, distance):
    return lax.ppermute(x, "rows", [(i, i ^ distance) for i in range(peers)])


def exchange(rows_out, peers):
    count, width = rows_out.shape
    sent = rows_out.reshape(peers, count // peers, width)
    got = lax.all_to_all(sent, "rows", split_axis=0, concat_axis=0, tiled=True)
    return got.reshape(count, width)


def across(planes, peers):
    order = plane_order(len(planes))
    return [swap(x, peers, GROUP * z) if z else x for z, x in zip(order, planes)]


def within(planes, peers, slots):
    depth, wide = planes[0].shape
    n = len(planes)
    other = call(
        gather_kernel,
        "gather",
        jax.ShapeDtypeStruct((n * depth // 2, wide), jnp.bfloat16),
        [VMEM] * n,
        VMEM,
        flops=LONG,
    )(*planes)
    other = swap(other, peers, 1)
    pairs = call(
        functools.partial(pair_kernel, slots),
        "pair",
        [jax.ShapeDtypeStruct((2 * n * slots, wide), jnp.bfloat16)] * (GROUP // 2),
        [VMEM] * (n + 1),
        [VMEM] * (GROUP // 2),
    )(*planes, other)
    return [swap(x, peers, 2 * q) if q else x for q, x in zip(pair_order(len(pairs)), pairs)]


def on_device(seeds, neighbor_pos, edge_weight, tile_blocks, wanted):
    rows, width = seeds.shape
    peers, slots = wanted.shape[1:]
    count = peers * slots
    neighbours = neighbor_pos.shape[1]
    planes = peers // GROUP
    wide = max(3 * width // 8 // BLK, 1) * BLK
    assert peers & (peers - 1) == 0 and peers >= GROUP
    me = lax.axis_index("rows").astype(jnp.int32).reshape(1)
    sems = pltpu.SemaphoreType.DMA
    bf16 = jnp.bfloat16
    plane_shape = jax.ShapeDtypeStruct((GROUP * slots, wide), bf16)
    n_a, n_out, n_sent = len(pieces_of(0, wide)), len(strips_of(rows)), len(strips_of(count))

    asked = lax.all_to_all(
        wanted.reshape(peers, 1, slots), "rows", split_axis=0, concat_axis=0, tiled=True
    )
    own, column, share, near_seeds = call(
        own_tiles_kernel,
        "own_tiles",
        [
            far_out((rows, rows)),
            near_out((neighbours, rows), jnp.int32),
            near_out((neighbours, rows), jnp.float32),
            near_out((rows, width)),
        ],
        [SMEM, VMEM, VMEM, HBM],
        [HBM, VMEM, VMEM, VMEM],
        [
            pltpu.VMEM((rows, rows), bf16),
            pltpu.VMEM((neighbours, rows), jnp.float32),
            sems((1 + rows // BLK,)),
        ],
        flops=neighbours * rows * rows,
    )(far_in(tile_blocks), far_in(neighbor_pos.T), far_in(edge_weight.T), far_in(seeds))
    pick, near_a, *sent_planes = call(
        pick_a_kernel,
        "pick_a",
        [near_out((count, rows)), near_out((count, wide))] + [plane_shape] * planes,
        [SMEM, VMEM, VMEM, HBM],
        [VMEM] * (2 + planes),
        flops=2 * count * rows * wide,
    )(me, asked, near_seeds, far_in(own))
    got_planes = across(sent_planes, peers)
    sent_a, sent_b, early = call(
        pick_b_kernel,
        "pick_b",
        [
            far_out((count, wide)),
            far_out((count, width - wide)),
            near_out((rows, count // BLK * EARLY // 8 * BLK)),
        ],
        [VMEM] * 5,
        [HBM, HBM, VMEM],
        [
            pltpu.VMEM((count, width - wide), bf16),
            pltpu.VMEM((neighbours, rows), jnp.float32),
            sems((1 + n_sent,)),
        ],
        flops=2 * count * rows * (width - wide),
    )(pick, near_seeds, near_a, column, share)
    received_b = exchange(sent_b, peers)
    got_pairs = within(got_planes, peers, slots)
    far, picked_far, sent_base = call(
        far_kernel,
        "far",
        [far_out((rows, count)), near_out((count, count)), near_out((count, width))],
        [VMEM] * 8 + [ANY],
        [VMEM] * 3,
        [
            pltpu.VMEM((count, rows), bf16),
            pltpu.VMEM((count, rows), bf16),
            pltpu.VMEM((neighbours, rows), jnp.float32),
        ],
        flops=2 * rows * count * (count + rows + width) + neighbours * rows * count,
    )(
        asked,
        early,
        far_in(own),
        column,
        share,
        far_in(seeds),
        far_in(sent_a),
        far_in(sent_b),
        got_pairs[0],
    )
    received_a, *sent_planes = call(
        functools.partial(send_a_kernel, slots=slots),
        "send_a",
        [far_out((count, wide))] + [plane_shape] * planes,
        [SMEM] + [VMEM] * (2 + GROUP // 2),
        [HBM] + [VMEM] * planes,
        [pltpu.VMEM((count, wide), bf16), pltpu.VMEM((count, wide), bf16), sems],
        flops=2 * count * count * wide,
    )(me, picked_far, sent_base, *got_pairs)
    got_planes = across(sent_planes, peers)
    sent_b, received_b = call(
        send_b_kernel,
        "send_b",
        [far_out((count, width - wide)), far_out((count, width - wide))],
        [VMEM] * 3 + [ANY],
        [HBM, HBM],
        [pltpu.VMEM((count, width - wide), bf16), sems((1 + n_sent,))],
        flops=2 * count * count * (width - wide),
        nbytes=2 * count * (3 * (width - wide) + count + width),
    )(picked_far, sent_base, received_b, sent_planes[0])
    last_b = exchange(sent_b, peers)
    got_pairs = within(got_planes, peers, slots)
    next_base, rest, near_far = call(
        labels_kernel,
        "labels",
        [
            near_out((rows, width)),
            near_out((rows, width), jnp.float8_e4m3fn),
            near_out((rows, count)),
        ],
        [VMEM] * 5 + [ANY],
        [VMEM] * 3,
        flops=2 * rows * (count + 2 * rows) * width,
    )(
        far_in(own),
        far_in(far),
        far_in(seeds),
        far_in(received_a),
        far_in(received_b),
        got_pairs[0],
    )
    first = call(
        functools.partial(last_a_kernel, slots=slots),
        "last_a",
        far_out((rows, width)),
        [SMEM] + [VMEM] * (3 + GROUP // 2),
        HBM,
        [pltpu.VMEM((count, wide), bf16), pltpu.VMEM((rows, wide), bf16), sems((n_a,))],
        flops=2 * rows * count * wide,
    )(me, near_far, next_base, rest, *got_pairs)
    return call(
        last_b_kernel,
        "last_b",
        far_out((rows, width)),
        [VMEM] * 4 + [HBM],
        HBM,
        [pltpu.VMEM((rows, width - wide), bf16), sems((n_out,))],
        flops=2 * rows * count * (width - wide),
        nbytes=2 * rows * count + 5 * rows * width + 2 * count * width,
        aliases={4: 0},
    )(near_far, next_base, rest, last_b, far_in(first))


def solution(mesh):
    in_specs = (
        P(("parts", "rows"), "cls"),
        P(("parts", "rows"), None),
        P(("parts", "rows"), None),
        P(("parts", "rows"), None),
        P(("parts", "rows"), None, None),
    )
    out_specs = P(("parts", "rows"), "cls")
    return jax.shard_map(
        on_device, mesh=mesh, in_specs=in_specs, out_specs=out_specs, check_vma=False
    )
```

```python
import functools
import math

import jax
import jax.numpy as jnp
from jax import lax
from jax.experimental import pallas as pl
from jax.experimental.pallas import tpu as pltpu
from jax.sharding import PartitionSpec as P

BLK = 128
COLS = 256
GROUP = 8
PACK = 16
VMEM_LIMIT = 32 * 1024 * 1024
NEAR_BYTES = 1024 * 1024
KEEP = 0.85
ANCHOR = 0.15
REST_SCALE = 4096.0
LONG = 4 * 10**10
EARLY = 2

SMEM = pl.BlockSpec(memory_space=pltpu.SMEM)
VMEM = pl.BlockSpec(memory_space=pltpu.VMEM)
HBM = pl.BlockSpec(memory_space=pltpu.HBM)
ANY = pl.BlockSpec(memory_space=pl.ANY)


def far_out(shape, dtype=jnp.bfloat16):
    return pltpu.HBM(shape, dtype)


def far_in(x):
    return pltpu.with_memory_space_constraint(x, pltpu.HBM)


def near_out(shape, dtype=jnp.bfloat16):
    small = math.prod(shape) * jnp.dtype(dtype).itemsize <= NEAR_BYTES
    return pltpu.VMEM(shape, dtype) if small else jax.ShapeDtypeStruct(shape, dtype)


def call(kernel, name, out_shape, in_specs, out_specs, scratch_shapes=(), flops=0, nbytes=0, aliases=None):
    return pl.pallas_call(
        kernel,
        out_shape=out_shape,
        in_specs=in_specs,
        out_specs=out_specs,
        scratch_shapes=scratch_shapes,
        input_output_aliases=aliases or {},
        compiler_params=pltpu.CompilerParams(vmem_limit_bytes=VMEM_LIMIT),
        cost_estimate=pl.CostEstimate(flops=flops, bytes_accessed=nbytes, transcendentals=0),
        name=name,
    )


def dot(a, b):
    return jnp.dot(a, b, preferred_element_type=jnp.float32)


def pieces_of(first, last):
    return [slice(c, min(c + COLS, last)) for c in range(first, last, COLS)]


def strips_of(count):
    return [slice(r, r + BLK) for r in range(0, count, BLK)]


def moved(cols, by):
    return slice(cols.start + by, cols.stop + by)


def push(source, target, sem):
    copy = pltpu.make_async_copy(source, target, sem)
    copy.start()
    return copy


def picks(asked, rows):
    peers, _, slots = asked.shape
    count = peers * slots
    spread = jnp.broadcast_to(asked.astype(jnp.float32), (peers, slots, slots))
    spread = spread.reshape(count, slots)
    slot = lax.broadcasted_iota(jnp.int32, (count, slots), 0) % slots
    lane = lax.broadcasted_iota(jnp.int32, (count, slots), 1)
    row = jnp.sum(jnp.where(slot == lane, spread, 0.0), axis=1, keepdims=True)
    hits = lax.broadcasted_iota(jnp.int32, (count, rows), 1) == row.astype(jnp.int32)
    return hits.astype(jnp.float32).astype(jnp.bfloat16)


def block(peer, slots):
    return pl.ds(pl.multiple_of(peer * slots, slots), slots)


def pair_order(pairs):
    return [0] + list(range(pairs - 1, 0, -1))


def plane_order(planes):
    return [0] + list(range(2, planes)) + [1]


def to_planes(me, rows_ref, plane_refs, slots):
    for z, plane_ref in zip(plane_order(len(plane_refs)), plane_refs):
        for s in range(2):
            for q in range(GROUP // 2):
                peer = me ^ (GROUP * z + 2 * q + s)
                at = (s * (GROUP // 2) + q) * slots
                plane_ref[at : at + slots, :] = rows_ref[block(peer, slots), :]


def from_pairs(me, pair_refs, rows_ref, slots):
    planes = pair_refs[0].shape[0] // (2 * slots)
    for q, pair_ref in zip(pair_order(len(pair_refs)), pair_refs):
        for s in range(2):
            for i, z in enumerate(plane_order(planes)):
                peer = me ^ (GROUP * z + 2 * q + s)
                at = (s * planes + i) * slots
                rows_ref[block(peer, slots), :] = pair_ref[at : at + slots, :]


def fill_edges(blocks_ref, pos_ref, weight_ref, column_ref, share_ref):
    block_count, tile_count = blocks_ref.shape
    neighbours = pos_ref.shape[0]
    column_ref[...] = jnp.full(column_ref.shape, -1, jnp.int32)
    share_ref[...] = jnp.zeros(share_ref.shape, jnp.float32)
    weights = weight_ref[...].astype(jnp.float32)
    share = weights / jnp.sum(weights, axis=0, keepdims=True)
    share_ref[:neighbours, :] = share.astype(jnp.bfloat16).astype(jnp.float32)
    for b in range(block_count):
        lanes = slice(b * BLK, (b + 1) * BLK)
        pos = pos_ref[:, lanes]
        tile = pos // BLK
        base = jnp.full(pos.shape, blocks_ref[b, 0], jnp.int32)
        for j in range(1, tile_count):
            base = jnp.where(tile == j, blocks_ref[b, j], base)
        column_ref[:neighbours, lanes] = base * BLK + pos % BLK


def fill_tiles(neighbours, column_ref, share_ref, tiles_ref, spot_ref, start, chunks):
    rows = column_ref.shape[1]
    sub = lax.broadcasted_iota(jnp.int32, (BLK, BLK), 0).astype(jnp.float32).astype(jnp.bfloat16)
    sub = sub.reshape(BLK // PACK, PACK, BLK)

    @pl.loop(*chunks)
    def _(chunk):
        first = pl.multiple_of(chunk * BLK, BLK)
        spot = column_ref[...] - (start + first)
        spot_ref[...] = jnp.where((spot >= 0) & (spot < BLK), spot, -1).astype(jnp.float32)

        @pl.loop(0, rows // BLK)
        def _(b):
            lanes = pl.ds(pl.multiple_of(b * BLK, BLK), BLK)
            row = lambda ref, k: jnp.broadcast_to(ref[k : k + 1, lanes], (PACK, BLK))
            total = jnp.zeros(sub.shape, jnp.bfloat16)
            for k in range(neighbours):
                spot = row(spot_ref, k).astype(jnp.bfloat16)
                share = row(share_ref, k).astype(jnp.bfloat16)
                total = jnp.where(sub == spot[None], share[None], total)
            tiles_ref[lanes, pl.ds(first, BLK)] = total.reshape(BLK, BLK).T


def own_tiles_kernel(
    blocks_ref,
    pos_ref,
    weight_ref,
    seeds_hbm,
    own_hbm,
    column_ref,
    share_ref,
    near_ref,
    own_ref,
    spot_ref,
    sems,
):
    copies = [push(seeds_hbm, near_ref, sems.at[0])]
    fill_edges(blocks_ref, pos_ref, weight_ref, column_ref, share_ref)
    for i in range(own_ref.shape[1] // BLK):
        cols = slice(i * BLK, (i + 1) * BLK)
        fill_tiles(pos_ref.shape[0], column_ref, share_ref, own_ref, spot_ref, 0, (i, i + 1))
        copies.append(push(own_ref.at[:, cols], own_hbm.at[:, cols], sems.at[1 + i]))
    for copy in copies:
        copy.wait()


def pick_a_kernel(me_ref, asked_ref, seeds_ref, after_ref, pick_ref, a_ref, *plane_refs):
    del after_ref
    pick_ref[...] = picks(asked_ref[...], seeds_ref.shape[0])
    for cols in pieces_of(0, a_ref.shape[1]):
        a_ref[:, cols] = dot(pick_ref[...], seeds_ref[:, cols]).astype(jnp.bfloat16)
    to_planes(me_ref[0], a_ref, plane_refs, asked_ref.shape[2])


def pick_b_kernel(
    pick_ref,
    seeds_ref,
    a_ref,
    column_ref,
    share_ref,
    out_a,
    out_b,
    early_ref,
    b_ref,
    spot_ref,
    sems,
    *,
    neighbours,
):
    rows = seeds_ref.shape[0]
    wide = a_ref.shape[1]
    copies = [push(a_ref, out_a, sems.at[0])]
    for i, rows_here in enumerate(strips_of(pick_ref.shape[0])):
        b_ref[rows_here, :] = dot(pick_ref[rows_here, :], seeds_ref[:, wide:]).astype(jnp.bfloat16)
        copies.append(push(b_ref.at[rows_here], out_b.at[rows_here], sems.at[1 + i]))
    chunks = (0, early_ref.shape[1] // BLK)
    fill_tiles(neighbours, column_ref, share_ref, early_ref, spot_ref, rows, chunks)
    for copy in copies:
        copy.wait()


def far_kernel(
    asked_ref,
    early_ref,
    own_ref,
    column_ref,
    share_ref,
    seeds_ref,
    sent_a_ref,
    sent_b_ref,
    after_ref,
    far_ref,
    picked_far_ref,
    sent_base_ref,
    pick_ref,
    picked_ref,
    spot_ref,
    *,
    neighbours,
):
    del after_ref
    rows, width = seeds_ref.shape
    wide = sent_a_ref.shape[1]
    done = early_ref.shape[1]
    far_ref[:, :done] = early_ref[...]
    chunks = (done // BLK, far_ref.shape[1] // BLK)
    fill_tiles(neighbours, column_ref, share_ref, far_ref, spot_ref, rows, chunks)
    pick_ref[...] = picks(asked_ref[...], rows)
    for cols in pieces_of(0, far_ref.shape[1]):
        picked_far_ref[:, cols] = dot(pick_ref[...], far_ref[:, cols]).astype(jnp.bfloat16)
    for cols in pieces_of(0, rows):
        picked_ref[:, cols] = dot(pick_ref[...], own_ref[:, cols]).astype(jnp.bfloat16)
    for cols in pieces_of(0, wide) + pieces_of(wide, width):
        sent = sent_a_ref[:, cols] if cols.stop <= wide else sent_b_ref[:, moved(cols, -wide)]
        sent_base = KEEP * dot(picked_ref[...], seeds_ref[:, cols])
        sent_base = sent_base + ANCHOR * sent.astype(jnp.float32)
        sent_base_ref[:, cols] = sent_base.astype(jnp.bfloat16)


def gather_kernel(*refs):
    *plane_refs, out_ref = refs
    half = plane_refs[0].shape[0] // 2
    for z, plane_ref in enumerate(plane_refs):
        out_ref[z * half : (z + 1) * half, :] = plane_ref[half:, :]


def pair_kernel(slots, *refs):
    count = GROUP // 2
    *plane_refs, other_ref = refs[:-count]
    planes = len(plane_refs)
    for q, out_ref in zip(pair_order(count), refs[-count:]):
        for z, plane_ref in enumerate(plane_refs):
            here = slice(z * slots, (z + 1) * slots)
            there = slice((planes + z) * slots, (planes + z + 1) * slots)
            other = (z * count + q) * slots
            out_ref[here, :] = plane_ref[q * slots : (q + 1) * slots, :]
            out_ref[there, :] = other_ref[other : other + slots, :]


def send_a_kernel(me_ref, tiles_ref, base_ref, *refs, slots):
    pair_refs = refs[: GROUP // 2]
    out_hbm, *plane_refs, received_ref, out_ref, sem = refs[GROUP // 2 :]
    me = me_ref[0]
    from_pairs(me, pair_refs, received_ref, slots)
    copy = push(received_ref, out_hbm, sem)
    for cols in pieces_of(0, received_ref.shape[1]):
        total = KEEP * dot(tiles_ref[...], received_ref[:, cols])
        out_ref[:, cols] = (total + base_ref[:, cols].astype(jnp.float32)).astype(jnp.bfloat16)
    to_planes(me, out_ref, plane_refs, slots)
    copy.wait()


def send_b_kernel(tiles_ref, base_ref, received_ref, after_ref, out_hbm, kept_hbm, out_ref, sems):
    del after_ref
    wide = base_ref.shape[1] - received_ref.shape[1]
    copies = [push(received_ref, kept_hbm, sems.at[0])]
    for i, rows in enumerate(strips_of(out_ref.shape[0])):
        total = KEEP * dot(tiles_ref[rows, :], received_ref[...])
        total = total + base_ref[rows, wide:].astype(jnp.float32)
        out_ref[rows, :] = total.astype(jnp.bfloat16)
        copies.append(push(out_ref.at[rows], out_hbm.at[rows], sems.at[1 + i]))
    for copy in copies:
        copy.wait()


def labels_kernel(
    own_ref,
    far_ref,
    seeds_ref,
    received_a_ref,
    received_b_ref,
    after_ref,
    next_ref,
    rest_ref,
    near_ref,
):
    del after_ref
    near_ref[...] = far_ref[...]
    wide = received_a_ref.shape[1]
    width = seeds_ref.shape[1]
    for cols in pieces_of(0, wide) + pieces_of(wide, width):
        first = cols.stop <= wide
        received = received_a_ref[:, cols] if first else received_b_ref[:, moved(cols, -wide)]
        seeds = ANCHOR * seeds_ref[:, cols].astype(jnp.float32)
        total = dot(own_ref[...], seeds_ref[:, cols]) + dot(far_ref[...], received)
        labels = (KEEP * total + seeds).astype(jnp.bfloat16)
        base = KEEP * dot(own_ref[...], labels) + seeds
        kept = base.astype(jnp.bfloat16)
        next_ref[:, cols] = kept
        rest = (base - kept.astype(jnp.float32)) * REST_SCALE
        rest_ref[:, cols] = rest.astype(jnp.float8_e4m3fn)


def result(tiles_ref, received, base_ref, rest_ref, rows, cols):
    total = KEEP * dot(tiles_ref[rows, :], received) + base_ref[rows, cols].astype(jnp.float32)
    total = total + rest_ref[rows, cols].astype(jnp.float32) * (1 / REST_SCALE)
    return total.astype(jnp.bfloat16)


def last_a_kernel(me_ref, tiles_ref, base_ref, rest_ref, *refs, slots):
    pair_refs = refs[: GROUP // 2]
    out_hbm, received_ref, out_ref, sems = refs[GROUP // 2 :]
    from_pairs(me_ref[0], pair_refs, received_ref, slots)
    copies = []
    for i, cols in enumerate(pieces_of(0, received_ref.shape[1])):
        received = received_ref[:, cols]
        out_ref[:, cols] = result(tiles_ref, received, base_ref, rest_ref, slice(None), cols)
        copies.append(push(out_ref.at[:, cols], out_hbm.at[:, cols], sems.at[i]))
    for copy in copies:
        copy.wait()


def last_b_kernel(tiles_ref, base_ref, rest_ref, received_ref, same_ref, out_hbm, out_ref, sems):
    del same_ref
    width = base_ref.shape[1]
    wide = width - received_ref.shape[1]
    copies = []
    cols = slice(wide, width)
    for i, rows in enumerate(strips_of(out_ref.shape[0])):
        out_ref[rows, :] = result(tiles_ref, received_ref[...], base_ref, rest_ref, rows, cols)
        copies.append(push(out_ref.at[rows], out_hbm.at[rows, cols], sems.at[i]))
    for copy in copies:
        copy.wait()


def swap(x, peers, distance):
    return lax.ppermute(x, "rows", [(i, i ^ distance) for i in range(peers)])


def exchange(rows_out, peers):
    count, width = rows_out.shape
    sent = rows_out.reshape(peers, count // peers, width)
    got = lax.all_to_all(sent, "rows", split_axis=0, concat_axis=0, tiled=True)
    return got.reshape(count, width)


def across(planes, peers):
    order = plane_order(len(planes))
    return [swap(x, peers, GROUP * z) if z else x for z, x in zip(order, planes)]


def within(planes, peers, slots):
    depth, wide = planes[0].shape
    n = len(planes)
    other = call(
        gather_kernel,
        "gather",
        jax.ShapeDtypeStruct((n * depth // 2, wide), jnp.bfloat16),
        [VMEM] * n,
        VMEM,
        flops=LONG,
    )(*planes)
    other = swap(other, peers, 1)
    pairs = call(
        functools.partial(pair_kernel, slots),
        "pair",
        [jax.ShapeDtypeStruct((2 * n * slots, wide), jnp.bfloat16)] * (GROUP // 2),
        [VMEM] * (n + 1),
        [VMEM] * (GROUP // 2),
    )(*planes, other)
    return [swap(x, peers, 2 * q) if q else x for q, x in zip(pair_order(len(pairs)), pairs)]


def on_device(seeds, neighbor_pos, edge_weight, tile_blocks, wanted):
    rows, width = seeds.shape
    peers, slots = wanted.shape[1:]
    count = peers * slots
    neighbours = neighbor_pos.shape[1]
    depth = -(-neighbours // PACK) * PACK
    planes = peers // GROUP
    wide = max(3 * width // 8 // BLK, 1) * BLK
    assert peers & (peers - 1) == 0 and peers >= GROUP
    me = lax.axis_index("rows").astype(jnp.int32).reshape(1)
    sems = pltpu.SemaphoreType.DMA
    bf16 = jnp.bfloat16
    plane_shape = jax.ShapeDtypeStruct((GROUP * slots, wide), bf16)
    n_a, n_out, n_sent = len(pieces_of(0, wide)), len(strips_of(rows)), len(strips_of(count))

    asked = lax.all_to_all(
        wanted.reshape(peers, 1, slots), "rows", split_axis=0, concat_axis=0, tiled=True
    )
    own, column, share, near_seeds = call(
        own_tiles_kernel,
        "own_tiles",
        [
            far_out((rows, rows)),
            near_out((depth, rows), jnp.int32),
            near_out((depth, rows), jnp.float32),
            near_out((rows, width)),
        ],
        [SMEM, VMEM, VMEM, HBM],
        [HBM, VMEM, VMEM, VMEM],
        [
            pltpu.VMEM((rows, rows), bf16),
            pltpu.VMEM((depth, rows), jnp.float32),
            sems((1 + rows // BLK,)),
        ],
        flops=neighbours * rows * rows,
    )(far_in(tile_blocks), far_in(neighbor_pos.T), far_in(edge_weight.T), far_in(seeds))
    pick, near_a, *sent_planes = call(
        pick_a_kernel,
        "pick_a",
        [near_out((count, rows)), near_out((count, wide))] + [plane_shape] * planes,
        [SMEM, VMEM, VMEM, HBM],
        [VMEM] * (2 + planes),
        flops=2 * count * rows * wide,
    )(me, asked, near_seeds, far_in(own))
    got_planes = across(sent_planes, peers)
    sent_a, sent_b, early = call(
        functools.partial(pick_b_kernel, neighbours=neighbours),
        "pick_b",
        [
            far_out((count, wide)),
            far_out((count, width - wide)),
            near_out((rows, count // BLK * EARLY // 8 * BLK)),
        ],
        [VMEM] * 5,
        [HBM, HBM, VMEM],
        [
            pltpu.VMEM((count, width - wide), bf16),
            pltpu.VMEM((depth, rows), jnp.float32),
            sems((1 + n_sent,)),
        ],
        flops=2 * count * rows * (width - wide),
    )(pick, near_seeds, near_a, column, share)
    received_b = exchange(sent_b, peers)
    got_pairs = within(got_planes, peers, slots)
    far, picked_far, sent_base = call(
        functools.partial(far_kernel, neighbours=neighbours),
        "far",
        [far_out((rows, count)), near_out((count, count)), near_out((count, width))],
        [VMEM] * 8 + [ANY],
        [VMEM] * 3,
        [
            pltpu.VMEM((count, rows), bf16),
            pltpu.VMEM((count, rows), bf16),
            pltpu.VMEM((depth, rows), jnp.float32),
        ],
        flops=2 * rows * count * (count + rows + width) + neighbours * rows * count,
    )(
        asked,
        early,
        far_in(own),
        column,
        share,
        far_in(seeds),
        far_in(sent_a),
        far_in(sent_b),
        got_pairs[0],
    )
    received_a, *sent_planes = call(
        functools.partial(send_a_kernel, slots=slots),
        "send_a",
        [far_out((count, wide))] + [plane_shape] * planes,
        [SMEM] + [VMEM] * (2 + GROUP // 2),
        [HBM] + [VMEM] * planes,
        [pltpu.VMEM((count, wide), bf16), pltpu.VMEM((count, wide), bf16), sems],
        flops=2 * count * count * wide,
    )(me, picked_far, sent_base, *got_pairs)
    got_planes = across(sent_planes, peers)
    sent_b, received_b = call(
        send_b_kernel,
        "send_b",
        [far_out((count, width - wide)), far_out((count, width - wide))],
        [VMEM] * 3 + [ANY],
        [HBM, HBM],
        [pltpu.VMEM((count, width - wide), bf16), sems((1 + n_sent,))],
        flops=2 * count * count * (width - wide),
        nbytes=2 * count * (3 * (width - wide) + count + width),
    )(picked_far, sent_base, received_b, sent_planes[0])
    last_b = exchange(sent_b, peers)
    got_pairs = within(got_planes, peers, slots)
    next_base, rest, near_far = call(
        labels_kernel,
        "labels",
        [
            near_out((rows, width)),
            near_out((rows, width), jnp.float8_e4m3fn),
            near_out((rows, count)),
        ],
        [VMEM] * 5 + [ANY],
        [VMEM] * 3,
        flops=2 * rows * (count + 2 * rows) * width,
    )(
        far_in(own),
        far_in(far),
        far_in(seeds),
        far_in(received_a),
        far_in(received_b),
        got_pairs[0],
    )
    first = call(
        functools.partial(last_a_kernel, slots=slots),
        "last_a",
        far_out((rows, width)),
        [SMEM] + [VMEM] * (3 + GROUP // 2),
        HBM,
        [pltpu.VMEM((count, wide), bf16), pltpu.VMEM((rows, wide), bf16), sems((n_a,))],
        flops=2 * rows * count * wide,
    )(me, near_far, next_base, rest, *got_pairs)
    return call(
        last_b_kernel,
        "last_b",
        far_out((rows, width)),
        [VMEM] * 4 + [HBM],
        HBM,
        [pltpu.VMEM((rows, width - wide), bf16), sems((n_out,))],
        flops=2 * rows * count * (width - wide),
        nbytes=2 * rows * count + 5 * rows * width + 2 * count * width,
        aliases={4: 0},
    )(near_far, next_base, rest, last_b, far_in(first))


def solution(mesh):
    in_specs = (
        P(("parts", "rows"), "cls"),
        P(("parts", "rows"), None),
        P(("parts", "rows"), None),
        P(("parts", "rows"), None),
        P(("parts", "rows"), None, None),
    )
    out_specs = P(("parts", "rows"), "cls")
    return jax.shard_map(
        on_device, mesh=mesh, in_specs=in_specs, out_specs=out_specs, check_vma=False
    )
```

```python
import functools
import math

import jax
import jax.numpy as jnp
from jax import lax
from jax.experimental import pallas as pl
from jax.experimental.pallas import tpu as pltpu
from jax.sharding import PartitionSpec as P

BLK = 128
COLS = 256
GROUP = 8
PACK = 16
VMEM_LIMIT = 32 * 1024 * 1024
NEAR_BYTES = 1024 * 1024
KEEP = 0.85
ANCHOR = 0.15
REST_SCALE = 4096.0
LONG = 4 * 10**10
EARLY = 2

SMEM = pl.BlockSpec(memory_space=pltpu.SMEM)
VMEM = pl.BlockSpec(memory_space=pltpu.VMEM)
HBM = pl.BlockSpec(memory_space=pltpu.HBM)
ANY = pl.BlockSpec(memory_space=pl.ANY)


def far_out(shape, dtype=jnp.bfloat16):
    return pltpu.HBM(shape, dtype)


def far_in(x):
    return pltpu.with_memory_space_constraint(x, pltpu.HBM)


def near_out(shape, dtype=jnp.bfloat16):
    small = math.prod(shape) * jnp.dtype(dtype).itemsize <= NEAR_BYTES
    return pltpu.VMEM(shape, dtype) if small else jax.ShapeDtypeStruct(shape, dtype)


def call(kernel, name, out_shape, in_specs, out_specs, scratch_shapes=(), flops=0, nbytes=0, aliases=None):
    return pl.pallas_call(
        kernel,
        out_shape=out_shape,
        in_specs=in_specs,
        out_specs=out_specs,
        scratch_shapes=scratch_shapes,
        input_output_aliases=aliases or {},
        compiler_params=pltpu.CompilerParams(vmem_limit_bytes=VMEM_LIMIT),
        cost_estimate=pl.CostEstimate(flops=flops, bytes_accessed=nbytes, transcendentals=0),
        name=name,
    )


def dot(a, b):
    return jnp.dot(a, b, preferred_element_type=jnp.float32)


def pieces_of(first, last):
    return [slice(c, min(c + COLS, last)) for c in range(first, last, COLS)]


def strips_of(count):
    return [slice(r, r + BLK) for r in range(0, count, BLK)]


def moved(cols, by):
    return slice(cols.start + by, cols.stop + by)


def push(source, target, sem):
    copy = pltpu.make_async_copy(source, target, sem)
    copy.start()
    return copy


def picks(asked, rows):
    peers, _, slots = asked.shape
    count = peers * slots
    spread = jnp.broadcast_to(asked.astype(jnp.float32), (peers, slots, slots))
    spread = spread.reshape(count, slots)
    slot = lax.broadcasted_iota(jnp.int32, (count, slots), 0) % slots
    lane = lax.broadcasted_iota(jnp.int32, (count, slots), 1)
    row = jnp.sum(jnp.where(slot == lane, spread, 0.0), axis=1, keepdims=True)
    hits = lax.broadcasted_iota(jnp.int32, (count, rows), 1) == row.astype(jnp.int32)
    return hits.astype(jnp.float32).astype(jnp.bfloat16)


def block(peer, slots):
    return pl.ds(pl.multiple_of(peer * slots, slots), slots)


def pair_order(pairs):
    return [0] + list(range(pairs - 1, 0, -1))


def plane_order(planes):
    return [0] + list(range(2, planes)) + [1]


def to_planes(me, rows_ref, plane_refs, slots):
    for z, plane_ref in zip(plane_order(len(plane_refs)), plane_refs):
        for s in range(2):
            for q in range(GROUP // 2):
                peer = me ^ (GROUP * z + 2 * q + s)
                at = (s * (GROUP // 2) + q) * slots
                plane_ref[at : at + slots, :] = rows_ref[block(peer, slots), :]


def from_pairs(me, pair_refs, rows_ref, slots):
    planes = pair_refs[0].shape[0] // (2 * slots)
    for q, pair_ref in zip(pair_order(len(pair_refs)), pair_refs):
        for s in range(2):
            for i, z in enumerate(plane_order(planes)):
                peer = me ^ (GROUP * z + 2 * q + s)
                at = (s * planes + i) * slots
                rows_ref[block(peer, slots), :] = pair_ref[at : at + slots, :]


def fill_edges(blocks_ref, pos_ref, weight_ref, column_ref, share_ref):
    block_count, tile_count = blocks_ref.shape
    neighbours = pos_ref.shape[0]
    column_ref[...] = jnp.full(column_ref.shape, -1, jnp.int32)
    share_ref[...] = jnp.zeros(share_ref.shape, jnp.float32)
    weights = weight_ref[...].astype(jnp.float32)
    share = weights / jnp.sum(weights, axis=0, keepdims=True)
    share_ref[:neighbours, :] = share.astype(jnp.bfloat16).astype(jnp.float32)
    for b in range(block_count):
        lanes = slice(b * BLK, (b + 1) * BLK)
        pos = pos_ref[:, lanes]
        tile = pos // BLK
        base = jnp.full(pos.shape, blocks_ref[b, 0], jnp.int32)
        for j in range(1, tile_count):
            base = jnp.where(tile == j, blocks_ref[b, j], base)
        column_ref[:neighbours, lanes] = base * BLK + pos % BLK


def fill_tiles(neighbours, column_ref, share_ref, tiles_ref, spot_ref, start, chunks):
    rows = column_ref.shape[1]
    sub = lax.broadcasted_iota(jnp.int32, (BLK, BLK), 0).astype(jnp.float32).astype(jnp.bfloat16)
    sub = sub.reshape(BLK // PACK, PACK, BLK)

    @pl.loop(*chunks)
    def _(chunk):
        first = pl.multiple_of(chunk * BLK, BLK)
        spot = column_ref[...] - (start + first)
        spot_ref[...] = jnp.where((spot >= 0) & (spot < BLK), spot, -1).astype(jnp.float32)

        @pl.loop(0, rows // BLK)
        def _(b):
            lanes = pl.ds(pl.multiple_of(b * BLK, BLK), BLK)
            row = lambda ref, k: jnp.broadcast_to(ref[k : k + 1, lanes], (PACK, BLK))
            total = jnp.zeros(sub.shape, jnp.bfloat16)
            for k in range(neighbours):
                spot = row(spot_ref, k).astype(jnp.bfloat16)
                share = row(share_ref, k).astype(jnp.bfloat16)
                total = jnp.where(sub == spot[None], share[None], total)
            tiles_ref[lanes, pl.ds(first, BLK)] = total.reshape(BLK, BLK).T


def own_tiles_kernel(
    blocks_ref,
    pos_ref,
    weight_ref,
    seeds_hbm,
    own_hbm,
    column_ref,
    share_ref,
    near_ref,
    own_ref,
    spot_ref,
    sems,
):
    copies = [push(seeds_hbm, near_ref, sems.at[0])]
    fill_edges(blocks_ref, pos_ref, weight_ref, column_ref, share_ref)
    for i in range(own_ref.shape[1] // BLK):
        cols = slice(i * BLK, (i + 1) * BLK)
        fill_tiles(pos_ref.shape[0], column_ref, share_ref, own_ref, spot_ref, 0, (i, i + 1))
        copies.append(push(own_ref.at[:, cols], own_hbm.at[:, cols], sems.at[1 + i]))
    for copy in copies:
        copy.wait()


def pick_a_kernel(me_ref, asked_ref, seeds_ref, after_ref, pick_ref, a_ref, *plane_refs):
    del after_ref
    pick_ref[...] = picks(asked_ref[...], seeds_ref.shape[0])
    for cols in pieces_of(0, a_ref.shape[1]):
        a_ref[:, cols] = dot(pick_ref[...], seeds_ref[:, cols]).astype(jnp.bfloat16)
    to_planes(me_ref[0], a_ref, plane_refs, asked_ref.shape[2])


def pick_b_kernel(
    pick_ref,
    seeds_ref,
    a_ref,
    column_ref,
    share_ref,
    out_a,
    out_b,
    early_ref,
    b_ref,
    spot_ref,
    sems,
    *,
    neighbours,
):
    rows = seeds_ref.shape[0]
    wide = a_ref.shape[1]
    copies = [push(a_ref, out_a, sems.at[0])]
    for i, rows_here in enumerate(strips_of(pick_ref.shape[0])):
        b_ref[rows_here, :] = dot(pick_ref[rows_here, :], seeds_ref[:, wide:]).astype(jnp.bfloat16)
        copies.append(push(b_ref.at[rows_here], out_b.at[rows_here], sems.at[1 + i]))
    chunks = (0, early_ref.shape[1] // BLK)
    fill_tiles(neighbours, column_ref, share_ref, early_ref, spot_ref, rows, chunks)
    for copy in copies:
        copy.wait()


def far_kernel(
    asked_ref,
    early_ref,
    own_ref,
    column_ref,
    share_ref,
    seeds_ref,
    sent_a_ref,
    sent_b_ref,
    after_ref,
    far_ref,
    picked_far_ref,
    sent_base_ref,
    whole_ref,
    pick_ref,
    picked_ref,
    spot_ref,
    *,
    neighbours,
):
    del after_ref
    rows, width = seeds_ref.shape
    head = own_ref.shape[1]
    whole_ref[:, :head] = own_ref[...]
    chunks = (head // BLK, rows // BLK)
    fill_tiles(neighbours, column_ref, share_ref, whole_ref, spot_ref, 0, chunks)
    wide = sent_a_ref.shape[1]
    done = early_ref.shape[1]
    far_ref[:, :done] = early_ref[...]
    chunks = (done // BLK, far_ref.shape[1] // BLK)
    fill_tiles(neighbours, column_ref, share_ref, far_ref, spot_ref, rows, chunks)
    pick_ref[...] = picks(asked_ref[...], rows)
    for cols in pieces_of(0, far_ref.shape[1]):
        picked_far_ref[:, cols] = dot(pick_ref[...], far_ref[:, cols]).astype(jnp.bfloat16)
    for cols in pieces_of(0, rows):
        picked_ref[:, cols] = dot(pick_ref[...], whole_ref[:, cols]).astype(jnp.bfloat16)
    for cols in pieces_of(0, wide) + pieces_of(wide, width):
        sent = sent_a_ref[:, cols] if cols.stop <= wide else sent_b_ref[:, moved(cols, -wide)]
        sent_base = KEEP * dot(picked_ref[...], seeds_ref[:, cols])
        sent_base = sent_base + ANCHOR * sent.astype(jnp.float32)
        sent_base_ref[:, cols] = sent_base.astype(jnp.bfloat16)


def gather_kernel(*refs):
    *plane_refs, out_ref = refs
    half = plane_refs[0].shape[0] // 2
    for z, plane_ref in enumerate(plane_refs):
        out_ref[z * half : (z + 1) * half, :] = plane_ref[half:, :]


def pair_kernel(slots, *refs):
    count = GROUP // 2
    *plane_refs, other_ref = refs[:-count]
    planes = len(plane_refs)
    for q, out_ref in zip(pair_order(count), refs[-count:]):
        for z, plane_ref in enumerate(plane_refs):
            here = slice(z * slots, (z + 1) * slots)
            there = slice((planes + z) * slots, (planes + z + 1) * slots)
            other = (z * count + q) * slots
            out_ref[here, :] = plane_ref[q * slots : (q + 1) * slots, :]
            out_ref[there, :] = other_ref[other : other + slots, :]


def send_a_kernel(me_ref, tiles_ref, base_ref, *refs, slots):
    pair_refs = refs[: GROUP // 2]
    out_hbm, *plane_refs, received_ref, out_ref, sem = refs[GROUP // 2 :]
    me = me_ref[0]
    from_pairs(me, pair_refs, received_ref, slots)
    copy = push(received_ref, out_hbm, sem)
    for cols in pieces_of(0, received_ref.shape[1]):
        total = KEEP * dot(tiles_ref[...], received_ref[:, cols])
        out_ref[:, cols] = (total + base_ref[:, cols].astype(jnp.float32)).astype(jnp.bfloat16)
    to_planes(me, out_ref, plane_refs, slots)
    copy.wait()


def send_b_kernel(tiles_ref, base_ref, received_ref, after_ref, out_hbm, kept_hbm, out_ref, sems):
    del after_ref
    wide = base_ref.shape[1] - received_ref.shape[1]
    copies = [push(received_ref, kept_hbm, sems.at[0])]
    for i, rows in enumerate(strips_of(out_ref.shape[0])):
        total = KEEP * dot(tiles_ref[rows, :], received_ref[...])
        total = total + base_ref[rows, wide:].astype(jnp.float32)
        out_ref[rows, :] = total.astype(jnp.bfloat16)
        copies.append(push(out_ref.at[rows], out_hbm.at[rows], sems.at[1 + i]))
    for copy in copies:
        copy.wait()


def labels_kernel(
    own_ref,
    far_ref,
    seeds_ref,
    received_a_ref,
    received_b_ref,
    after_ref,
    next_ref,
    rest_ref,
    near_ref,
):
    del after_ref
    near_ref[...] = far_ref[...]
    wide = received_a_ref.shape[1]
    width = seeds_ref.shape[1]
    for cols in pieces_of(0, wide) + pieces_of(wide, width):
        first = cols.stop <= wide
        received = received_a_ref[:, cols] if first else received_b_ref[:, moved(cols, -wide)]
        seeds = ANCHOR * seeds_ref[:, cols].astype(jnp.float32)
        total = dot(own_ref[...], seeds_ref[:, cols]) + dot(far_ref[...], received)
        labels = (KEEP * total + seeds).astype(jnp.bfloat16)
        base = KEEP * dot(own_ref[...], labels) + seeds
        kept = base.astype(jnp.bfloat16)
        next_ref[:, cols] = kept
        rest = (base - kept.astype(jnp.float32)) * REST_SCALE
        rest_ref[:, cols] = rest.astype(jnp.float8_e4m3fn)


def result(tiles_ref, received, base_ref, rest_ref, rows, cols):
    total = KEEP * dot(tiles_ref[rows, :], received) + base_ref[rows, cols].astype(jnp.float32)
    total = total + rest_ref[rows, cols].astype(jnp.float32) * (1 / REST_SCALE)
    return total.astype(jnp.bfloat16)


def last_a_kernel(me_ref, tiles_ref, base_ref, rest_ref, *refs, slots):
    pair_refs = refs[: GROUP // 2]
    out_hbm, received_ref, out_ref, sems = refs[GROUP // 2 :]
    from_pairs(me_ref[0], pair_refs, received_ref, slots)
    copies = []
    for i, cols in enumerate(pieces_of(0, received_ref.shape[1])):
        received = received_ref[:, cols]
        out_ref[:, cols] = result(tiles_ref, received, base_ref, rest_ref, slice(None), cols)
        copies.append(push(out_ref.at[:, cols], out_hbm.at[:, cols], sems.at[i]))
    for copy in copies:
        copy.wait()


def last_b_kernel(tiles_ref, base_ref, rest_ref, received_ref, same_ref, out_hbm, out_ref, sems):
    del same_ref
    width = base_ref.shape[1]
    wide = width - received_ref.shape[1]
    copies = []
    cols = slice(wide, width)
    for i, rows in enumerate(strips_of(out_ref.shape[0])):
        out_ref[rows, :] = result(tiles_ref, received_ref[...], base_ref, rest_ref, rows, cols)
        copies.append(push(out_ref.at[rows], out_hbm.at[rows, cols], sems.at[i]))
    for copy in copies:
        copy.wait()


def swap(x, peers, distance):
    return lax.ppermute(x, "rows", [(i, i ^ distance) for i in range(peers)])


def exchange(rows_out, peers):
    count, width = rows_out.shape
    sent = rows_out.reshape(peers, count // peers, width)
    got = lax.all_to_all(sent, "rows", split_axis=0, concat_axis=0, tiled=True)
    return got.reshape(count, width)


def across(planes, peers):
    order = plane_order(len(planes))
    return [swap(x, peers, GROUP * z) if z else x for z, x in zip(order, planes)]


def within(planes, peers, slots):
    depth, wide = planes[0].shape
    n = len(planes)
    other = call(
        gather_kernel,
        "gather",
        jax.ShapeDtypeStruct((n * depth // 2, wide), jnp.bfloat16),
        [VMEM] * n,
        VMEM,
        flops=LONG,
    )(*planes)
    other = swap(other, peers, 1)
    pairs = call(
        functools.partial(pair_kernel, slots),
        "pair",
        [jax.ShapeDtypeStruct((2 * n * slots, wide), jnp.bfloat16)] * (GROUP // 2),
        [VMEM] * (n + 1),
        [VMEM] * (GROUP // 2),
    )(*planes, other)
    return [swap(x, peers, 2 * q) if q else x for q, x in zip(pair_order(len(pairs)), pairs)]


def on_device(seeds, neighbor_pos, edge_weight, tile_blocks, wanted):
    rows, width = seeds.shape
    peers, slots = wanted.shape[1:]
    count = peers * slots
    neighbours = neighbor_pos.shape[1]
    depth = -(-neighbours // PACK) * PACK
    planes = peers // GROUP
    wide = max(3 * width // 8 // BLK, 1) * BLK
    assert peers & (peers - 1) == 0 and peers >= GROUP
    head = rows - BLK
    me = lax.axis_index("rows").astype(jnp.int32).reshape(1)
    sems = pltpu.SemaphoreType.DMA
    bf16 = jnp.bfloat16
    plane_shape = jax.ShapeDtypeStruct((GROUP * slots, wide), bf16)
    n_a, n_out, n_sent = len(pieces_of(0, wide)), len(strips_of(rows)), len(strips_of(count))

    asked = lax.all_to_all(
        wanted.reshape(peers, 1, slots), "rows", split_axis=0, concat_axis=0, tiled=True
    )
    own, column, share, near_seeds = call(
        own_tiles_kernel,
        "own_tiles",
        [
            far_out((rows, head)),
            near_out((depth, rows), jnp.int32),
            near_out((depth, rows), jnp.float32),
            near_out((rows, width)),
        ],
        [SMEM, VMEM, VMEM, HBM],
        [HBM, VMEM, VMEM, VMEM],
        [
            pltpu.VMEM((rows, head), bf16),
            pltpu.VMEM((depth, rows), jnp.float32),
            sems((1 + head // BLK,)),
        ],
        flops=neighbours * rows * rows,
    )(far_in(tile_blocks), far_in(neighbor_pos.T), far_in(edge_weight.T), far_in(seeds))
    pick, near_a, *sent_planes = call(
        pick_a_kernel,
        "pick_a",
        [near_out((count, rows)), near_out((count, wide))] + [plane_shape] * planes,
        [SMEM, VMEM, VMEM, HBM],
        [VMEM] * (2 + planes),
        flops=2 * count * rows * wide,
    )(me, asked, near_seeds, far_in(own))
    got_planes = across(sent_planes, peers)
    sent_a, sent_b, early = call(
        functools.partial(pick_b_kernel, neighbours=neighbours),
        "pick_b",
        [
            far_out((count, wide)),
            far_out((count, width - wide)),
            near_out((rows, count // BLK * EARLY // 8 * BLK)),
        ],
        [VMEM] * 5,
        [HBM, HBM, VMEM],
        [
            pltpu.VMEM((count, width - wide), bf16),
            pltpu.VMEM((depth, rows), jnp.float32),
            sems((1 + n_sent,)),
        ],
        flops=2 * count * rows * (width - wide),
    )(pick, near_seeds, near_a, column, share)
    received_b = exchange(sent_b, peers)
    got_pairs = within(got_planes, peers, slots)
    far, picked_far, sent_base, own = call(
        functools.partial(far_kernel, neighbours=neighbours),
        "far",
        [
            far_out((rows, count)),
            near_out((count, count)),
            near_out((count, width)),
            far_out((rows, rows)),
        ],
        [VMEM] * 8 + [ANY],
        [VMEM] * 4,
        [
            pltpu.VMEM((count, rows), bf16),
            pltpu.VMEM((count, rows), bf16),
            pltpu.VMEM((depth, rows), jnp.float32),
        ],
        flops=2 * rows * count * (count + rows + width) + neighbours * rows * count,
    )(
        asked,
        early,
        far_in(own),
        column,
        share,
        far_in(seeds),
        far_in(sent_a),
        far_in(sent_b),
        got_pairs[0],
    )
    received_a, *sent_planes = call(
        functools.partial(send_a_kernel, slots=slots),
        "send_a",
        [far_out((count, wide))] + [plane_shape] * planes,
        [SMEM] + [VMEM] * (2 + GROUP // 2),
        [HBM] + [VMEM] * planes,
        [pltpu.VMEM((count, wide), bf16), pltpu.VMEM((count, wide), bf16), sems],
        flops=2 * count * count * wide,
    )(me, picked_far, sent_base, *got_pairs)
    got_planes = across(sent_planes, peers)
    sent_b, received_b = call(
        send_b_kernel,
        "send_b",
        [far_out((count, width - wide)), far_out((count, width - wide))],
        [VMEM] * 3 + [ANY],
        [HBM, HBM],
        [pltpu.VMEM((count, width - wide), bf16), sems((1 + n_sent,))],
        flops=2 * count * count * (width - wide),
        nbytes=2 * count * (3 * (width - wide) + count + width),
    )(picked_far, sent_base, received_b, sent_planes[0])
    last_b = exchange(sent_b, peers)
    got_pairs = within(got_planes, peers, slots)
    next_base, rest, near_far = call(
        labels_kernel,
        "labels",
        [
            near_out((rows, width)),
            near_out((rows, width), jnp.float8_e4m3fn),
            near_out((rows, count)),
        ],
        [VMEM] * 5 + [ANY],
        [VMEM] * 3,
        flops=2 * rows * (count + 2 * rows) * width,
    )(
        far_in(own),
        far_in(far),
        far_in(seeds),
        far_in(received_a),
        far_in(received_b),
        got_pairs[0],
    )
    first = call(
        functools.partial(last_a_kernel, slots=slots),
        "last_a",
        far_out((rows, width)),
        [SMEM] + [VMEM] * (3 + GROUP // 2),
        HBM,
        [pltpu.VMEM((count, wide), bf16), pltpu.VMEM((rows, wide), bf16), sems((n_a,))],
        flops=2 * rows * count * wide,
    )(me, near_far, next_base, rest, *got_pairs)
    return call(
        last_b_kernel,
        "last_b",
        far_out((rows, width)),
        [VMEM] * 4 + [HBM],
        HBM,
        [pltpu.VMEM((rows, width - wide), bf16), sems((n_out,))],
        flops=2 * rows * count * (width - wide),
        nbytes=2 * rows * count + 5 * rows * width + 2 * count * width,
        aliases={4: 0},
    )(near_far, next_base, rest, last_b, far_in(first))


def solution(mesh):
    in_specs = (
        P(("parts", "rows"), "cls"),
        P(("parts", "rows"), None),
        P(("parts", "rows"), None),
        P(("parts", "rows"), None),
        P(("parts", "rows"), None, None),
    )
    out_specs = P(("parts", "rows"), "cls")
    return jax.shard_map(
        on_device, mesh=mesh, in_specs=in_specs, out_specs=out_specs, check_vma=False
    )
```

```python
import functools
import math

import jax
import jax.numpy as jnp
from jax import lax
from jax.experimental import pallas as pl
from jax.experimental.pallas import tpu as pltpu
from jax.sharding import PartitionSpec as P

BLK = 128
COLS = 256
GROUP = 8
PACK = 16
VMEM_LIMIT = 32 * 1024 * 1024
NEAR_BYTES = 1024 * 1024
KEEP = 0.85
ANCHOR = 0.15
REST_SCALE = 4096.0
LONG = 4 * 10**10
EARLY = 2

SMEM = pl.BlockSpec(memory_space=pltpu.SMEM)
VMEM = pl.BlockSpec(memory_space=pltpu.VMEM)
HBM = pl.BlockSpec(memory_space=pltpu.HBM)
ANY = pl.BlockSpec(memory_space=pl.ANY)


def far_out(shape, dtype=jnp.bfloat16):
    return pltpu.HBM(shape, dtype)


def far_in(x):
    return pltpu.with_memory_space_constraint(x, pltpu.HBM)


def near_out(shape, dtype=jnp.bfloat16):
    small = math.prod(shape) * jnp.dtype(dtype).itemsize <= NEAR_BYTES
    return pltpu.VMEM(shape, dtype) if small else jax.ShapeDtypeStruct(shape, dtype)


def call(kernel, name, out_shape, in_specs, out_specs, scratch_shapes=(), flops=0, nbytes=0, aliases=None):
    return pl.pallas_call(
        kernel,
        out_shape=out_shape,
        in_specs=in_specs,
        out_specs=out_specs,
        scratch_shapes=scratch_shapes,
        input_output_aliases=aliases or {},
        compiler_params=pltpu.CompilerParams(vmem_limit_bytes=VMEM_LIMIT),
        cost_estimate=pl.CostEstimate(flops=flops, bytes_accessed=nbytes, transcendentals=0),
        name=name,
    )


def dot(a, b):
    return jnp.dot(a, b, preferred_element_type=jnp.float32)


def pieces_of(first, last):
    return [slice(c, min(c + COLS, last)) for c in range(first, last, COLS)]


def strips_of(count):
    return [slice(r, r + BLK) for r in range(0, count, BLK)]


def moved(cols, by):
    return slice(cols.start + by, cols.stop + by)


def push(source, target, sem):
    copy = pltpu.make_async_copy(source, target, sem)
    copy.start()
    return copy


def picks(asked, rows):
    peers, _, slots = asked.shape
    count = peers * slots
    spread = jnp.broadcast_to(asked.astype(jnp.float32), (peers, slots, slots))
    spread = spread.reshape(count, slots)
    slot = lax.broadcasted_iota(jnp.int32, (count, slots), 0) % slots
    lane = lax.broadcasted_iota(jnp.int32, (count, slots), 1)
    row = jnp.sum(jnp.where(slot == lane, spread, 0.0), axis=1, keepdims=True)
    hits = lax.broadcasted_iota(jnp.int32, (count, rows), 1) == row.astype(jnp.int32)
    return hits.astype(jnp.float32).astype(jnp.bfloat16)


def block(peer, slots):
    return pl.ds(pl.multiple_of(peer * slots, slots), slots)


def pair_order(pairs):
    return [0] + list(range(pairs - 1, 0, -1))


def plane_order(planes):
    return [0] + list(range(2, planes)) + [1]


def plane_of(z, planes, device):
    other = {1: 2, 2: 3, 3: 1}.get(z, z) if planes > 3 else z
    return z + (device & 1) * (other - z)


def to_planes(me, rows_ref, plane_refs, slots):
    for z, plane_ref in zip(plane_order(len(plane_refs)), plane_refs):
        for s in range(2):
            for q in range(GROUP // 2):
                peer = me ^ (GROUP * plane_of(z, len(plane_refs), me) + 2 * q + s)
                at = (s * (GROUP // 2) + q) * slots
                plane_ref[at : at + slots, :] = rows_ref[block(peer, slots), :]


def from_pairs(me, pair_refs, rows_ref, slots):
    planes = pair_refs[0].shape[0] // (2 * slots)
    for q, pair_ref in zip(pair_order(len(pair_refs)), pair_refs):
        for s in range(2):
            for i, z in enumerate(plane_order(planes)):
                holder = me ^ (2 * q + s)
                peer = holder ^ (GROUP * plane_of(z, planes, holder))
                at = (s * planes + i) * slots
                rows_ref[block(peer, slots), :] = pair_ref[at : at + slots, :]


def fill_edges(blocks_ref, pos_ref, weight_ref, column_ref, share_ref):
    block_count, tile_count = blocks_ref.shape
    neighbours = pos_ref.shape[0]
    column_ref[...] = jnp.full(column_ref.shape, -1, jnp.int32)
    share_ref[...] = jnp.zeros(share_ref.shape, jnp.float32)
    weights = weight_ref[...].astype(jnp.float32)
    share = weights / jnp.sum(weights, axis=0, keepdims=True)
    share_ref[:neighbours, :] = share.astype(jnp.bfloat16).astype(jnp.float32)
    for b in range(block_count):
        lanes = slice(b * BLK, (b + 1) * BLK)
        pos = pos_ref[:, lanes]
        tile = pos // BLK
        base = jnp.full(pos.shape, blocks_ref[b, 0], jnp.int32)
        for j in range(1, tile_count):
            base = jnp.where(tile == j, blocks_ref[b, j], base)
        column_ref[:neighbours, lanes] = base * BLK + pos % BLK


def fill_tiles(neighbours, column_ref, share_ref, tiles_ref, spot_ref, start, chunks):
    rows = column_ref.shape[1]
    sub = lax.broadcasted_iota(jnp.int32, (BLK, BLK), 0).astype(jnp.float32).astype(jnp.bfloat16)
    sub = sub.reshape(BLK // PACK, PACK, BLK)

    @pl.loop(*chunks)
    def _(chunk):
        first = pl.multiple_of(chunk * BLK, BLK)
        spot = column_ref[...] - (start + first)
        spot_ref[...] = jnp.where((spot >= 0) & (spot < BLK), spot, -1).astype(jnp.float32)

        @pl.loop(0, rows // BLK)
        def _(b):
            lanes = pl.ds(pl.multiple_of(b * BLK, BLK), BLK)
            row = lambda ref, k: jnp.broadcast_to(ref[k : k + 1, lanes], (PACK, BLK))
            total = jnp.zeros(sub.shape, jnp.bfloat16)
            for k in range(neighbours):
                spot = row(spot_ref, k).astype(jnp.bfloat16)
                share = row(share_ref, k).astype(jnp.bfloat16)
                total = jnp.where(sub == spot[None], share[None], total)
            tiles_ref[lanes, pl.ds(first, BLK)] = total.reshape(BLK, BLK).T


def own_tiles_kernel(
    blocks_ref,
    pos_ref,
    weight_ref,
    seeds_hbm,
    own_hbm,
    column_ref,
    share_ref,
    near_ref,
    own_ref,
    spot_ref,
    sems,
):
    copies = [push(seeds_hbm, near_ref, sems.at[0])]
    fill_edges(blocks_ref, pos_ref, weight_ref, column_ref, share_ref)
    for i in range(own_ref.shape[1] // BLK):
        cols = slice(i * BLK, (i + 1) * BLK)
        fill_tiles(pos_ref.shape[0], column_ref, share_ref, own_ref, spot_ref, 0, (i, i + 1))
        copies.append(push(own_ref.at[:, cols], own_hbm.at[:, cols], sems.at[1 + i]))
    for copy in copies:
        copy.wait()


def pick_a_kernel(me_ref, asked_ref, seeds_ref, after_ref, pick_ref, *refs):
    *plane_refs, a_ref = refs
    del after_ref
    pick_ref[...] = picks(asked_ref[...], seeds_ref.shape[0])
    for cols in pieces_of(0, a_ref.shape[1]):
        a_ref[:, cols] = dot(pick_ref[...], seeds_ref[:, cols]).astype(jnp.bfloat16)
    to_planes(me_ref[0], a_ref, plane_refs, asked_ref.shape[2])


def pick_b_kernel(
    pick_ref,
    seeds_ref,
    column_ref,
    share_ref,
    out_b,
    early_ref,
    b_ref,
    spot_ref,
    sems,
    *,
    neighbours,
):
    rows, width = seeds_ref.shape
    wide = width - b_ref.shape[1]
    copies = []
    for i, rows_here in enumerate(strips_of(pick_ref.shape[0])):
        b_ref[rows_here, :] = dot(pick_ref[rows_here, :], seeds_ref[:, wide:]).astype(jnp.bfloat16)
        copies.append(push(b_ref.at[rows_here], out_b.at[rows_here], sems.at[i]))
    chunks = (0, early_ref.shape[1] // BLK)
    fill_tiles(neighbours, column_ref, share_ref, early_ref, spot_ref, rows, chunks)
    for copy in copies:
        copy.wait()


def far_kernel(
    asked_ref,
    early_ref,
    own_ref,
    column_ref,
    share_ref,
    seeds_ref,
    after_ref,
    far_ref,
    picked_far_ref,
    sent_base_ref,
    whole_ref,
    pick_ref,
    picked_ref,
    spot_ref,
    *,
    neighbours,
):
    del after_ref
    rows, width = seeds_ref.shape
    head = own_ref.shape[1]
    whole_ref[:, :head] = own_ref[...]
    chunks = (head // BLK, rows // BLK)
    fill_tiles(neighbours, column_ref, share_ref, whole_ref, spot_ref, 0, chunks)
    done = early_ref.shape[1]
    far_ref[:, :done] = early_ref[...]
    chunks = (done // BLK, far_ref.shape[1] // BLK)
    fill_tiles(neighbours, column_ref, share_ref, far_ref, spot_ref, rows, chunks)
    pick_ref[...] = picks(asked_ref[...], rows)
    for cols in pieces_of(0, far_ref.shape[1]):
        picked_far_ref[:, cols] = dot(pick_ref[...], far_ref[:, cols]).astype(jnp.bfloat16)
    for cols in pieces_of(0, rows):
        picked_ref[:, cols] = dot(pick_ref[...], whole_ref[:, cols]).astype(jnp.bfloat16)
    for cols in pieces_of(0, width):
        seeds = seeds_ref[:, cols]
        sent_base = KEEP * dot(picked_ref[...], seeds) + ANCHOR * dot(pick_ref[...], seeds)
        sent_base_ref[:, cols] = sent_base.astype(jnp.bfloat16)


def gather_kernel(*refs):
    *plane_refs, out_ref = refs
    half = plane_refs[0].shape[0] // 2
    for z, plane_ref in enumerate(plane_refs):
        out_ref[z * half : (z + 1) * half, :] = plane_ref[half:, :]


def pair_kernel(slots, *refs):
    count = GROUP // 2
    *plane_refs, other_ref = refs[:-count]
    planes = len(plane_refs)
    for q, out_ref in zip(pair_order(count), refs[-count:]):
        for z, plane_ref in enumerate(plane_refs):
            here = slice(z * slots, (z + 1) * slots)
            there = slice((planes + z) * slots, (planes + z + 1) * slots)
            other = (z * count + q) * slots
            out_ref[here, :] = plane_ref[q * slots : (q + 1) * slots, :]
            out_ref[there, :] = other_ref[other : other + slots, :]


def send_a_kernel(me_ref, tiles_ref, base_ref, *refs, slots):
    pair_refs = refs[: GROUP // 2]
    out_hbm, *plane_refs, received_ref, out_ref, sem = refs[GROUP // 2 :]
    me = me_ref[0]
    from_pairs(me, pair_refs, received_ref, slots)
    copy = push(received_ref, out_hbm, sem)
    for cols in pieces_of(0, received_ref.shape[1]):
        total = KEEP * dot(tiles_ref[...], received_ref[:, cols])
        out_ref[:, cols] = (total + base_ref[:, cols].astype(jnp.float32)).astype(jnp.bfloat16)
    to_planes(me, out_ref, plane_refs, slots)
    copy.wait()


def send_b_kernel(tiles_ref, base_ref, received_ref, after_ref, out_hbm, kept_hbm, out_ref, sems):
    del after_ref
    wide = base_ref.shape[1] - received_ref.shape[1]
    copies = [push(received_ref, kept_hbm, sems.at[0])]
    for i, rows in enumerate(strips_of(out_ref.shape[0])):
        total = KEEP * dot(tiles_ref[rows, :], received_ref[...])
        total = total + base_ref[rows, wide:].astype(jnp.float32)
        out_ref[rows, :] = total.astype(jnp.bfloat16)
        copies.append(push(out_ref.at[rows], out_hbm.at[rows], sems.at[1 + i]))
    for copy in copies:
        copy.wait()


def labels_kernel(
    own_ref,
    far_ref,
    seeds_ref,
    received_a_ref,
    received_b_ref,
    after_ref,
    next_ref,
    rest_ref,
    near_ref,
):
    del after_ref
    near_ref[...] = far_ref[...]
    wide = received_a_ref.shape[1]
    width = seeds_ref.shape[1]
    for cols in pieces_of(0, wide) + pieces_of(wide, width):
        first = cols.stop <= wide
        received = received_a_ref[:, cols] if first else received_b_ref[:, moved(cols, -wide)]
        seeds = ANCHOR * seeds_ref[:, cols].astype(jnp.float32)
        total = dot(own_ref[...], seeds_ref[:, cols]) + dot(far_ref[...], received)
        labels = (KEEP * total + seeds).astype(jnp.bfloat16)
        base = KEEP * dot(own_ref[...], labels) + seeds
        kept = base.astype(jnp.bfloat16)
        next_ref[:, cols] = kept
        rest = (base - kept.astype(jnp.float32)) * REST_SCALE
        rest_ref[:, cols] = rest.astype(jnp.float8_e4m3fn)


def result(tiles_ref, received, base_ref, rest_ref, rows, cols):
    total = KEEP * dot(tiles_ref[rows, :], received) + base_ref[rows, cols].astype(jnp.float32)
    total = total + rest_ref[rows, cols].astype(jnp.float32) * (1 / REST_SCALE)
    return total.astype(jnp.bfloat16)


def last_a_kernel(me_ref, tiles_ref, base_ref, rest_ref, *refs, slots):
    pair_refs = refs[: GROUP // 2]
    out_hbm, received_ref, out_ref, sems = refs[GROUP // 2 :]
    from_pairs(me_ref[0], pair_refs, received_ref, slots)
    copies = []
    for i, cols in enumerate(pieces_of(0, received_ref.shape[1])):
        received = received_ref[:, cols]
        out_ref[:, cols] = result(tiles_ref, received, base_ref, rest_ref, slice(None), cols)
        copies.append(push(out_ref.at[:, cols], out_hbm.at[:, cols], sems.at[i]))
    for copy in copies:
        copy.wait()


def last_b_kernel(tiles_ref, base_ref, rest_ref, received_ref, same_ref, out_hbm, out_ref, sems):
    del same_ref
    width = base_ref.shape[1]
    wide = width - received_ref.shape[1]
    copies = []
    cols = slice(wide, width)
    for i, rows in enumerate(strips_of(out_ref.shape[0])):
        out_ref[rows, :] = result(tiles_ref, received_ref[...], base_ref, rest_ref, rows, cols)
        copies.append(push(out_ref.at[rows], out_hbm.at[rows, cols], sems.at[i]))
    for copy in copies:
        copy.wait()


def swap(x, peers, distance):
    return lax.ppermute(x, "rows", [(i, i ^ distance(i)) for i in range(peers)])


def exchange(rows_out, peers):
    count, width = rows_out.shape
    sent = rows_out.reshape(peers, count // peers, width)
    got = lax.all_to_all(sent, "rows", split_axis=0, concat_axis=0, tiled=True)
    return got.reshape(count, width)


def across(planes, peers):
    order = plane_order(len(planes))
    far = lambda z: lambda i: GROUP * plane_of(z, len(planes), i)
    return [swap(x, peers, far(z)) if z else x for z, x in zip(order, planes)]


def within(planes, peers, slots):
    depth, wide = planes[0].shape
    n = len(planes)
    other = call(
        gather_kernel,
        "gather",
        jax.ShapeDtypeStruct((n * depth // 2, wide), jnp.bfloat16),
        [VMEM] * n,
        VMEM,
        flops=LONG,
    )(*planes)
    other = swap(other, peers, lambda i: 1)
    pairs = call(
        functools.partial(pair_kernel, slots),
        "pair",
        [jax.ShapeDtypeStruct((2 * n * slots, wide), jnp.bfloat16)] * (GROUP // 2),
        [VMEM] * (n + 1),
        [VMEM] * (GROUP // 2),
    )(*planes, other)
    return [swap(x, peers, lambda i, q=q: 2 * q) if q else x for q, x in zip(pair_order(len(pairs)), pairs)]


def on_device(seeds, neighbor_pos, edge_weight, tile_blocks, wanted):
    rows, width = seeds.shape
    peers, slots = wanted.shape[1:]
    count = peers * slots
    neighbours = neighbor_pos.shape[1]
    depth = -(-neighbours // PACK) * PACK
    planes = peers // GROUP
    wide = max(3 * width // 8 // BLK, 1) * BLK
    assert peers & (peers - 1) == 0 and peers >= GROUP
    head = rows - BLK
    me = lax.axis_index("rows").astype(jnp.int32).reshape(1)
    sems = pltpu.SemaphoreType.DMA
    bf16 = jnp.bfloat16
    plane_shape = jax.ShapeDtypeStruct((GROUP * slots, wide), bf16)
    n_a, n_out, n_sent = len(pieces_of(0, wide)), len(strips_of(rows)), len(strips_of(count))

    asked = lax.all_to_all(
        wanted.reshape(peers, 1, slots), "rows", split_axis=0, concat_axis=0, tiled=True
    )
    own, column, share, near_seeds = call(
        own_tiles_kernel,
        "own_tiles",
        [
            far_out((rows, head)),
            near_out((depth, rows), jnp.int32),
            near_out((depth, rows), jnp.float32),
            near_out((rows, width)),
        ],
        [SMEM, VMEM, VMEM, HBM],
        [HBM, VMEM, VMEM, VMEM],
        [
            pltpu.VMEM((rows, head), bf16),
            pltpu.VMEM((depth, rows), jnp.float32),
            sems((1 + head // BLK,)),
        ],
        flops=neighbours * rows * rows,
    )(far_in(tile_blocks), far_in(neighbor_pos.T), far_in(edge_weight.T), far_in(seeds))
    pick, *sent_planes = call(
        pick_a_kernel,
        "pick_a",
        [near_out((count, rows))] + [plane_shape] * planes,
        [SMEM, VMEM, VMEM, HBM],
        [VMEM] * (1 + planes),
        [pltpu.VMEM((count, wide), bf16)],
        flops=2 * count * rows * wide,
    )(me, asked, near_seeds, far_in(own))
    got_planes = across(sent_planes, peers)
    sent_b, early = call(
        functools.partial(pick_b_kernel, neighbours=neighbours),
        "pick_b",
        [
            far_out((count, width - wide)),
            near_out((rows, count // BLK * EARLY // 8 * BLK)),
        ],
        [VMEM] * 4,
        [HBM, VMEM],
        [
            pltpu.VMEM((count, width - wide), bf16),
            pltpu.VMEM((depth, rows), jnp.float32),
            sems((n_sent,)),
        ],
        flops=2 * count * rows * (width - wide),
    )(pick, near_seeds, column, share)
    received_b = exchange(sent_b, peers)
    got_pairs = within(got_planes, peers, slots)
    far, picked_far, sent_base, own = call(
        functools.partial(far_kernel, neighbours=neighbours),
        "far",
        [
            far_out((rows, count)),
            near_out((count, count)),
            near_out((count, width)),
            far_out((rows, rows)),
        ],
        [VMEM] * 6 + [ANY],
        [VMEM] * 4,
        [
            pltpu.VMEM((count, rows), bf16),
            pltpu.VMEM((count, rows), bf16),
            pltpu.VMEM((depth, rows), jnp.float32),
        ],
        flops=2 * rows * count * (count + rows + width) + neighbours * rows * count,
    )(
        asked,
        early,
        far_in(own),
        column,
        share,
        far_in(seeds),
        got_pairs[0],
    )
    received_a, *sent_planes = call(
        functools.partial(send_a_kernel, slots=slots),
        "send_a",
        [far_out((count, wide))] + [plane_shape] * planes,
        [SMEM] + [VMEM] * (2 + GROUP // 2),
        [HBM] + [VMEM] * planes,
        [pltpu.VMEM((count, wide), bf16), pltpu.VMEM((count, wide), bf16), sems],
        flops=2 * count * count * wide,
    )(me, picked_far, sent_base, *got_pairs)
    got_planes = across(sent_planes, peers)
    sent_b, received_b = call(
        send_b_kernel,
        "send_b",
        [far_out((count, width - wide)), far_out((count, width - wide))],
        [VMEM] * 3 + [ANY],
        [HBM, HBM],
        [pltpu.VMEM((count, width - wide), bf16), sems((1 + n_sent,))],
        flops=2 * count * count * (width - wide),
        nbytes=2 * count * (3 * (width - wide) + count + width),
    )(picked_far, sent_base, received_b, sent_planes[0])
    last_b = exchange(sent_b, peers)
    got_pairs = within(got_planes, peers, slots)
    next_base, rest, near_far = call(
        labels_kernel,
        "labels",
        [
            near_out((rows, width)),
            near_out((rows, width), jnp.float8_e4m3fn),
            near_out((rows, count)),
        ],
        [VMEM] * 5 + [ANY],
        [VMEM] * 3,
        flops=2 * rows * (count + 2 * rows) * width,
    )(
        far_in(own),
        far_in(far),
        far_in(seeds),
        far_in(received_a),
        far_in(received_b),
        got_pairs[0],
    )
    first = call(
        functools.partial(last_a_kernel, slots=slots),
        "last_a",
        far_out((rows, width)),
        [SMEM] + [VMEM] * (3 + GROUP // 2),
        HBM,
        [pltpu.VMEM((count, wide), bf16), pltpu.VMEM((rows, wide), bf16), sems((n_a,))],
        flops=2 * rows * count * wide,
    )(me, near_far, next_base, rest, *got_pairs)
    return call(
        last_b_kernel,
        "last_b",
        far_out((rows, width)),
        [VMEM] * 4 + [HBM],
        HBM,
        [pltpu.VMEM((rows, width - wide), bf16), sems((n_out,))],
        flops=2 * rows * count * (width - wide),
        nbytes=2 * rows * count + 5 * rows * width + 2 * count * width,
        aliases={4: 0},
    )(near_far, next_base, rest, last_b, far_in(first))


def solution(mesh):
    in_specs = (
        P(("parts", "rows"), "cls"),
        P(("parts", "rows"), None),
        P(("parts", "rows"), None),
        P(("parts", "rows"), None),
        P(("parts", "rows"), None, None),
    )
    out_specs = P(("parts", "rows"), "cls")
    return jax.shard_map(
        on_device, mesh=mesh, in_specs=in_specs, out_specs=out_specs, check_vma=False
    )
```

```python
import functools
import math

import jax
import jax.numpy as jnp
from jax import lax
from jax.experimental import pallas as pl
from jax.experimental.pallas import tpu as pltpu
from jax.sharding import PartitionSpec as P

BLK = 128
COLS = 256
GROUP = 8
PACK = 16
VMEM_LIMIT = 32 * 1024 * 1024
NEAR_BYTES = 1024 * 1024
KEEP = 0.85
ANCHOR = 0.15
REST_SCALE = 4096.0
LONG = 4 * 10**10
EARLY = 2

SMEM = pl.BlockSpec(memory_space=pltpu.SMEM)
VMEM = pl.BlockSpec(memory_space=pltpu.VMEM)
HBM = pl.BlockSpec(memory_space=pltpu.HBM)
ANY = pl.BlockSpec(memory_space=pl.ANY)


def far_out(shape, dtype=jnp.bfloat16):
    return pltpu.HBM(shape, dtype)


def far_in(x):
    return pltpu.with_memory_space_constraint(x, pltpu.HBM)


def near_out(shape, dtype=jnp.bfloat16):
    small = math.prod(shape) * jnp.dtype(dtype).itemsize <= NEAR_BYTES
    return pltpu.VMEM(shape, dtype) if small else jax.ShapeDtypeStruct(shape, dtype)


def call(kernel, name, out_shape, in_specs, out_specs, scratch_shapes=(), flops=0, nbytes=0, aliases=None):
    return pl.pallas_call(
        kernel,
        out_shape=out_shape,
        in_specs=in_specs,
        out_specs=out_specs,
        scratch_shapes=scratch_shapes,
        input_output_aliases=aliases or {},
        compiler_params=pltpu.CompilerParams(vmem_limit_bytes=VMEM_LIMIT),
        cost_estimate=pl.CostEstimate(flops=flops, bytes_accessed=nbytes, transcendentals=0),
        name=name,
    )


def dot(a, b):
    return jnp.dot(a, b, preferred_element_type=jnp.float32)


def pieces_of(first, last):
    return [slice(c, min(c + COLS, last)) for c in range(first, last, COLS)]


def strips_of(count):
    return [slice(r, r + BLK) for r in range(0, count, BLK)]


def moved(cols, by):
    return slice(cols.start + by, cols.stop + by)


def push(source, target, sem):
    copy = pltpu.make_async_copy(source, target, sem)
    copy.start()
    return copy


def picks(asked, rows):
    peers, _, slots = asked.shape
    count = peers * slots
    spread = jnp.broadcast_to(asked.astype(jnp.float32), (peers, slots, slots))
    spread = spread.reshape(count, slots)
    slot = lax.broadcasted_iota(jnp.int32, (count, slots), 0) % slots
    lane = lax.broadcasted_iota(jnp.int32, (count, slots), 1)
    row = jnp.sum(jnp.where(slot == lane, spread, 0.0), axis=1, keepdims=True)
    hits = lax.broadcasted_iota(jnp.int32, (count, rows), 1) == row.astype(jnp.int32)
    return hits.astype(jnp.float32).astype(jnp.bfloat16)


def block(peer, slots):
    return pl.ds(pl.multiple_of(peer * slots, slots), slots)


def pair_order(pairs):
    return [0] + list(range(pairs - 1, 0, -1))


def plane_order(planes):
    return [0] + list(range(2, planes)) + [1]


def pair_of(q, device):
    other = {3: 2, 2: 1, 1: 3}.get(q, q)
    return q + (device & 1) * (other - q)


def plane_of(z, planes, device):
    other = {1: 2, 2: 3, 3: 1}.get(z, z) if planes > 3 else z
    return z + (device & 1) * (other - z)


def to_planes(me, rows_ref, plane_refs, slots):
    for z, plane_ref in zip(plane_order(len(plane_refs)), plane_refs):
        for s in range(2):
            for q in range(GROUP // 2):
                peer = me ^ (GROUP * plane_of(z, len(plane_refs), me) + 2 * q + s)
                at = (s * (GROUP // 2) + q) * slots
                plane_ref[at : at + slots, :] = rows_ref[block(peer, slots), :]


def from_pairs(me, pair_refs, rows_ref, slots):
    planes = pair_refs[0].shape[0] // (2 * slots)
    for q, pair_ref in zip(pair_order(len(pair_refs)), pair_refs):
        for s in range(2):
            for i, z in enumerate(plane_order(planes)):
                holder = me ^ (2 * pair_of(q, me) + s)
                peer = holder ^ (GROUP * plane_of(z, planes, holder))
                at = (s * planes + i) * slots
                rows_ref[block(peer, slots), :] = pair_ref[at : at + slots, :]


def fill_edges(blocks_ref, pos_ref, weight_ref, column_ref, share_ref):
    block_count, tile_count = blocks_ref.shape
    neighbours = pos_ref.shape[0]
    column_ref[...] = jnp.full(column_ref.shape, -1, jnp.int32)
    share_ref[...] = jnp.zeros(share_ref.shape, jnp.float32)
    weights = weight_ref[...].astype(jnp.float32)
    share = weights / jnp.sum(weights, axis=0, keepdims=True)
    share_ref[:neighbours, :] = share.astype(jnp.bfloat16).astype(jnp.float32)
    for b in range(block_count):
        lanes = slice(b * BLK, (b + 1) * BLK)
        pos = pos_ref[:, lanes]
        tile = pos // BLK
        base = jnp.full(pos.shape, blocks_ref[b, 0], jnp.int32)
        for j in range(1, tile_count):
            base = jnp.where(tile == j, blocks_ref[b, j], base)
        column_ref[:neighbours, lanes] = base * BLK + pos % BLK


def fill_tiles(neighbours, column_ref, share_ref, tiles_ref, spot_ref, start, chunks):
    rows = column_ref.shape[1]
    sub = lax.broadcasted_iota(jnp.int32, (BLK, BLK), 0).astype(jnp.float32).astype(jnp.bfloat16)
    sub = sub.reshape(BLK // PACK, PACK, BLK)

    @pl.loop(*chunks)
    def _(chunk):
        first = pl.multiple_of(chunk * BLK, BLK)
        spot = column_ref[...] - (start + first)
        spot_ref[...] = jnp.where((spot >= 0) & (spot < BLK), spot, -1).astype(jnp.float32)

        @pl.loop(0, rows // BLK)
        def _(b):
            lanes = pl.ds(pl.multiple_of(b * BLK, BLK), BLK)
            row = lambda ref, k: jnp.broadcast_to(ref[k : k + 1, lanes], (PACK, BLK))
            total = jnp.zeros(sub.shape, jnp.bfloat16)
            for k in range(neighbours):
                spot = row(spot_ref, k).astype(jnp.bfloat16)
                share = row(share_ref, k).astype(jnp.bfloat16)
                total = jnp.where(sub == spot[None], share[None], total)
            tiles_ref[lanes, pl.ds(first, BLK)] = total.reshape(BLK, BLK).T


def own_tiles_kernel(
    blocks_ref,
    pos_ref,
    weight_ref,
    seeds_hbm,
    own_hbm,
    column_ref,
    share_ref,
    near_ref,
    own_ref,
    spot_ref,
    sems,
):
    copies = [push(seeds_hbm, near_ref, sems.at[0])]
    fill_edges(blocks_ref, pos_ref, weight_ref, column_ref, share_ref)
    for i in range(own_ref.shape[1] // BLK):
        cols = slice(i * BLK, (i + 1) * BLK)
        fill_tiles(pos_ref.shape[0], column_ref, share_ref, own_ref, spot_ref, 0, (i, i + 1))
        copies.append(push(own_ref.at[:, cols], own_hbm.at[:, cols], sems.at[1 + i]))
    for copy in copies:
        copy.wait()


def pick_a_kernel(me_ref, asked_ref, seeds_ref, after_ref, pick_ref, *refs):
    *plane_refs, a_ref = refs
    del after_ref
    pick_ref[...] = picks(asked_ref[...], seeds_ref.shape[0])
    for cols in pieces_of(0, a_ref.shape[1]):
        a_ref[:, cols] = dot(pick_ref[...], seeds_ref[:, cols]).astype(jnp.bfloat16)
    to_planes(me_ref[0], a_ref, plane_refs, asked_ref.shape[2])


def pick_b_kernel(
    pick_ref,
    seeds_ref,
    column_ref,
    share_ref,
    out_b,
    early_ref,
    b_ref,
    spot_ref,
    sems,
    *,
    neighbours,
):
    rows, width = seeds_ref.shape
    wide = width - b_ref.shape[1]
    copies = []
    for i, rows_here in enumerate(strips_of(pick_ref.shape[0])):
        b_ref[rows_here, :] = dot(pick_ref[rows_here, :], seeds_ref[:, wide:]).astype(jnp.bfloat16)
        copies.append(push(b_ref.at[rows_here], out_b.at[rows_here], sems.at[i]))
    chunks = (0, early_ref.shape[1] // BLK)
    fill_tiles(neighbours, column_ref, share_ref, early_ref, spot_ref, rows, chunks)
    for copy in copies:
        copy.wait()


def far_kernel(
    asked_ref,
    early_ref,
    own_ref,
    column_ref,
    share_ref,
    seeds_ref,
    after_ref,
    far_ref,
    picked_far_ref,
    sent_base_ref,
    whole_ref,
    pick_ref,
    picked_ref,
    spot_ref,
    *,
    neighbours,
):
    del after_ref
    rows, width = seeds_ref.shape
    head = own_ref.shape[1]
    whole_ref[:, :head] = own_ref[...]
    chunks = (head // BLK, rows // BLK)
    fill_tiles(neighbours, column_ref, share_ref, whole_ref, spot_ref, 0, chunks)
    done = early_ref.shape[1]
    far_ref[:, :done] = early_ref[...]
    chunks = (done // BLK, far_ref.shape[1] // BLK)
    fill_tiles(neighbours, column_ref, share_ref, far_ref, spot_ref, rows, chunks)
    pick_ref[...] = picks(asked_ref[...], rows)
    for cols in pieces_of(0, far_ref.shape[1]):
        picked_far_ref[:, cols] = dot(pick_ref[...], far_ref[:, cols]).astype(jnp.bfloat16)
    for cols in pieces_of(0, rows):
        picked_ref[:, cols] = dot(pick_ref[...], whole_ref[:, cols]).astype(jnp.bfloat16)
    for cols in pieces_of(0, width):
        seeds = seeds_ref[:, cols]
        sent_base = KEEP * dot(picked_ref[...], seeds) + ANCHOR * dot(pick_ref[...], seeds)
        sent_base_ref[:, cols] = sent_base.astype(jnp.bfloat16)


def gather_kernel(*refs):
    *plane_refs, out_ref = refs
    half = plane_refs[0].shape[0] // 2
    for z, plane_ref in enumerate(plane_refs):
        out_ref[z * half : (z + 1) * half, :] = plane_ref[half:, :]


def pair_kernel(slots, me_ref, *refs):
    count = GROUP // 2
    *plane_refs, other_ref = refs[:-count]
    planes = len(plane_refs)
    for q, out_ref in zip(pair_order(count), refs[-count:]):
        q = pair_of(q, me_ref[0])
        for z, plane_ref in enumerate(plane_refs):
            here = slice(z * slots, (z + 1) * slots)
            there = slice((planes + z) * slots, (planes + z + 1) * slots)
            out_ref[here, :] = plane_ref[block(q, slots), :]
            out_ref[there, :] = other_ref[block(z * count + q, slots), :]


def send_a_kernel(me_ref, tiles_ref, base_ref, *refs, slots):
    pair_refs = refs[: GROUP // 2]
    out_hbm, *plane_refs, received_ref, out_ref, sem = refs[GROUP // 2 :]
    me = me_ref[0]
    from_pairs(me, pair_refs, received_ref, slots)
    copy = push(received_ref, out_hbm, sem)
    for cols in pieces_of(0, received_ref.shape[1]):
        total = KEEP * dot(tiles_ref[...], received_ref[:, cols])
        out_ref[:, cols] = (total + base_ref[:, cols].astype(jnp.float32)).astype(jnp.bfloat16)
    to_planes(me, out_ref, plane_refs, slots)
    copy.wait()


def send_b_kernel(tiles_ref, base_ref, received_ref, after_ref, out_hbm, kept_hbm, out_ref, sems):
    del after_ref
    wide = base_ref.shape[1] - received_ref.shape[1]
    copies = [push(received_ref, kept_hbm, sems.at[0])]
    for i, rows in enumerate(strips_of(out_ref.shape[0])):
        total = KEEP * dot(tiles_ref[rows, :], received_ref[...])
        total = total + base_ref[rows, wide:].astype(jnp.float32)
        out_ref[rows, :] = total.astype(jnp.bfloat16)
        copies.append(push(out_ref.at[rows], out_hbm.at[rows], sems.at[1 + i]))
    for copy in copies:
        copy.wait()


def labels_kernel(
    own_ref,
    far_ref,
    seeds_ref,
    received_a_ref,
    received_b_ref,
    after_ref,
    next_ref,
    rest_ref,
    near_ref,
):
    del after_ref
    near_ref[...] = far_ref[...]
    wide = received_a_ref.shape[1]
    width = seeds_ref.shape[1]
    for cols in pieces_of(0, wide) + pieces_of(wide, width):
        first = cols.stop <= wide
        received = received_a_ref[:, cols] if first else received_b_ref[:, moved(cols, -wide)]
        seeds = ANCHOR * seeds_ref[:, cols].astype(jnp.float32)
        total = dot(own_ref[...], seeds_ref[:, cols]) + dot(far_ref[...], received)
        labels = (KEEP * total + seeds).astype(jnp.bfloat16)
        base = KEEP * dot(own_ref[...], labels) + seeds
        kept = base.astype(jnp.bfloat16)
        next_ref[:, cols] = kept
        rest = (base - kept.astype(jnp.float32)) * REST_SCALE
        rest_ref[:, cols] = rest.astype(jnp.float8_e4m3fn)


def result(tiles_ref, received, base_ref, rest_ref, rows, cols):
    total = KEEP * dot(tiles_ref[rows, :], received) + base_ref[rows, cols].astype(jnp.float32)
    total = total + rest_ref[rows, cols].astype(jnp.float32) * (1 / REST_SCALE)
    return total.astype(jnp.bfloat16)


def last_a_kernel(me_ref, tiles_ref, base_ref, rest_ref, *refs, slots):
    pair_refs = refs[: GROUP // 2]
    out_hbm, received_ref, out_ref, sems = refs[GROUP // 2 :]
    from_pairs(me_ref[0], pair_refs, received_ref, slots)
    copies = []
    for i, cols in enumerate(pieces_of(0, received_ref.shape[1])):
        received = received_ref[:, cols]
        out_ref[:, cols] = result(tiles_ref, received, base_ref, rest_ref, slice(None), cols)
        copies.append(push(out_ref.at[:, cols], out_hbm.at[:, cols], sems.at[i]))
    for copy in copies:
        copy.wait()


def last_b_kernel(tiles_ref, base_ref, rest_ref, received_ref, same_ref, out_hbm, out_ref, sems):
    del same_ref
    width = base_ref.shape[1]
    wide = width - received_ref.shape[1]
    copies = []
    cols = slice(wide, width)
    for i, rows in enumerate(strips_of(out_ref.shape[0])):
        out_ref[rows, :] = result(tiles_ref, received_ref[...], base_ref, rest_ref, rows, cols)
        copies.append(push(out_ref.at[rows], out_hbm.at[rows, cols], sems.at[i]))
    for copy in copies:
        copy.wait()


def swap(x, peers, distance):
    return lax.ppermute(x, "rows", [(i, i ^ distance(i)) for i in range(peers)])


def exchange(rows_out, peers):
    count, width = rows_out.shape
    sent = rows_out.reshape(peers, count // peers, width)
    got = lax.all_to_all(sent, "rows", split_axis=0, concat_axis=0, tiled=True)
    return got.reshape(count, width)


def across(planes, peers):
    order = plane_order(len(planes))
    far = lambda z: lambda i: GROUP * plane_of(z, len(planes), i)
    return [swap(x, peers, far(z)) if z else x for z, x in zip(order, planes)]


def within(me, planes, peers, slots):
    depth, wide = planes[0].shape
    n = len(planes)
    other = call(
        gather_kernel,
        "gather",
        jax.ShapeDtypeStruct((n * depth // 2, wide), jnp.bfloat16),
        [VMEM] * n,
        VMEM,
        flops=LONG,
    )(*planes)
    other = swap(other, peers, lambda i: 1)
    pairs = call(
        functools.partial(pair_kernel, slots),
        "pair",
        [jax.ShapeDtypeStruct((2 * n * slots, wide), jnp.bfloat16)] * (GROUP // 2),
        [SMEM] + [VMEM] * (n + 1),
        [VMEM] * (GROUP // 2),
    )(me, *planes, other)
    even = lambda q: lambda i: 2 * pair_of(q, i)
    return [swap(x, peers, even(q)) if q else x for q, x in zip(pair_order(len(pairs)), pairs)]


def on_device(seeds, neighbor_pos, edge_weight, tile_blocks, wanted):
    rows, width = seeds.shape
    peers, slots = wanted.shape[1:]
    count = peers * slots
    neighbours = neighbor_pos.shape[1]
    depth = -(-neighbours // PACK) * PACK
    planes = peers // GROUP
    wide = max(3 * width // 8 // BLK, 1) * BLK
    assert peers & (peers - 1) == 0 and peers >= GROUP
    head = rows - BLK
    me = lax.axis_index("rows").astype(jnp.int32).reshape(1)
    sems = pltpu.SemaphoreType.DMA
    bf16 = jnp.bfloat16
    plane_shape = jax.ShapeDtypeStruct((GROUP * slots, wide), bf16)
    n_a, n_out, n_sent = len(pieces_of(0, wide)), len(strips_of(rows)), len(strips_of(count))

    asked = lax.all_to_all(
        wanted.reshape(peers, 1, slots), "rows", split_axis=0, concat_axis=0, tiled=True
    )
    own, column, share, near_seeds = call(
        own_tiles_kernel,
        "own_tiles",
        [
            far_out((rows, head)),
            near_out((depth, rows), jnp.int32),
            near_out((depth, rows), jnp.float32),
            near_out((rows, width)),
        ],
        [SMEM, VMEM, VMEM, HBM],
        [HBM, VMEM, VMEM, VMEM],
        [
            pltpu.VMEM((rows, head), bf16),
            pltpu.VMEM((depth, rows), jnp.float32),
            sems((1 + head // BLK,)),
        ],
        flops=neighbours * rows * rows,
    )(far_in(tile_blocks), far_in(neighbor_pos.T), far_in(edge_weight.T), far_in(seeds))
    pick, *sent_planes = call(
        pick_a_kernel,
        "pick_a",
        [near_out((count, rows))] + [plane_shape] * planes,
        [SMEM, VMEM, VMEM, HBM],
        [VMEM] * (1 + planes),
        [pltpu.VMEM((count, wide), bf16)],
        flops=2 * count * rows * wide,
    )(me, asked, near_seeds, far_in(own))
    got_planes = across(sent_planes, peers)
    sent_b, early = call(
        functools.partial(pick_b_kernel, neighbours=neighbours),
        "pick_b",
        [
            far_out((count, width - wide)),
            near_out((rows, count // BLK * EARLY // 8 * BLK)),
        ],
        [VMEM] * 4,
        [HBM, VMEM],
        [
            pltpu.VMEM((count, width - wide), bf16),
            pltpu.VMEM((depth, rows), jnp.float32),
            sems((n_sent,)),
        ],
        flops=2 * count * rows * (width - wide),
    )(pick, near_seeds, column, share)
    received_b = exchange(sent_b, peers)
    got_pairs = within(me, got_planes, peers, slots)
    far, picked_far, sent_base, own = call(
        functools.partial(far_kernel, neighbours=neighbours),
        "far",
        [
            far_out((rows, count)),
            near_out((count, count)),
            near_out((count, width)),
            far_out((rows, rows)),
        ],
        [VMEM] * 6 + [ANY],
        [VMEM] * 4,
        [
            pltpu.VMEM((count, rows), bf16),
            pltpu.VMEM((count, rows), bf16),
            pltpu.VMEM((depth, rows), jnp.float32),
        ],
        flops=2 * rows * count * (count + rows + width) + neighbours * rows * count,
    )(
        asked,
        early,
        far_in(own),
        column,
        share,
        far_in(seeds),
        got_pairs[0],
    )
    received_a, *sent_planes = call(
        functools.partial(send_a_kernel, slots=slots),
        "send_a",
        [far_out((count, wide))] + [plane_shape] * planes,
        [SMEM] + [VMEM] * (2 + GROUP // 2),
        [HBM] + [VMEM] * planes,
        [pltpu.VMEM((count, wide), bf16), pltpu.VMEM((count, wide), bf16), sems],
        flops=2 * count * count * wide,
    )(me, picked_far, sent_base, *got_pairs)
    got_planes = across(sent_planes, peers)
    sent_b, received_b = call(
        send_b_kernel,
        "send_b",
        [far_out((count, width - wide)), far_out((count, width - wide))],
        [VMEM] * 3 + [ANY],
        [HBM, HBM],
        [pltpu.VMEM((count, width - wide), bf16), sems((1 + n_sent,))],
        flops=2 * count * count * (width - wide),
        nbytes=2 * count * (3 * (width - wide) + count + width),
    )(picked_far, sent_base, received_b, sent_planes[0])
    last_b = exchange(sent_b, peers)
    got_pairs = within(me, got_planes, peers, slots)
    next_base, rest, near_far = call(
        labels_kernel,
        "labels",
        [
            near_out((rows, width)),
            near_out((rows, width), jnp.float8_e4m3fn),
            near_out((rows, count)),
        ],
        [VMEM] * 5 + [ANY],
        [VMEM] * 3,
        flops=2 * rows * (count + 2 * rows) * width,
    )(
        far_in(own),
        far_in(far),
        far_in(seeds),
        far_in(received_a),
        far_in(received_b),
        got_pairs[0],
    )
    first = call(
        functools.partial(last_a_kernel, slots=slots),
        "last_a",
        far_out((rows, width)),
        [SMEM] + [VMEM] * (3 + GROUP // 2),
        HBM,
        [pltpu.VMEM((count, wide), bf16), pltpu.VMEM((rows, wide), bf16), sems((n_a,))],
        flops=2 * rows * count * wide,
    )(me, near_far, next_base, rest, *got_pairs)
    return call(
        last_b_kernel,
        "last_b",
        far_out((rows, width)),
        [VMEM] * 4 + [HBM],
        HBM,
        [pltpu.VMEM((rows, width - wide), bf16), sems((n_out,))],
        flops=2 * rows * count * (width - wide),
        nbytes=2 * rows * count + 5 * rows * width + 2 * count * width,
        aliases={4: 0},
    )(near_far, next_base, rest, last_b, far_in(first))


def solution(mesh):
    in_specs = (
        P(("parts", "rows"), "cls"),
        P(("parts", "rows"), None),
        P(("parts", "rows"), None),
        P(("parts", "rows"), None),
        P(("parts", "rows"), None, None),
    )
    out_specs = P(("parts", "rows"), "cls")
    return jax.shard_map(
        on_device, mesh=mesh, in_specs=in_specs, out_specs=out_specs, check_vma=False
    )
```

```python
import functools
import math

import jax
import jax.numpy as jnp
from jax import lax
from jax.experimental import pallas as pl
from jax.experimental.pallas import tpu as pltpu
from jax.sharding import PartitionSpec as P

BLK = 128
COLS = 256
GROUP = 8
PACK = 16
VMEM_LIMIT = 32 * 1024 * 1024
NEAR_BYTES = 1024 * 1024
KEEP = 0.85
ANCHOR = 0.15
REST_SCALE = 4096.0
LONG = 4 * 10**10
EARLY = 2

SMEM = pl.BlockSpec(memory_space=pltpu.SMEM)
VMEM = pl.BlockSpec(memory_space=pltpu.VMEM)
HBM = pl.BlockSpec(memory_space=pltpu.HBM)
ANY = pl.BlockSpec(memory_space=pl.ANY)


def far_out(shape, dtype=jnp.bfloat16):
    return pltpu.HBM(shape, dtype)


def far_in(x):
    return pltpu.with_memory_space_constraint(x, pltpu.HBM)


def near_out(shape, dtype=jnp.bfloat16):
    small = math.prod(shape) * jnp.dtype(dtype).itemsize <= NEAR_BYTES
    return pltpu.VMEM(shape, dtype) if small else jax.ShapeDtypeStruct(shape, dtype)


def call(kernel, name, out_shape, in_specs, out_specs, scratch_shapes=(), flops=0, nbytes=0, aliases=None):
    return pl.pallas_call(
        kernel,
        out_shape=out_shape,
        in_specs=in_specs,
        out_specs=out_specs,
        scratch_shapes=scratch_shapes,
        input_output_aliases=aliases or {},
        compiler_params=pltpu.CompilerParams(vmem_limit_bytes=VMEM_LIMIT),
        cost_estimate=pl.CostEstimate(flops=flops, bytes_accessed=nbytes, transcendentals=0),
        name=name,
    )


def dot(a, b):
    return jnp.dot(a, b, preferred_element_type=jnp.float32)


def pieces_of(first, last):
    return [slice(c, min(c + COLS, last)) for c in range(first, last, COLS)]


def strips_of(count):
    return [slice(r, r + BLK) for r in range(0, count, BLK)]


def moved(cols, by):
    return slice(cols.start + by, cols.stop + by)


def push(source, target, sem):
    copy = pltpu.make_async_copy(source, target, sem)
    copy.start()
    return copy


def picks(asked, rows):
    peers, _, slots = asked.shape
    count = peers * slots
    spread = jnp.broadcast_to(asked.astype(jnp.float32), (peers, slots, slots))
    spread = spread.reshape(count, slots)
    slot = lax.broadcasted_iota(jnp.int32, (count, slots), 0) % slots
    lane = lax.broadcasted_iota(jnp.int32, (count, slots), 1)
    row = jnp.sum(jnp.where(slot == lane, spread, 0.0), axis=1, keepdims=True)
    hits = lax.broadcasted_iota(jnp.int32, (count, rows), 1) == row.astype(jnp.int32)
    return hits.astype(jnp.float32).astype(jnp.bfloat16)


def block(peer, slots):
    return pl.ds(pl.multiple_of(peer * slots, slots), slots)


def pair_order(pairs):
    return [0] + list(range(pairs - 1, 0, -1))


def plane_order(planes):
    return [0] + list(range(2, planes)) + [1]


def pair_of(q, device):
    other = {3: 2, 2: 1, 1: 3}.get(q, q)
    return q + (device & 1) * (other - q)


def plane_of(z, planes, device):
    other = {2: 3, 3: 2}.get(z, z) if planes > 3 else z
    return z + (device & 1) * (other - z)


def to_planes(me, rows_ref, plane_refs, slots):
    for z, plane_ref in zip(plane_order(len(plane_refs)), plane_refs):
        for s in range(2):
            for q in range(GROUP // 2):
                peer = me ^ (GROUP * plane_of(z, len(plane_refs), me) + 2 * q + s)
                at = (s * (GROUP // 2) + q) * slots
                plane_ref[at : at + slots, :] = rows_ref[block(peer, slots), :]


def from_pairs(me, pair_refs, rows_ref, slots):
    planes = pair_refs[0].shape[0] // (2 * slots)
    for q, pair_ref in zip(pair_order(len(pair_refs)), pair_refs):
        for s in range(2):
            for i, z in enumerate(plane_order(planes)):
                holder = me ^ (2 * pair_of(q, me) + s)
                peer = holder ^ (GROUP * plane_of(z, planes, holder))
                at = (s * planes + i) * slots
                rows_ref[block(peer, slots), :] = pair_ref[at : at + slots, :]


def fill_edges(blocks_ref, pos_ref, weight_ref, column_ref, share_ref):
    block_count, tile_count = blocks_ref.shape
    neighbours = pos_ref.shape[0]
    column_ref[...] = jnp.full(column_ref.shape, -1, jnp.int32)
    share_ref[...] = jnp.zeros(share_ref.shape, jnp.float32)
    weights = weight_ref[...].astype(jnp.float32)
    share = weights / jnp.sum(weights, axis=0, keepdims=True)
    share_ref[:neighbours, :] = share.astype(jnp.bfloat16).astype(jnp.float32)
    for b in range(block_count):
        lanes = slice(b * BLK, (b + 1) * BLK)
        pos = pos_ref[:, lanes]
        tile = pos // BLK
        base = jnp.full(pos.shape, blocks_ref[b, 0], jnp.int32)
        for j in range(1, tile_count):
            base = jnp.where(tile == j, blocks_ref[b, j], base)
        column_ref[:neighbours, lanes] = base * BLK + pos % BLK


def fill_tiles(neighbours, column_ref, share_ref, tiles_ref, spot_ref, start, chunks):
    rows = column_ref.shape[1]
    sub = lax.broadcasted_iota(jnp.int32, (BLK, BLK), 0).astype(jnp.float32).astype(jnp.bfloat16)
    sub = sub.reshape(BLK // PACK, PACK, BLK)

    @pl.loop(*chunks)
    def _(chunk):
        first = pl.multiple_of(chunk * BLK, BLK)
        spot = column_ref[...] - (start + first)
        spot_ref[...] = jnp.where((spot >= 0) & (spot < BLK), spot, -1).astype(jnp.float32)

        @pl.loop(0, rows // BLK)
        def _(b):
            lanes = pl.ds(pl.multiple_of(b * BLK, BLK), BLK)
            row = lambda ref, k: jnp.broadcast_to(ref[k : k + 1, lanes], (PACK, BLK))
            total = jnp.zeros(sub.shape, jnp.bfloat16)
            for k in range(neighbours):
                spot = row(spot_ref, k).astype(jnp.bfloat16)
                share = row(share_ref, k).astype(jnp.bfloat16)
                total = jnp.where(sub == spot[None], share[None], total)
            tiles_ref[lanes, pl.ds(first, BLK)] = total.reshape(BLK, BLK).T


def own_tiles_kernel(
    blocks_ref,
    pos_ref,
    weight_ref,
    seeds_hbm,
    own_hbm,
    column_ref,
    share_ref,
    near_ref,
    own_ref,
    spot_ref,
    sems,
):
    copies = [push(seeds_hbm, near_ref, sems.at[0])]
    fill_edges(blocks_ref, pos_ref, weight_ref, column_ref, share_ref)
    for i in range(own_ref.shape[1] // BLK):
        cols = slice(i * BLK, (i + 1) * BLK)
        fill_tiles(pos_ref.shape[0], column_ref, share_ref, own_ref, spot_ref, 0, (i, i + 1))
        copies.append(push(own_ref.at[:, cols], own_hbm.at[:, cols], sems.at[1 + i]))
    for copy in copies:
        copy.wait()


def pick_a_kernel(me_ref, asked_ref, seeds_ref, after_ref, pick_ref, *refs):
    *plane_refs, a_ref = refs
    del after_ref
    pick_ref[...] = picks(asked_ref[...], seeds_ref.shape[0])
    for cols in pieces_of(0, a_ref.shape[1]):
        a_ref[:, cols] = dot(pick_ref[...], seeds_ref[:, cols]).astype(jnp.bfloat16)
    to_planes(me_ref[0], a_ref, plane_refs, asked_ref.shape[2])


def pick_b_kernel(
    pick_ref,
    seeds_ref,
    column_ref,
    share_ref,
    out_b,
    early_ref,
    b_ref,
    spot_ref,
    sems,
    *,
    neighbours,
):
    rows, width = seeds_ref.shape
    wide = width - b_ref.shape[1]
    copies = []
    for i, rows_here in enumerate(strips_of(pick_ref.shape[0])):
        b_ref[rows_here, :] = dot(pick_ref[rows_here, :], seeds_ref[:, wide:]).astype(jnp.bfloat16)
        copies.append(push(b_ref.at[rows_here], out_b.at[rows_here], sems.at[i]))
    chunks = (0, early_ref.shape[1] // BLK)
    fill_tiles(neighbours, column_ref, share_ref, early_ref, spot_ref, rows, chunks)
    for copy in copies:
        copy.wait()


def far_kernel(
    asked_ref,
    early_ref,
    own_ref,
    column_ref,
    share_ref,
    seeds_ref,
    after_ref,
    far_ref,
    picked_far_ref,
    sent_base_ref,
    whole_ref,
    pick_ref,
    picked_ref,
    spot_ref,
    *,
    neighbours,
):
    del after_ref
    rows, width = seeds_ref.shape
    head = own_ref.shape[1]
    whole_ref[:, :head] = own_ref[...]
    chunks = (head // BLK, rows // BLK)
    fill_tiles(neighbours, column_ref, share_ref, whole_ref, spot_ref, 0, chunks)
    done = early_ref.shape[1]
    far_ref[:, :done] = early_ref[...]
    chunks = (done // BLK, far_ref.shape[1] // BLK)
    fill_tiles(neighbours, column_ref, share_ref, far_ref, spot_ref, rows, chunks)
    pick_ref[...] = picks(asked_ref[...], rows)
    for cols in pieces_of(0, far_ref.shape[1]):
        picked_far_ref[:, cols] = dot(pick_ref[...], far_ref[:, cols]).astype(jnp.bfloat16)
    for cols in pieces_of(0, rows):
        picked_ref[:, cols] = dot(pick_ref[...], whole_ref[:, cols]).astype(jnp.bfloat16)
    for cols in pieces_of(0, width):
        seeds = seeds_ref[:, cols]
        sent_base = KEEP * dot(picked_ref[...], seeds) + ANCHOR * dot(pick_ref[...], seeds)
        sent_base_ref[:, cols] = sent_base.astype(jnp.bfloat16)


def gather_kernel(*refs):
    *plane_refs, out_ref = refs
    half = plane_refs[0].shape[0] // 2
    for z, plane_ref in enumerate(plane_refs):
        out_ref[z * half : (z + 1) * half, :] = plane_ref[half:, :]


def pair_kernel(slots, me_ref, *refs):
    count = GROUP // 2
    *plane_refs, other_ref = refs[:-count]
    planes = len(plane_refs)
    for q, out_ref in zip(pair_order(count), refs[-count:]):
        q = pair_of(q, me_ref[0])
        for z, plane_ref in enumerate(plane_refs):
            here = slice(z * slots, (z + 1) * slots)
            there = slice((planes + z) * slots, (planes + z + 1) * slots)
            out_ref[here, :] = plane_ref[block(q, slots), :]
            out_ref[there, :] = other_ref[block(z * count + q, slots), :]


def send_a_kernel(me_ref, tiles_ref, base_ref, *refs, slots):
    pair_refs = refs[: GROUP // 2]
    out_hbm, *plane_refs, received_ref, out_ref, sem = refs[GROUP // 2 :]
    me = me_ref[0]
    from_pairs(me, pair_refs, received_ref, slots)
    copy = push(received_ref, out_hbm, sem)
    for cols in pieces_of(0, received_ref.shape[1]):
        total = KEEP * dot(tiles_ref[...], received_ref[:, cols])
        out_ref[:, cols] = (total + base_ref[:, cols].astype(jnp.float32)).astype(jnp.bfloat16)
    to_planes(me, out_ref, plane_refs, slots)
    copy.wait()


def send_b_kernel(tiles_ref, base_ref, received_ref, after_ref, out_hbm, kept_hbm, out_ref, sems):
    del after_ref
    wide = base_ref.shape[1] - received_ref.shape[1]
    copies = [push(received_ref, kept_hbm, sems.at[0])]
    for i, rows in enumerate(strips_of(out_ref.shape[0])):
        total = KEEP * dot(tiles_ref[rows, :], received_ref[...])
        total = total + base_ref[rows, wide:].astype(jnp.float32)
        out_ref[rows, :] = total.astype(jnp.bfloat16)
        copies.append(push(out_ref.at[rows], out_hbm.at[rows], sems.at[1 + i]))
    for copy in copies:
        copy.wait()


def labels_kernel(
    own_ref,
    far_ref,
    seeds_ref,
    received_a_ref,
    received_b_ref,
    after_ref,
    next_ref,
    rest_ref,
    near_ref,
):
    del after_ref
    near_ref[...] = far_ref[...]
    wide = received_a_ref.shape[1]
    width = seeds_ref.shape[1]
    for cols in pieces_of(0, wide) + pieces_of(wide, width):
        first = cols.stop <= wide
        received = received_a_ref[:, cols] if first else received_b_ref[:, moved(cols, -wide)]
        seeds = ANCHOR * seeds_ref[:, cols].astype(jnp.float32)
        total = dot(own_ref[...], seeds_ref[:, cols]) + dot(far_ref[...], received)
        labels = (KEEP * total + seeds).astype(jnp.bfloat16)
        base = KEEP * dot(own_ref[...], labels) + seeds
        kept = base.astype(jnp.bfloat16)
        next_ref[:, cols] = kept
        rest = (base - kept.astype(jnp.float32)) * REST_SCALE
        rest_ref[:, cols] = rest.astype(jnp.float8_e4m3fn)


def result(tiles_ref, received, base_ref, rest_ref, rows, cols):
    total = KEEP * dot(tiles_ref[rows, :], received) + base_ref[rows, cols].astype(jnp.float32)
    total = total + rest_ref[rows, cols].astype(jnp.float32) * (1 / REST_SCALE)
    return total.astype(jnp.bfloat16)


def last_a_kernel(me_ref, tiles_ref, base_ref, rest_ref, *refs, slots):
    pair_refs = refs[: GROUP // 2]
    out_hbm, received_ref, out_ref, sems = refs[GROUP // 2 :]
    from_pairs(me_ref[0], pair_refs, received_ref, slots)
    copies = []
    for i, cols in enumerate(pieces_of(0, received_ref.shape[1])):
        received = received_ref[:, cols]
        out_ref[:, cols] = result(tiles_ref, received, base_ref, rest_ref, slice(None), cols)
        copies.append(push(out_ref.at[:, cols], out_hbm.at[:, cols], sems.at[i]))
    for copy in copies:
        copy.wait()


def last_b_kernel(tiles_ref, base_ref, rest_ref, received_ref, same_ref, out_hbm, out_ref, sems):
    del same_ref
    width = base_ref.shape[1]
    wide = width - received_ref.shape[1]
    copies = []
    cols = slice(wide, width)
    for i, rows in enumerate(strips_of(out_ref.shape[0])):
        out_ref[rows, :] = result(tiles_ref, received_ref[...], base_ref, rest_ref, rows, cols)
        copies.append(push(out_ref.at[rows], out_hbm.at[rows, cols], sems.at[i]))
    for copy in copies:
        copy.wait()


def swap(x, peers, distance):
    return lax.ppermute(x, "rows", [(i, i ^ distance(i)) for i in range(peers)])


def exchange(rows_out, peers):
    count, width = rows_out.shape
    sent = rows_out.reshape(peers, count // peers, width)
    got = lax.all_to_all(sent, "rows", split_axis=0, concat_axis=0, tiled=True)
    return got.reshape(count, width)


def across(planes, peers):
    order = plane_order(len(planes))
    far = lambda z: lambda i: GROUP * plane_of(z, len(planes), i)
    return [swap(x, peers, far(z)) if z else x for z, x in zip(order, planes)]


def within(me, planes, peers, slots):
    depth, wide = planes[0].shape
    n = len(planes)
    other = call(
        gather_kernel,
        "gather",
        jax.ShapeDtypeStruct((n * depth // 2, wide), jnp.bfloat16),
        [VMEM] * n,
        VMEM,
        flops=LONG,
    )(*planes)
    other = swap(other, peers, lambda i: 1)
    pairs = call(
        functools.partial(pair_kernel, slots),
        "pair",
        [jax.ShapeDtypeStruct((2 * n * slots, wide), jnp.bfloat16)] * (GROUP // 2),
        [SMEM] + [VMEM] * (n + 1),
        [VMEM] * (GROUP // 2),
    )(me, *planes, other)
    even = lambda q: lambda i: 2 * pair_of(q, i)
    return [swap(x, peers, even(q)) if q else x for q, x in zip(pair_order(len(pairs)), pairs)]


def on_device(seeds, neighbor_pos, edge_weight, tile_blocks, wanted):
    rows, width = seeds.shape
    peers, slots = wanted.shape[1:]
    count = peers * slots
    neighbours = neighbor_pos.shape[1]
    depth = -(-neighbours // PACK) * PACK
    planes = peers // GROUP
    wide = max(3 * width // 8 // BLK, 1) * BLK
    assert peers & (peers - 1) == 0 and peers >= GROUP
    head = rows - BLK
    me = lax.axis_index("rows").astype(jnp.int32).reshape(1)
    sems = pltpu.SemaphoreType.DMA
    bf16 = jnp.bfloat16
    plane_shape = jax.ShapeDtypeStruct((GROUP * slots, wide), bf16)
    n_a, n_out, n_sent = len(pieces_of(0, wide)), len(strips_of(rows)), len(strips_of(count))

    asked = lax.all_to_all(
        wanted.reshape(peers, 1, slots), "rows", split_axis=0, concat_axis=0, tiled=True
    )
    own, column, share, near_seeds = call(
        own_tiles_kernel,
        "own_tiles",
        [
            far_out((rows, head)),
            near_out((depth, rows), jnp.int32),
            near_out((depth, rows), jnp.float32),
            near_out((rows, width)),
        ],
        [SMEM, VMEM, VMEM, HBM],
        [HBM, VMEM, VMEM, VMEM],
        [
            pltpu.VMEM((rows, head), bf16),
            pltpu.VMEM((depth, rows), jnp.float32),
            sems((1 + head // BLK,)),
        ],
        flops=neighbours * rows * rows,
    )(far_in(tile_blocks), far_in(neighbor_pos.T), far_in(edge_weight.T), far_in(seeds))
    pick, *sent_planes = call(
        pick_a_kernel,
        "pick_a",
        [near_out((count, rows))] + [plane_shape] * planes,
        [SMEM, VMEM, VMEM, HBM],
        [VMEM] * (1 + planes),
        [pltpu.VMEM((count, wide), bf16)],
        flops=2 * count * rows * wide,
    )(me, asked, near_seeds, far_in(own))
    got_planes = across(sent_planes, peers)
    sent_b, early = call(
        functools.partial(pick_b_kernel, neighbours=neighbours),
        "pick_b",
        [
            far_out((count, width - wide)),
            near_out((rows, count // BLK * EARLY // 8 * BLK)),
        ],
        [VMEM] * 4,
        [HBM, VMEM],
        [
            pltpu.VMEM((count, width - wide), bf16),
            pltpu.VMEM((depth, rows), jnp.float32),
            sems((n_sent,)),
        ],
        flops=2 * count * rows * (width - wide),
    )(pick, near_seeds, column, share)
    received_b = exchange(sent_b, peers)
    got_pairs = within(me, got_planes, peers, slots)
    far, picked_far, sent_base, own = call(
        functools.partial(far_kernel, neighbours=neighbours),
        "far",
        [
            far_out((rows, count)),
            near_out((count, count)),
            near_out((count, width)),
            far_out((rows, rows)),
        ],
        [VMEM] * 6 + [ANY],
        [VMEM] * 4,
        [
            pltpu.VMEM((count, rows), bf16),
            pltpu.VMEM((count, rows), bf16),
            pltpu.VMEM((depth, rows), jnp.float32),
        ],
        flops=2 * rows * count * (count + rows + width) + neighbours * rows * count,
    )(
        asked,
        early,
        far_in(own),
        column,
        share,
        far_in(seeds),
        got_pairs[0],
    )
    received_a, *sent_planes = call(
        functools.partial(send_a_kernel, slots=slots),
        "send_a",
        [far_out((count, wide))] + [plane_shape] * planes,
        [SMEM] + [VMEM] * (2 + GROUP // 2),
        [HBM] + [VMEM] * planes,
        [pltpu.VMEM((count, wide), bf16), pltpu.VMEM((count, wide), bf16), sems],
        flops=2 * count * count * wide,
    )(me, picked_far, sent_base, *got_pairs)
    got_planes = across(sent_planes, peers)
    sent_b, received_b = call(
        send_b_kernel,
        "send_b",
        [far_out((count, width - wide)), far_out((count, width - wide))],
        [VMEM] * 3 + [ANY],
        [HBM, HBM],
        [pltpu.VMEM((count, width - wide), bf16), sems((1 + n_sent,))],
        flops=2 * count * count * (width - wide),
        nbytes=2 * count * (3 * (width - wide) + count + width),
    )(picked_far, sent_base, received_b, sent_planes[0])
    last_b = exchange(sent_b, peers)
    got_pairs = within(me, got_planes, peers, slots)
    next_base, rest, near_far = call(
        labels_kernel,
        "labels",
        [
            near_out((rows, width)),
            near_out((rows, width), jnp.float8_e4m3fn),
            near_out((rows, count)),
        ],
        [VMEM] * 5 + [ANY],
        [VMEM] * 3,
        flops=2 * rows * (count + 2 * rows) * width,
    )(
        far_in(own),
        far_in(far),
        far_in(seeds),
        far_in(received_a),
        far_in(received_b),
        got_pairs[0],
    )
    first = call(
        functools.partial(last_a_kernel, slots=slots),
        "last_a",
        far_out((rows, width)),
        [SMEM] + [VMEM] * (3 + GROUP // 2),
        HBM,
        [pltpu.VMEM((count, wide), bf16), pltpu.VMEM((rows, wide), bf16), sems((n_a,))],
        flops=2 * rows * count * wide,
    )(me, near_far, next_base, rest, *got_pairs)
    return call(
        last_b_kernel,
        "last_b",
        far_out((rows, width)),
        [VMEM] * 4 + [HBM],
        HBM,
        [pltpu.VMEM((rows, width - wide), bf16), sems((n_out,))],
        flops=2 * rows * count * (width - wide),
        nbytes=2 * rows * count + 5 * rows * width + 2 * count * width,
        aliases={4: 0},
    )(near_far, next_base, rest, last_b, far_in(first))


def solution(mesh):
    in_specs = (
        P(("parts", "rows"), "cls"),
        P(("parts", "rows"), None),
        P(("parts", "rows"), None),
        P(("parts", "rows"), None),
        P(("parts", "rows"), None, None),
    )
    out_specs = P(("parts", "rows"), "cls")
    return jax.shard_map(
        on_device, mesh=mesh, in_specs=in_specs, out_specs=out_specs, check_vma=False
    )
```

```python
import functools
import math

import jax
import jax.numpy as jnp
from jax import lax
from jax.experimental import pallas as pl
from jax.experimental.pallas import tpu as pltpu
from jax.sharding import PartitionSpec as P

BLK = 128
COLS = 256
GROUP = 8
PACK = 16
VMEM_LIMIT = 32 * 1024 * 1024
NEAR_BYTES = 1024 * 1024
KEEP = 0.85
ANCHOR = 0.15
REST_SCALE = 4096.0
LONG = 4 * 10**10
EARLY = 2

SMEM = pl.BlockSpec(memory_space=pltpu.SMEM)
VMEM = pl.BlockSpec(memory_space=pltpu.VMEM)
HBM = pl.BlockSpec(memory_space=pltpu.HBM)
ANY = pl.BlockSpec(memory_space=pl.ANY)


def far_out(shape, dtype=jnp.bfloat16):
    return pltpu.HBM(shape, dtype)


def far_in(x):
    return pltpu.with_memory_space_constraint(x, pltpu.HBM)


def near_out(shape, dtype=jnp.bfloat16):
    small = math.prod(shape) * jnp.dtype(dtype).itemsize <= NEAR_BYTES
    return pltpu.VMEM(shape, dtype) if small else jax.ShapeDtypeStruct(shape, dtype)


def call(kernel, name, out_shape, in_specs, out_specs, scratch_shapes=(), flops=0, nbytes=0, aliases=None):
    return pl.pallas_call(
        kernel,
        out_shape=out_shape,
        in_specs=in_specs,
        out_specs=out_specs,
        scratch_shapes=scratch_shapes,
        input_output_aliases=aliases or {},
        compiler_params=pltpu.CompilerParams(vmem_limit_bytes=VMEM_LIMIT),
        cost_estimate=pl.CostEstimate(flops=flops, bytes_accessed=nbytes, transcendentals=0),
        name=name,
    )


def dot(a, b):
    return jnp.dot(a, b, preferred_element_type=jnp.float32)


def pieces_of(first, last):
    return [slice(c, min(c + COLS, last)) for c in range(first, last, COLS)]


def strips_of(count):
    return [slice(r, r + BLK) for r in range(0, count, BLK)]


def moved(cols, by):
    return slice(cols.start + by, cols.stop + by)


def push(source, target, sem):
    copy = pltpu.make_async_copy(source, target, sem)
    copy.start()
    return copy


def picks(asked, rows):
    peers, _, slots = asked.shape
    count = peers * slots
    spread = jnp.broadcast_to(asked.astype(jnp.float32), (peers, slots, slots))
    spread = spread.reshape(count, slots)
    slot = lax.broadcasted_iota(jnp.int32, (count, slots), 0) % slots
    lane = lax.broadcasted_iota(jnp.int32, (count, slots), 1)
    row = jnp.sum(jnp.where(slot == lane, spread, 0.0), axis=1, keepdims=True)
    hits = lax.broadcasted_iota(jnp.int32, (count, rows), 1) == row.astype(jnp.int32)
    return hits.astype(jnp.float32).astype(jnp.bfloat16)


def block(peer, slots):
    return pl.ds(pl.multiple_of(peer * slots, slots), slots)


def pair_order(pairs):
    return [0] + list(range(pairs - 1, 0, -1))


def plane_order(planes):
    return [0] + list(range(2, planes)) + [1]


def pair_of(q, device):
    other = {3: 2, 2: 1, 1: 3}.get(q, q)
    return q + (device & 1) * (other - q)


def plane_of(z, planes, device):
    other = {2: 3, 3: 2}.get(z, z) if planes > 3 else z
    return z + (device & 1) * (other - z)


def to_planes(me, rows_ref, plane_refs, slots):
    for z, plane_ref in zip(plane_order(len(plane_refs)), plane_refs):
        for s in range(2):
            for q in range(GROUP // 2):
                peer = me ^ (GROUP * plane_of(z, len(plane_refs), me) + 2 * q + s)
                at = (s * (GROUP // 2) + q) * slots
                plane_ref[at : at + slots, :] = rows_ref[block(peer, slots), :]


def from_pairs(me, pair_refs, rows_ref, slots):
    planes = pair_refs[0].shape[0] // (2 * slots)
    for q, pair_ref in zip(pair_order(len(pair_refs)), pair_refs):
        for s in range(2):
            for i, z in enumerate(plane_order(planes)):
                holder = me ^ (2 * pair_of(q, me) + s)
                peer = holder ^ (GROUP * plane_of(z, planes, holder))
                at = (s * planes + i) * slots
                rows_ref[block(peer, slots), :] = pair_ref[at : at + slots, :]


def fill_edges(blocks_ref, pos_ref, weight_ref, column_ref, share_ref):
    block_count, tile_count = blocks_ref.shape
    neighbours = pos_ref.shape[0]
    column_ref[...] = jnp.full(column_ref.shape, -1, jnp.int32)
    share_ref[...] = jnp.zeros(share_ref.shape, jnp.float32)
    weights = weight_ref[...].astype(jnp.float32)
    share = weights / jnp.sum(weights, axis=0, keepdims=True)
    share_ref[:neighbours, :] = share.astype(jnp.bfloat16).astype(jnp.float32)
    for b in range(block_count):
        lanes = slice(b * BLK, (b + 1) * BLK)
        pos = pos_ref[:, lanes]
        tile = pos // BLK
        base = jnp.full(pos.shape, blocks_ref[b, 0], jnp.int32)
        for j in range(1, tile_count):
            base = jnp.where(tile == j, blocks_ref[b, j], base)
        column_ref[:neighbours, lanes] = base * BLK + pos % BLK


def fill_tiles(neighbours, column_ref, share_ref, tiles_ref, spot_ref, start, chunks):
    rows = column_ref.shape[1]
    sub = lax.broadcasted_iota(jnp.int32, (BLK, BLK), 0).astype(jnp.float32).astype(jnp.bfloat16)
    sub = sub.reshape(BLK // PACK, PACK, BLK)

    @pl.loop(*chunks)
    def _(chunk):
        first = pl.multiple_of(chunk * BLK, BLK)
        spot = column_ref[...] - (start + first)
        spot_ref[...] = jnp.where((spot >= 0) & (spot < BLK), spot, -1).astype(jnp.float32)

        @pl.loop(0, rows // BLK)
        def _(b):
            lanes = pl.ds(pl.multiple_of(b * BLK, BLK), BLK)
            row = lambda ref, k: jnp.broadcast_to(ref[k : k + 1, lanes], (PACK, BLK))
            total = jnp.zeros(sub.shape, jnp.bfloat16)
            for k in range(neighbours):
                spot = row(spot_ref, k).astype(jnp.bfloat16)
                share = row(share_ref, k).astype(jnp.bfloat16)
                total = jnp.where(sub == spot[None], share[None], total)
            tiles_ref[lanes, pl.ds(first, BLK)] = total.reshape(BLK, BLK).T


def own_tiles_kernel(
    blocks_ref,
    pos_ref,
    weight_ref,
    seeds_hbm,
    own_hbm,
    column_ref,
    share_ref,
    near_ref,
    own_ref,
    spot_ref,
    sems,
):
    copies = [push(seeds_hbm, near_ref, sems.at[0])]
    fill_edges(blocks_ref, pos_ref, weight_ref, column_ref, share_ref)
    for i in range(own_ref.shape[1] // BLK):
        cols = slice(i * BLK, (i + 1) * BLK)
        fill_tiles(pos_ref.shape[0], column_ref, share_ref, own_ref, spot_ref, 0, (i, i + 1))
        copies.append(push(own_ref.at[:, cols], own_hbm.at[:, cols], sems.at[1 + i]))
    for copy in copies:
        copy.wait()


def pick_a_kernel(me_ref, asked_ref, seeds_ref, after_ref, pick_ref, *refs):
    *plane_refs, a_ref = refs
    del after_ref
    pick_ref[...] = picks(asked_ref[...], seeds_ref.shape[0])
    for cols in pieces_of(0, a_ref.shape[1]):
        a_ref[:, cols] = dot(pick_ref[...], seeds_ref[:, cols]).astype(jnp.bfloat16)
    to_planes(me_ref[0], a_ref, plane_refs, asked_ref.shape[2])


def pick_b_kernel(
    pick_ref,
    seeds_ref,
    column_ref,
    share_ref,
    out_b,
    early_ref,
    b_ref,
    spot_ref,
    sems,
    *,
    neighbours,
):
    rows, width = seeds_ref.shape
    wide = width - b_ref.shape[1]
    copies = []
    for i, rows_here in enumerate(strips_of(pick_ref.shape[0])):
        b_ref[rows_here, :] = dot(pick_ref[rows_here, :], seeds_ref[:, wide:]).astype(jnp.bfloat16)
        copies.append(push(b_ref.at[rows_here], out_b.at[rows_here], sems.at[i]))
    chunks = (0, early_ref.shape[1] // BLK)
    fill_tiles(neighbours, column_ref, share_ref, early_ref, spot_ref, rows, chunks)
    for copy in copies:
        copy.wait()


def far_kernel(
    asked_ref,
    early_ref,
    own_ref,
    column_ref,
    share_ref,
    seeds_ref,
    after_ref,
    far_ref,
    picked_far_ref,
    sent_base_ref,
    whole_ref,
    pick_ref,
    picked_ref,
    spot_ref,
    *,
    neighbours,
):
    del after_ref
    rows, width = seeds_ref.shape
    head = own_ref.shape[1]
    whole_ref[:, :head] = own_ref[...]
    chunks = (head // BLK, rows // BLK)
    fill_tiles(neighbours, column_ref, share_ref, whole_ref, spot_ref, 0, chunks)
    done = early_ref.shape[1]
    far_ref[:, :done] = early_ref[...]
    chunks = (done // BLK, far_ref.shape[1] // BLK)
    fill_tiles(neighbours, column_ref, share_ref, far_ref, spot_ref, rows, chunks)
    pick_ref[...] = picks(asked_ref[...], rows)
    for cols in pieces_of(0, far_ref.shape[1]):
        picked_far_ref[:, cols] = dot(pick_ref[...], far_ref[:, cols]).astype(jnp.bfloat16)
    for cols in pieces_of(0, rows):
        picked_ref[:, cols] = dot(pick_ref[...], whole_ref[:, cols]).astype(jnp.bfloat16)
    for cols in pieces_of(0, width):
        seeds = seeds_ref[:, cols]
        sent_base = KEEP * dot(picked_ref[...], seeds) + ANCHOR * dot(pick_ref[...], seeds)
        sent_base_ref[:, cols] = sent_base.astype(jnp.bfloat16)


def gather_kernel(*refs):
    *plane_refs, out_ref = refs
    half = plane_refs[0].shape[0] // 2
    for z, plane_ref in enumerate(plane_refs):
        out_ref[z * half : (z + 1) * half, :] = plane_ref[half:, :]


def pair_kernel(slots, me_ref, *refs):
    count = GROUP // 2
    *plane_refs, other_ref = refs[:-count]
    planes = len(plane_refs)
    for q, out_ref in zip(pair_order(count), refs[-count:]):
        q = pair_of(q, me_ref[0])
        for z, plane_ref in enumerate(plane_refs):
            here = slice(z * slots, (z + 1) * slots)
            there = slice((planes + z) * slots, (planes + z + 1) * slots)
            out_ref[here, :] = plane_ref[block(q, slots), :]
            out_ref[there, :] = other_ref[block(z * count + q, slots), :]


def send_a_kernel(me_ref, tiles_ref, base_ref, *refs, slots):
    pair_refs = refs[: GROUP // 2]
    out_hbm, *plane_refs, received_ref, out_ref, sem = refs[GROUP // 2 :]
    me = me_ref[0]
    from_pairs(me, pair_refs, received_ref, slots)
    copy = push(received_ref, out_hbm, sem)
    for cols in pieces_of(0, received_ref.shape[1]):
        total = KEEP * dot(tiles_ref[...], received_ref[:, cols])
        out_ref[:, cols] = (total + base_ref[:, cols].astype(jnp.float32)).astype(jnp.bfloat16)
    to_planes(me, out_ref, plane_refs, slots)
    copy.wait()


def send_b_kernel(tiles_ref, base_ref, received_ref, after_ref, out_hbm, kept_hbm, out_ref, sems):
    del after_ref
    wide = base_ref.shape[1] - received_ref.shape[1]
    copies = [push(received_ref, kept_hbm, sems.at[0])]
    for i, rows in enumerate(strips_of(out_ref.shape[0])):
        total = KEEP * dot(tiles_ref[rows, :], received_ref[...])
        total = total + base_ref[rows, wide:].astype(jnp.float32)
        out_ref[rows, :] = total.astype(jnp.bfloat16)
        copies.append(push(out_ref.at[rows], out_hbm.at[rows], sems.at[1 + i]))
    for copy in copies:
        copy.wait()


def labels_kernel(
    own_ref,
    far_ref,
    seeds_ref,
    received_a_ref,
    received_b_ref,
    after_ref,
    next_ref,
    rest_ref,
    near_ref,
):
    del after_ref
    near_ref[...] = far_ref[...]
    wide = received_a_ref.shape[1]
    width = seeds_ref.shape[1]
    for cols in pieces_of(0, wide) + pieces_of(wide, width):
        first = cols.stop <= wide
        received = received_a_ref[:, cols] if first else received_b_ref[:, moved(cols, -wide)]
        seeds = ANCHOR * seeds_ref[:, cols].astype(jnp.float32)
        total = dot(own_ref[...], seeds_ref[:, cols]) + dot(far_ref[...], received)
        labels = (KEEP * total + seeds).astype(jnp.bfloat16)
        base = KEEP * dot(own_ref[...], labels) + seeds
        kept = base.astype(jnp.bfloat16)
        next_ref[:, cols] = kept
        rest = (base - kept.astype(jnp.float32)) * REST_SCALE
        rest_ref[:, cols] = rest.astype(jnp.float8_e4m3fn)


def result(tiles_ref, received, base_ref, rest_ref, rows, cols):
    total = KEEP * dot(tiles_ref[rows, :], received) + base_ref[rows, cols].astype(jnp.float32)
    total = total + rest_ref[rows, cols].astype(jnp.float32) * (1 / REST_SCALE)
    return total.astype(jnp.bfloat16)


def last_a_kernel(me_ref, tiles_ref, base_ref, rest_ref, *refs, slots):
    pair_refs = refs[: GROUP // 2]
    out_hbm, received_ref, out_ref, sems = refs[GROUP // 2 :]
    from_pairs(me_ref[0], pair_refs, received_ref, slots)
    copies = []
    for i, cols in enumerate(pieces_of(0, received_ref.shape[1])):
        received = received_ref[:, cols]
        out_ref[:, cols] = result(tiles_ref, received, base_ref, rest_ref, slice(None), cols)
        copies.append(push(out_ref.at[:, cols], out_hbm.at[:, cols], sems.at[i]))
    for copy in copies:
        copy.wait()


def last_b_kernel(tiles_ref, base_ref, rest_ref, received_ref, same_ref, out_hbm, out_ref, sems):
    del same_ref
    width = base_ref.shape[1]
    wide = width - received_ref.shape[1]
    copies = []
    cols = slice(wide, width)
    for i, rows in enumerate(strips_of(out_ref.shape[0])):
        out_ref[rows, :] = result(tiles_ref, received_ref[...], base_ref, rest_ref, rows, cols)
        copies.append(push(out_ref.at[rows], out_hbm.at[rows, cols], sems.at[i]))
    for copy in copies:
        copy.wait()


def swap(x, peers, distance):
    return lax.ppermute(x, "rows", [(i, i ^ distance(i)) for i in range(peers)])


def exchange(rows_out, peers):
    count, width = rows_out.shape
    sent = rows_out.reshape(peers, count // peers, width)
    got = lax.all_to_all(sent, "rows", split_axis=0, concat_axis=0, tiled=True)
    return got.reshape(count, width)


def across(planes, peers):
    order = plane_order(len(planes))
    far = lambda z: lambda i: GROUP * plane_of(z, len(planes), i)
    return [swap(x, peers, far(z)) if z else x for z, x in zip(order, planes)]


def within(me, planes, peers, slots):
    depth, wide = planes[0].shape
    n = len(planes)
    other = call(
        gather_kernel,
        "gather",
        jax.ShapeDtypeStruct((n * depth // 2, wide), jnp.bfloat16),
        [VMEM] * n,
        VMEM,
        flops=LONG,
    )(*planes)
    other = swap(other, peers, lambda i: 1)
    pairs = call(
        functools.partial(pair_kernel, slots),
        "pair",
        [jax.ShapeDtypeStruct((2 * n * slots, wide), jnp.bfloat16)] * (GROUP // 2),
        [SMEM] + [VMEM] * (n + 1),
        [VMEM] * (GROUP // 2),
    )(me, *planes, other)
    even = lambda q: lambda i: 2 * pair_of(q, i)
    return [swap(x, peers, even(q)) if q else x for q, x in zip(pair_order(len(pairs)), pairs)]


def on_device(seeds, neighbor_pos, edge_weight, tile_blocks, wanted):
    rows, width = seeds.shape
    peers, slots = wanted.shape[1:]
    count = peers * slots
    neighbours = neighbor_pos.shape[1]
    depth = -(-neighbours // PACK) * PACK
    planes = peers // GROUP
    wide = max(3 * width // 8 // BLK, 1) * BLK
    assert peers & (peers - 1) == 0 and peers >= GROUP
    head = rows - 2 * BLK
    me = lax.axis_index("rows").astype(jnp.int32).reshape(1)
    sems = pltpu.SemaphoreType.DMA
    bf16 = jnp.bfloat16
    plane_shape = jax.ShapeDtypeStruct((GROUP * slots, wide), bf16)
    n_a, n_out, n_sent = len(pieces_of(0, wide)), len(strips_of(rows)), len(strips_of(count))

    asked = lax.all_to_all(
        wanted.reshape(peers, 1, slots), "rows", split_axis=0, concat_axis=0, tiled=True
    )
    own, column, share, near_seeds = call(
        own_tiles_kernel,
        "own_tiles",
        [
            far_out((rows, head)),
            near_out((depth, rows), jnp.int32),
            near_out((depth, rows), jnp.float32),
            near_out((rows, width)),
        ],
        [SMEM, VMEM, VMEM, HBM],
        [HBM, VMEM, VMEM, VMEM],
        [
            pltpu.VMEM((rows, head), bf16),
            pltpu.VMEM((depth, rows), jnp.float32),
            sems((1 + head // BLK,)),
        ],
        flops=neighbours * rows * rows,
    )(far_in(tile_blocks), far_in(neighbor_pos.T), far_in(edge_weight.T), far_in(seeds))
    pick, *sent_planes = call(
        pick_a_kernel,
        "pick_a",
        [near_out((count, rows))] + [plane_shape] * planes,
        [SMEM, VMEM, VMEM, HBM],
        [VMEM] * (1 + planes),
        [pltpu.VMEM((count, wide), bf16)],
        flops=2 * count * rows * wide,
    )(me, asked, near_seeds, far_in(own))
    got_planes = across(sent_planes, peers)
    sent_b, early = call(
        functools.partial(pick_b_kernel, neighbours=neighbours),
        "pick_b",
        [
            far_out((count, width - wide)),
            near_out((rows, count // BLK * EARLY // 8 * BLK)),
        ],
        [VMEM] * 4,
        [HBM, VMEM],
        [
            pltpu.VMEM((count, width - wide), bf16),
            pltpu.VMEM((depth, rows), jnp.float32),
            sems((n_sent,)),
        ],
        flops=2 * count * rows * (width - wide),
    )(pick, near_seeds, column, share)
    received_b = exchange(sent_b, peers)
    got_pairs = within(me, got_planes, peers, slots)
    far, picked_far, sent_base, own = call(
        functools.partial(far_kernel, neighbours=neighbours),
        "far",
        [
            far_out((rows, count)),
            near_out((count, count)),
            near_out((count, width)),
            far_out((rows, rows)),
        ],
        [VMEM] * 6 + [ANY],
        [VMEM] * 4,
        [
            pltpu.VMEM((count, rows), bf16),
            pltpu.VMEM((count, rows), bf16),
            pltpu.VMEM((depth, rows), jnp.float32),
        ],
        flops=2 * rows * count * (count + rows + width) + neighbours * rows * count,
    )(
        asked,
        early,
        far_in(own),
        column,
        share,
        far_in(seeds),
        got_pairs[0],
    )
    received_a, *sent_planes = call(
        functools.partial(send_a_kernel, slots=slots),
        "send_a",
        [far_out((count, wide))] + [plane_shape] * planes,
        [SMEM] + [VMEM] * (2 + GROUP // 2),
        [HBM] + [VMEM] * planes,
        [pltpu.VMEM((count, wide), bf16), pltpu.VMEM((count, wide), bf16), sems],
        flops=2 * count * count * wide,
    )(me, picked_far, sent_base, *got_pairs)
    got_planes = across(sent_planes, peers)
    sent_b, received_b = call(
        send_b_kernel,
        "send_b",
        [far_out((count, width - wide)), far_out((count, width - wide))],
        [VMEM] * 3 + [ANY],
        [HBM, HBM],
        [pltpu.VMEM((count, width - wide), bf16), sems((1 + n_sent,))],
        flops=2 * count * count * (width - wide),
        nbytes=2 * count * (3 * (width - wide) + count + width),
    )(picked_far, sent_base, received_b, sent_planes[0])
    last_b = exchange(sent_b, peers)
    got_pairs = within(me, got_planes, peers, slots)
    next_base, rest, near_far = call(
        labels_kernel,
        "labels",
        [
            near_out((rows, width)),
            near_out((rows, width), jnp.float8_e4m3fn),
            near_out((rows, count)),
        ],
        [VMEM] * 5 + [ANY],
        [VMEM] * 3,
        flops=2 * rows * (count + 2 * rows) * width,
    )(
        far_in(own),
        far_in(far),
        far_in(seeds),
        far_in(received_a),
        far_in(received_b),
        got_pairs[0],
    )
    first = call(
        functools.partial(last_a_kernel, slots=slots),
        "last_a",
        far_out((rows, width)),
        [SMEM] + [VMEM] * (3 + GROUP // 2),
        HBM,
        [pltpu.VMEM((count, wide), bf16), pltpu.VMEM((rows, wide), bf16), sems((n_a,))],
        flops=2 * rows * count * wide,
    )(me, near_far, next_base, rest, *got_pairs)
    return call(
        last_b_kernel,
        "last_b",
        far_out((rows, width)),
        [VMEM] * 4 + [HBM],
        HBM,
        [pltpu.VMEM((rows, width - wide), bf16), sems((n_out,))],
        flops=2 * rows * count * (width - wide),
        nbytes=2 * rows * count + 5 * rows * width + 2 * count * width,
        aliases={4: 0},
    )(near_far, next_base, rest, last_b, far_in(first))


def solution(mesh):
    in_specs = (
        P(("parts", "rows"), "cls"),
        P(("parts", "rows"), None),
        P(("parts", "rows"), None),
        P(("parts", "rows"), None),
        P(("parts", "rows"), None, None),
    )
    out_specs = P(("parts", "rows"), "cls")
    return jax.shard_map(
        on_device, mesh=mesh, in_specs=in_specs, out_specs=out_specs, check_vma=False
    )
```
